32 devices in a mesh: groups: 2 (over x), rows: 8 (over z, y), tensor: 2 (over core).
Axes of the slice: x: 2, y: 2, z: 4, core: 2. Of those that a mesh axis runs over, the one named last changes fastest.
Arguments:
- passages: bfloat16 [10240, 8192], P(('groups', 'rows'), 'tensor'), parts along dimension 0, may hold values from -6 to 6
- kv_weight: bfloat16 [8192, 2, 1024], P('rows', None, 'tensor'), may hold values from -0.0625 to 0.0625
- new_hidden: bfloat16 [128, 3, 8192], P(('groups', 'rows'), None, 'tensor'), parts along dimension 0, may hold values from -6 to 6
- queries: bfloat16 [128, 3, 8192], P(('groups', 'rows'), None, 'tensor'), parts along dimension 0, may hold values from -64 to 64
- lengths: int32 [16, 8], P('groups'), parts along dimension 0, may hold values from 1 to 160, 640 in all within a row
- destinations: int32 [16, 8], P('groups'), parts along dimension 0, may hold values from 0 to 7, as said below
Outputs:
- attended: bfloat16 [128, 3, 8192], P(('groups', 'rows'), None, 'tensor'), parts along dimension 0
The draws below stay inside these ranges and needn't reach their ends.
There are 2 independent parts, one for each index of `groups`. The reference program is written for one: setup_inputs(seed, part) draws one part's arguments, and reference() takes and returns one part's arrays. A program takes and returns all parts, laid end to end along the dimension named above; an argument that names none is the same for every part. Nothing has to cross between parts.
Inputs may be any that keep to these rules, and one draw needn't show every extreme that they name: `destinations`: row p names a different decode row for each of its 8 requests, and each decode row receives exactly one request from every prefill replica. `lengths`: each row sums to 640.
All inputs are finite; a program needn't handle non-finite values.
Results may differ from the reference program's by a relative error of at most 0.012.
The reference program's roundings to bfloat16 on the way (of `cache_keys`, `cache_values`, `new_keys` and `weights`) count: a program that leaves them out, or rounds other values in their place, can miss the bound.
Values may be sent and summed in bfloat16 or wider, within the bound.
No kernel may reach another device: no remote copies, remote signals or barrier semaphores. Data moves between devices by JAX's collectives and lax.ppermute only.
A program may use at most 128 MiB of HBM per device.

```python
import math
import jax
import jax.numpy as jnp
import numpy as np
from jax import lax

D = 8192
KVH = 8
QH = 64
HD = 128
STEPS = 3
TOK_DEV = 640
REQS_DEV = 8
MOST = 160
GROUP = 8
TOKENS = 5120
REQS = 64
N_ROWS = 8


def draw_queries(key, part):
    key = jax.random.fold_in(key, 11)
    base = jax.random.normal(key, (REQS, STEPS, QH * HD), jnp.float32)
    values = jnp.clip(base, -4.0, 4.0)
    return values.astype(jnp.bfloat16)


def draw_destinations(key, part):
    key = jax.random.fold_in(key, 23)
    first_key, second_key, third_key = jax.random.split(key, 3)
    first = jax.random.permutation(first_key, REQS_DEV)
    second = jax.random.permutation(second_key, REQS_DEV)
    third = jax.random.permutation(third_key, REQS_DEV)
    return third[(first[:, None] + second[None, :]) % REQS_DEV].astype(jnp.int32)


def block_scale(own_key, extent, cuts, least, high):
    level = 1.0
    for axis_at, shards_of in cuts:
        steps = jax.random.uniform(jax.random.fold_in(jax.random.fold_in(own_key, 6), axis_at), (shards_of,), jnp.float32, least / len(cuts), high / len(cuts))
        level = level * jnp.repeat(jnp.exp(steps), extent[axis_at] // shards_of).reshape((-1,) + (1,) * (len(extent) - 1 - axis_at))
    return level


def length_profile(amount, total, bound, lean):
    loads = [(1 << 20) // math.isqrt(rank ** lean) + 1 for rank in range(2, amount + 1)]
    spare, given = total - bound - (amount - 1), [1] * (amount - 1)
    while spare > 0:
        movable = [i for i in range(amount - 1) if given[i] < bound]
        whole, left = sum([loads[i] for i in movable]), spare
        for i in movable:
            addition = min(bound - given[i], max(1, left * loads[i] // whole), spare)
            given[i] = given[i] + addition
            spare = spare - addition
    return np.array([bound] + given)


def uneven_parts(own_key, number_of, total, limit, lean):
    if number_of == 2:
        one = jax.random.randint(own_key, (), max(1, total - limit), min(limit, total - 1) + 1)
        return jnp.stack([one, total - one])
    sizes = jnp.asarray(length_profile(number_of, total, limit, lean), jnp.int32)
    pairs = (number_of - 1) // 2
    donor, receiver = sizes[1:1 + 2 * pairs:2], sizes[2:2 + 2 * pairs:2]
    room = jnp.minimum(donor - 1, limit - receiver)
    passed = jax.random.randint(jax.random.fold_in(own_key, 1), (pairs,), 0, 1 << 20) % (room + 1)
    sizes = sizes.at[1:1 + 2 * pairs:2].set(donor - passed).at[2:2 + 2 * pairs:2].set(receiver + passed)
    return sizes[jax.random.permutation(jax.random.fold_in(own_key, 2), number_of)]


def scatter_about(key, dims, spread, reach, shards=(), kind=jnp.bfloat16):
    entries = spread * jax.random.normal(key, dims, jnp.float32)
    if shards:
        entries = entries * block_scale(key, dims, shards, -0.22, 0.18)
    return jnp.clip(entries, -reach, reach).astype(kind)


def setup_inputs(seed: int = 0, part: int = 0) -> dict:
    arg_keys = jax.random.split(jax.random.key(seed), 7)
    part_keys = jax.random.split(jax.random.fold_in(arg_keys[6], part), 7)
    return {
        "passages": scatter_about(part_keys[0], (TOKENS, D), 1.0, 6.0, ((0, 8), (1, 2))),
        "kv_weight": scatter_about(arg_keys[1], (D, 2, KVH * HD), D ** -0.5, 0.0625, ((0, 8), (2, 2))),
        "new_hidden": scatter_about(part_keys[2], (REQS, STEPS, D), 1.0, 6.0, ((0, 8), (2, 2))),
        "queries": draw_queries(jax.random.fold_in(jax.random.fold_in(arg_keys[6], part), 71), part),
        "lengths": jax.vmap(lambda own: uneven_parts(own, REQS_DEV, TOK_DEV, MOST, 2))(jax.random.split(part_keys[4], N_ROWS)).reshape((N_ROWS, REQS_DEV)).astype(jnp.int32),
        "destinations": draw_destinations(jax.random.fold_in(jax.random.fold_in(arg_keys[6], part), 71), part),
    }


def rotate(vectors, positions):
    half_size = HD // 2
    index_float = jnp.arange(half_size, dtype=jnp.float32)
    inverse = jnp.exp(index_float * (-2.0 * math.log(1000000.0) / HD))
    angles = positions.astype(jnp.float32)[..., None] * inverse
    cosine = jnp.cos(angles)
    sine = jnp.sin(angles)
    first = vectors[..., :half_size]
    second = vectors[..., half_size:]
    return jnp.concatenate([first * cosine - second * sine, second * cosine + first * sine], -1)

def token_positions(starts_row, count):
    token_index = jnp.arange(count, dtype=jnp.int32)
    began = jnp.where(starts_row[None, :] <= token_index[:, None], starts_row[None, :], 0)
    return token_index - lax.optimization_barrier(jnp.max(began, axis=1))

def reference(passages, kv_weight, new_hidden, queries, lengths, destinations):
    nrows = lengths.shape[0]
    weight_flat = kv_weight.reshape(D, 2 * KVH * HD)
    projected = jnp.dot(passages, weight_flat, preferred_element_type=jnp.float32).reshape(TOKENS, 2, KVH, HD)
    starts = (jnp.cumsum(lengths, axis=1) - lengths).astype(jnp.int32)
    positions = jax.vmap(lambda row: token_positions(row, TOK_DEV))(starts).reshape(TOKENS)
    cache_keys = rotate(projected[:, 0], positions[:, None]).astype(jnp.bfloat16)
    cache_values = projected[:, 1].astype(jnp.bfloat16)
    new_projected = jnp.dot(new_hidden.reshape(REQS * STEPS, D), weight_flat, preferred_element_type=jnp.float32)
    new_projected = new_projected.reshape(REQS, STEPS, 2, KVH, HD)
    request_index = jnp.arange(REQS, dtype=jnp.int32)
    decode_row = request_index // nrows
    source_row = request_index % nrows
    matched = destinations[source_row] == decode_row[:, None]
    request_length = lax.optimization_barrier(jnp.sum(jnp.where(matched, lengths[source_row], 0), axis=1)).astype(jnp.int32)
    request_start = lax.optimization_barrier(jnp.sum(jnp.where(matched, starts[source_row], 0), axis=1)).astype(jnp.int32)
    base_row = (source_row * TOK_DEV + request_start).astype(jnp.int32)
    step_index = jnp.arange(STEPS, dtype=jnp.int32)
    new_positions = request_length[:, None] + step_index[None, :]
    new_keys = rotate(new_projected[:, :, 0], new_positions[:, :, None]).astype(jnp.bfloat16)
    new_values = new_projected[:, :, 1].astype(jnp.bfloat16)
    keys_padded = jnp.concatenate([cache_keys, jnp.zeros((MOST, KVH, HD), jnp.bfloat16)], 0)
    values_padded = jnp.concatenate([cache_values, jnp.zeros((MOST, KVH, HD), jnp.bfloat16)], 0)
    scale = 1.0 / math.sqrt(HD)
    slot_index = jnp.arange(MOST + STEPS, dtype=jnp.int32)

    def one_request(items):
        query, key_new, value_new, base, length = items
        key_cache = lax.dynamic_slice_in_dim(keys_padded, base, MOST, 0)
        value_cache = lax.dynamic_slice_in_dim(values_padded, base, MOST, 0)
        keys_all = jnp.concatenate([key_cache, key_new], 0).astype(jnp.float32)
        values_all = jnp.concatenate([value_cache, value_new], 0).astype(jnp.float32)
        query_heads = query.reshape(STEPS, KVH, GROUP, HD).astype(jnp.float32)
        scores = jnp.einsum('tkgd,mkd->tkgm', query_heads, keys_all) * scale
        in_cache = (slot_index[None, :] < length) & (slot_index[None, :] < MOST)
        in_new = (slot_index[None, :] >= MOST) & (slot_index[None, :] - MOST <= step_index[:, None])
        allowed = (in_cache | in_new)[:, None, None, :]
        scores = jnp.where(allowed, scores, jnp.float32(-1e+30))
        largest = lax.optimization_barrier(jnp.max(scores, axis=-1, keepdims=True))
        raised = jnp.where(allowed, jnp.exp(scores - largest), jnp.float32(0.0))
        total = lax.optimization_barrier(jnp.sum(raised, axis=-1, keepdims=True))
        weights = (raised / total).astype(jnp.bfloat16)
        output = jnp.einsum('tkgm,mkd->tkgd', weights.astype(jnp.float32), values_all)
        return output.astype(jnp.bfloat16).reshape(STEPS, QH * HD)
    return lax.map(one_request, (queries, new_keys, new_values, base_row, request_length))
```

```python
import functools
import math

import jax
import jax.numpy as jnp
from jax import lax
from jax.experimental import pallas as pl
from jax.experimental.pallas import tpu as pltpu
from jax.sharding import PartitionSpec as P

HD = 128
HALF = HD // 2


def angle_tables(positions):
    index_float = jnp.arange(HALF, dtype=jnp.float32)
    inverse = jnp.exp(index_float * (-2.0 * math.log(1000000.0) / HD))
    angles = positions.astype(jnp.float32)[:, None] * inverse
    return jnp.cos(angles), jnp.sin(angles)


def token_tables(lengths, destinations, row_index, tokens, requests, steps, padded):
    my_lengths = lax.dynamic_index_in_dim(lengths, row_index, 0, keepdims=False)
    my_targets = lax.dynamic_index_in_dim(destinations, row_index, 0, keepdims=False)
    ends = jnp.cumsum(my_lengths)
    starts = ends - my_lengths
    token = jnp.arange(tokens, dtype=jnp.int32)[:, None]
    inside = (starts[None, :] <= token) & (token < ends[None, :])
    token_position = token[:, 0] - jnp.sum(jnp.where(inside, starts[None, :], 0), axis=1)
    token_target = jnp.sum(jnp.where(inside, my_targets[None, :], 0), axis=1)
    row_ids = jnp.arange(requests, dtype=jnp.int32)
    sending = my_targets[None, :] == row_ids[:, None]
    target_length = jnp.sum(jnp.where(sending, my_lengths[None, :], 0), axis=1)
    step = jnp.repeat(jnp.arange(steps, dtype=jnp.int32), requests)
    new_target = jnp.tile(row_ids, steps)
    new_position = jnp.tile(target_length, steps) + step
    spare = jnp.zeros((padded - tokens - requests * steps,), jnp.int32)
    position = jnp.concatenate([token_position, new_position, spare])
    target = jnp.concatenate([token_target, new_target, spare - 1])
    seen_from = jnp.concatenate([jnp.zeros_like(token_target), step, spare])
    query_info = jnp.stack([new_target, step], 1)
    return position, jnp.stack([target, seen_from], 0), query_info


def finish_kernel(heads, group, proj_ref, cos_ref, sin_ref, keys_ref, rows_ref, query_ref, out_ref):
    cosine, sine = cos_ref[...], sin_ref[...]
    allowed = (keys_ref[0:1, :] == rows_ref[:, 0:1]) & (keys_ref[1:2, :] <= rows_ref[:, 1:2])
    allowed = jnp.concatenate([allowed.astype(jnp.float32)] * group, 0) > 0.5
    queries = query_ref[...].astype(jnp.float32)
    count = queries.shape[0]
    width = heads * HD
    for h in range(heads):
        first = proj_ref[:, h * HD : h * HD + HALF]
        second = proj_ref[:, h * HD + HALF : (h + 1) * HD]
        keys = jnp.concatenate(
            [first * cosine - second * sine, second * cosine + first * sine], -1
        ).astype(jnp.bfloat16)
        values = proj_ref[:, width + h * HD : width + (h + 1) * HD].astype(jnp.bfloat16)
        at = h * group * HD
        query = jnp.concatenate(
            [queries[:, at + g * HD : at + (g + 1) * HD] for g in range(group)], 0
        ).astype(jnp.bfloat16)
        scores = lax.dot_general(
            query, keys, (((1,), (1,)), ((), ())), preferred_element_type=jnp.float32
        )
        scores = jnp.where(allowed, scores * (1.0 / math.sqrt(HD)), jnp.float32(-1e30))
        raised = jnp.exp(scores - jnp.max(scores, axis=-1, keepdims=True))
        total = jnp.sum(raised, axis=-1, keepdims=True)
        weights = (raised / total).astype(jnp.bfloat16)
        output = jnp.dot(weights, values, preferred_element_type=jnp.float32)
        for g in range(group):
            out_ref[:, at + g * HD : at + (g + 1) * HD] = output[
                g * count : (g + 1) * count
            ].astype(jnp.bfloat16)


def finish(projected, cosine, sine, key_info, query_info, queries):
    rows, width = projected.shape
    heads = width // (2 * HD)
    group = queries.shape[1] // (heads * HD)
    count = queries.shape[0]
    whole = pl.BlockSpec(memory_space=pltpu.VMEM)
    return pl.pallas_call(
        functools.partial(finish_kernel, heads, group),
        out_shape=jax.ShapeDtypeStruct(queries.shape, jnp.bfloat16),
        in_specs=[whole] * 6,
        out_specs=whole,
        compiler_params=pltpu.CompilerParams(vmem_limit_bytes=48 << 20),
        cost_estimate=pl.CostEstimate(
            flops=4 * heads * group * count * rows * HD,
            bytes_accessed=projected.size * 4 + 4 * queries.size,
            transcendentals=heads * group * count * rows,
        ),
        name="rotate_attend",
    )(projected, cosine, sine, key_info, query_info, queries)


def body(passages, kv_weight, new_hidden, queries, lengths, destinations):
    tokens = passages.shape[0]
    requests, steps, half_model = new_hidden.shape
    row_index = lax.axis_index("rows")
    count = requests * steps
    padded = -(-(tokens + count) // 16) * 16

    weight = kv_weight.reshape(kv_weight.shape[0], -1)
    weight = lax.all_gather(weight, "rows", axis=0, tiled=True)

    moved = jnp.concatenate([new_hidden, queries], 1)
    moved = lax.all_to_all(moved, "rows", split_axis=0, concat_axis=0, tiled=True)
    moved = jnp.swapaxes(moved, 0, 1)
    new_rows = moved[:steps].reshape(count, half_model)
    query_rows = moved[steps:].reshape(count, -1)

    hidden = jnp.concatenate(
        [passages, new_rows, jnp.zeros((padded - tokens - count, half_model), passages.dtype)], 0
    )
    hidden = lax.all_gather(hidden, "tensor", axis=1, tiled=True)

    position, key_info, query_info = token_tables(
        lengths, destinations, row_index, tokens, requests, steps, padded
    )
    cosine, sine = angle_tables(position)
    projected = jnp.dot(hidden, weight, preferred_element_type=jnp.float32)
    attended = finish(projected, cosine, sine, key_info, query_info, query_rows)
    attended = jnp.swapaxes(attended.reshape(steps, requests, -1), 0, 1)
    return lax.all_to_all(attended, "rows", split_axis=0, concat_axis=0, tiled=True)


def solution(mesh):
    placed = (
        P(("groups", "rows"), "tensor"),
        P("rows", None, "tensor"),
        P(("groups", "rows"), None, "tensor"),
        P(("groups", "rows"), None, "tensor"),
        P("groups", None),
        P("groups", None),
    )
    return jax.shard_map(
        body,
        mesh=mesh,
        in_specs=placed,
        out_specs=P(("groups", "rows"), None, "tensor"),
        check_vma=False,
    )
```

```python
import functools
import math

import jax
import jax.numpy as jnp
from jax import lax
from jax.experimental import pallas as pl
from jax.experimental.pallas import tpu as pltpu
from jax.sharding import PartitionSpec as P

HD = 128
HALF = HD // 2


def angle_tables(positions):
    index_float = jnp.arange(HALF, dtype=jnp.float32)
    inverse = jnp.exp(index_float * (-2.0 * math.log(1000000.0) / HD))
    angles = positions.astype(jnp.float32)[:, None] * inverse
    return jnp.cos(angles), jnp.sin(angles)


def token_tables(lengths, destinations, row_index, tokens, requests, steps, padded):
    my_lengths = lax.dynamic_index_in_dim(lengths, row_index, 0, keepdims=False)
    my_targets = lax.dynamic_index_in_dim(destinations, row_index, 0, keepdims=False)
    ends = jnp.cumsum(my_lengths)
    starts = ends - my_lengths
    token = jnp.arange(tokens, dtype=jnp.int32)[:, None]
    inside = (starts[None, :] <= token) & (token < ends[None, :])
    token_position = token[:, 0] - jnp.sum(jnp.where(inside, starts[None, :], 0), axis=1)
    token_target = jnp.sum(jnp.where(inside, my_targets[None, :], 0), axis=1)
    row_ids = jnp.arange(requests, dtype=jnp.int32)
    sending = my_targets[None, :] == row_ids[:, None]
    target_length = jnp.sum(jnp.where(sending, my_lengths[None, :], 0), axis=1)
    step = jnp.repeat(jnp.arange(steps, dtype=jnp.int32), requests)
    new_target = jnp.tile(row_ids, steps)
    new_position = jnp.tile(target_length, steps) + step
    spare = jnp.zeros((padded - tokens - requests * steps,), jnp.int32)
    position = jnp.concatenate([token_position, new_position, spare])
    target = jnp.concatenate([token_target, new_target, spare - 1])
    seen_from = jnp.concatenate([jnp.zeros_like(token_target), step, spare])
    query_info = jnp.stack([new_target, step], 1)
    return position, jnp.stack([target, seen_from], 0), query_info


def finish_kernel(heads, group, proj_ref, cos_ref, sin_ref, keys_ref, rows_ref, query_ref, out_ref):
    cosine, sine = cos_ref[...], sin_ref[...]
    allowed = (keys_ref[0:1, :] == rows_ref[:, 0:1]) & (keys_ref[1:2, :] <= rows_ref[:, 1:2])
    allowed = jnp.concatenate([allowed.astype(jnp.float32)] * group, 0) > 0.5
    queries = query_ref[...].astype(jnp.float32)
    count = queries.shape[0]
    width = heads * HD
    for h in range(heads):
        first = proj_ref[:, h * HD : h * HD + HALF]
        second = proj_ref[:, h * HD + HALF : (h + 1) * HD]
        keys = jnp.concatenate(
            [first * cosine - second * sine, second * cosine + first * sine], -1
        ).astype(jnp.bfloat16)
        values = proj_ref[:, width + h * HD : width + (h + 1) * HD].astype(jnp.bfloat16)
        at = h * group * HD
        query = jnp.concatenate(
            [queries[:, at + g * HD : at + (g + 1) * HD] for g in range(group)], 0
        ).astype(jnp.bfloat16)
        scores = lax.dot_general(
            query, keys, (((1,), (1,)), ((), ())), preferred_element_type=jnp.float32
        )
        scores = jnp.where(allowed, scores * (1.0 / math.sqrt(HD)), jnp.float32(-1e30))
        raised = jnp.exp(scores - jnp.max(scores, axis=-1, keepdims=True))
        total = jnp.sum(raised, axis=-1, keepdims=True)
        weights = (raised / total).astype(jnp.bfloat16)
        output = jnp.dot(weights, values, preferred_element_type=jnp.float32)
        for g in range(group):
            out_ref[:, at + g * HD : at + (g + 1) * HD] = output[
                g * count : (g + 1) * count
            ].astype(jnp.bfloat16)


def finish(projected, cosine, sine, key_info, query_info, queries):
    rows, width = projected.shape
    heads = width // (2 * HD)
    group = queries.shape[1] // (heads * HD)
    count = queries.shape[0]
    whole = pl.BlockSpec(memory_space=pltpu.VMEM)
    return pl.pallas_call(
        functools.partial(finish_kernel, heads, group),
        out_shape=jax.ShapeDtypeStruct(queries.shape, jnp.bfloat16),
        in_specs=[whole] * 6,
        out_specs=whole,
        compiler_params=pltpu.CompilerParams(vmem_limit_bytes=48 << 20),
        cost_estimate=pl.CostEstimate(
            flops=4 * heads * group * count * rows * HD,
            bytes_accessed=projected.size * 4 + 4 * queries.size,
            transcendentals=heads * group * count * rows,
        ),
        name="rotate_attend",
    )(projected, cosine, sine, key_info, query_info, queries)


def add_kernel(pieces, has_total, *refs):
    at_ref, refs = refs[0], refs[1:]
    hidden, weight = refs[:pieces], refs[pieces : 2 * pieces]
    total = refs[2 * pieces][...] if has_total else None
    for columns, piece in zip(hidden, weight):
        term = jnp.dot(columns[...], piece[...], preferred_element_type=jnp.float32)
        total = term if total is None else total + term
    refs[-1][...] = total


def add_products(total, hidden, weights, blocks):
    rows = hidden.shape[0]
    depth, width = weights[0].shape
    tile = min(width, 256)
    pieces = len(weights)
    out_block = pl.BlockSpec((rows, tile), lambda n, at: (0, n))
    in_specs = [
        pl.BlockSpec((rows, depth), functools.partial(lambda p, n, at: (0, at[p]), p))
        for p in range(pieces)
    ]
    in_specs += [pl.BlockSpec((depth, tile), lambda n, at: (0, n))] * pieces
    operands = [jnp.stack(blocks), *[hidden] * pieces, *weights]
    if total is not None:
        in_specs.append(out_block)
        operands.append(total)
    return pl.pallas_call(
        functools.partial(add_kernel, pieces, total is not None),
        out_shape=jax.ShapeDtypeStruct((rows, width), jnp.float32),
        grid_spec=pltpu.PrefetchScalarGridSpec(
            num_scalar_prefetch=1, grid=(width // tile,), in_specs=in_specs, out_specs=out_block
        ),
        input_output_aliases={} if total is None else {len(operands) - 1: 0},
        compiler_params=pltpu.CompilerParams(vmem_limit_bytes=32 << 20),
        cost_estimate=pl.CostEstimate(
            flops=2 * rows * depth * width * pieces,
            bytes_accessed=pieces * 2 * (rows * depth + depth * width) + 8 * rows * width,
            transcendentals=0,
        ),
        name="add_products",
    )(*operands)


def ring_order(row_count):
    evens = list(range(0, row_count, 2))
    odds = list(range(1, row_count, 2))
    return evens + odds[::-1]


def body(passages, kv_weight, new_hidden, queries, lengths, destinations):
    tokens = passages.shape[0]
    requests, steps, half_model = new_hidden.shape
    row_index = lax.axis_index("rows")
    count = requests * steps
    padded = -(-(tokens + count) // 16) * 16

    row_count = lax.axis_size("rows")
    depth = kv_weight.shape[0]
    half = depth // 2
    weight = kv_weight.reshape(depth, -1)
    order = ring_order(row_count)
    onward = [(order[i], order[(i + 1) % row_count]) for i in range(row_count)]
    back = [(b, a) for a, b in onward]
    place = {row: i for i, row in enumerate(order)}
    owners = jnp.array(
        [
            [
                [order[(place[r] - k) % row_count] for k in range(row_count)],
                [order[(place[r] + k) % row_count] for k in range(row_count)],
            ]
            for r in range(row_count)
        ],
        jnp.int32,
    )
    owners = lax.dynamic_index_in_dim(owners, row_index, 0, keepdims=False)
    pieces = [(weight[:half], weight[half:])]
    for _ in range(row_count - 1):
        first, second = pieces[-1]
        pieces.append((lax.ppermute(first, "rows", onward), lax.ppermute(second, "rows", back)))

    moved = jnp.concatenate([new_hidden, queries], 1)
    moved = lax.all_to_all(moved, "rows", split_axis=0, concat_axis=0, tiled=True)
    moved = jnp.swapaxes(moved, 0, 1)
    new_rows = moved[:steps].reshape(count, half_model)
    query_rows = moved[steps:].reshape(count, -1)

    hidden = jnp.concatenate(
        [passages, new_rows, jnp.zeros((padded - tokens - count, half_model), passages.dtype)], 0
    )
    hidden = lax.all_gather(hidden, "tensor", axis=1, tiled=True)

    position, key_info, query_info = token_tables(
        lengths, destinations, row_index, tokens, requests, steps, padded
    )
    cosine, sine = angle_tables(position)
    projected = None
    for k in range(row_count):
        blocks = [2 * owners[side, k] + side for side in range(2)]
        projected = add_products(projected, hidden, pieces[k], blocks)
    attended = finish(projected, cosine, sine, key_info, query_info, query_rows)
    attended = jnp.swapaxes(attended.reshape(steps, requests, -1), 0, 1)
    return lax.all_to_all(attended, "rows", split_axis=0, concat_axis=0, tiled=True)


def solution(mesh):
    placed = (
        P(("groups", "rows"), "tensor"),
        P("rows", None, "tensor"),
        P(("groups", "rows"), None, "tensor"),
        P(("groups", "rows"), None, "tensor"),
        P("groups", None),
        P("groups", None),
    )
    return jax.shard_map(
        body,
        mesh=mesh,
        in_specs=placed,
        out_specs=P(("groups", "rows"), None, "tensor"),
        check_vma=False,
    )
```

```python
import functools
import math

import jax
import jax.numpy as jnp
from jax import lax
from jax.experimental import pallas as pl
from jax.experimental.pallas import tpu as pltpu
from jax.sharding import PartitionSpec as P

HD = 128
HALF = HD // 2
CHUNKS = 2
LAG = 3
MOST_SHARDS = 8
MERGED = 4
RAISE = 16.0


def angle_tables(positions):
    index_float = jnp.arange(HALF, dtype=jnp.float32)
    inverse = jnp.exp(index_float * (-2.0 * math.log(1000000.0) / HD))
    angles = positions.astype(jnp.float32)[:, None] * inverse
    return jnp.cos(angles), jnp.sin(angles)


def token_tables(lengths, destinations, row_index, tokens, requests, steps, padded):
    my_lengths = lax.dynamic_index_in_dim(lengths, row_index, 0, keepdims=False)
    my_targets = lax.dynamic_index_in_dim(destinations, row_index, 0, keepdims=False)
    ends = jnp.cumsum(my_lengths)
    starts = ends - my_lengths
    token = jnp.arange(tokens, dtype=jnp.int32)[:, None]
    inside = (starts[None, :] <= token) & (token < ends[None, :])
    token_position = token[:, 0] - jnp.sum(jnp.where(inside, starts[None, :], 0), axis=1)
    token_target = jnp.sum(jnp.where(inside, my_targets[None, :], 0), axis=1)
    row_ids = jnp.arange(requests, dtype=jnp.int32)
    sending = my_targets[None, :] == row_ids[:, None]
    target_length = jnp.sum(jnp.where(sending, my_lengths[None, :], 0), axis=1)
    step = jnp.repeat(jnp.arange(steps, dtype=jnp.int32), requests)
    new_target = jnp.tile(row_ids, steps)
    new_position = jnp.tile(target_length, steps) + step
    spare = jnp.zeros((padded - tokens - requests * steps,), jnp.int32)
    position = jnp.concatenate([token_position, new_position, spare])
    target = jnp.concatenate([token_target, new_target, spare - 1])
    seen_from = jnp.concatenate([jnp.zeros_like(token_target), step, spare])
    query_info = jnp.stack([new_target, step], 1)
    return position, jnp.stack([target, seen_from], 0), query_info


def finish_kernel(heads, group, held_ref, back_ref, cos_ref, sin_ref, keys_ref, rows_ref, query_ref, out_ref):
    cosine, sine = cos_ref[...], sin_ref[...]
    allowed = (keys_ref[0:1, :] == rows_ref[:, 0:1]) & (keys_ref[1:2, :] <= rows_ref[:, 1:2])
    allowed = jnp.concatenate([allowed.astype(jnp.float32)] * group, 0) > 0.5
    queries = query_ref[...].astype(jnp.float32)
    count = queries.shape[0]
    width = heads * HD
    for h in range(heads):
        key_at, value_at = slice(h * HD, (h + 1) * HD), slice(width + h * HD, width + (h + 1) * HD)
        both = held_ref[:, key_at] + back_ref[:, key_at]
        first, second = both[:, :HALF], both[:, HALF:]
        keys = jnp.concatenate(
            [first * cosine - second * sine, second * cosine + first * sine], -1
        ).astype(jnp.bfloat16)
        values = held_ref[:, value_at] + back_ref[:, value_at]
        values = values.astype(jnp.bfloat16)
        at = h * group * HD
        query = jnp.concatenate(
            [queries[:, at + g * HD : at + (g + 1) * HD] for g in range(group)], 0
        ).astype(jnp.bfloat16)
        scores = lax.dot_general(
            query, keys, (((1,), (1,)), ((), ())), preferred_element_type=jnp.float32
        )
        scores = jnp.where(allowed, scores * (1.0 / math.sqrt(HD)), jnp.float32(-1e30))
        raised = jnp.exp(scores - jnp.max(scores, axis=-1, keepdims=True))
        total = jnp.sum(raised, axis=-1, keepdims=True)
        weights = (raised / total).astype(jnp.bfloat16)
        output = jnp.dot(weights, values, preferred_element_type=jnp.float32)
        for g in range(group):
            out_ref[:, at + g * HD : at + (g + 1) * HD] = output[
                g * count : (g + 1) * count
            ].astype(jnp.bfloat16)


def finish(projected, back, cosine, sine, key_info, query_info, queries):
    rows, width = projected.shape
    heads = width // (2 * HD)
    group = queries.shape[1] // (heads * HD)
    count = queries.shape[0]
    whole = pl.BlockSpec(memory_space=pltpu.VMEM)
    return pl.pallas_call(
        functools.partial(finish_kernel, heads, group),
        out_shape=jax.ShapeDtypeStruct(queries.shape, jnp.bfloat16),
        in_specs=[whole] * 7,
        out_specs=whole,
        compiler_params=pltpu.CompilerParams(vmem_limit_bytes=48 << 20),
        cost_estimate=pl.CostEstimate(
            flops=4 * heads * group * count * rows * HD,
            bytes_accessed=projected.size * 8 + 4 * queries.size,
            transcendentals=heads * group * count * rows,
        ),
        name="rotate_attend",
    )(projected, back, cosine, sine, key_info, query_info, queries)


def pick_kernel(side_ref, source_ref, out_ref):
    out_ref[...] = source_ref[...]


def pick_columns(source, side, half, first, count):
    rows = source.shape[0]
    return pl.pallas_call(
        pick_kernel,
        out_shape=jax.ShapeDtypeStruct((rows, count * half), source.dtype),
        grid_spec=pltpu.PrefetchScalarGridSpec(
            num_scalar_prefetch=1,
            grid=(count,),
            in_specs=[pl.BlockSpec((rows, half), lambda j, s: (0, 2 * (first + j) + s[0]))],
            out_specs=pl.BlockSpec((rows, half), lambda j, s: (0, j)),
        ),
        compiler_params=pltpu.CompilerParams(vmem_limit_bytes=24 << 20),
        cost_estimate=pl.CostEstimate(
            flops=0, bytes_accessed=4 * rows * count * half, transcendentals=0
        ),
        name="pick_columns",
    )(side.reshape(1), source)


def product_kernel(shards, split, layout, has_total, *refs):
    place_ref, refs = refs[0], refs[1:]
    hidden, refs = refs[: len(layout)], refs[len(layout) :]
    weights, refs = refs[: shards * split], refs[shards * split :]
    out_ref, held, sems = refs[-3:]
    half = held.shape[1] // shards
    spans = sorted({(part, at, rows) for part, at, rows, _, _, _ in layout})
    for p in range(shards):
        for (part, at, rows, row, first, blocks), source in zip(layout, hidden):
            block = place_ref[p] - first

            @pl.when((block >= 0) & (block < blocks))
            def _():
                columns = pl.ds(pl.multiple_of(block * half, half), half)
                pltpu.make_async_copy(
                    source.at[row : row + rows, columns],
                    held.at[at : at + rows, p * half : (p + 1) * half],
                    sems.at[p, part],
                ).start()

    total = refs[0][...] if has_total else None
    for begin in range(0, shards, MERGED):
        end = min(begin + MERGED, shards)
        for p in range(begin, end):
            for part, at, rows in spans:
                target = held.at[at : at + rows, p * half : (p + 1) * half]
                pltpu.make_async_copy(target, target, sems.at[p, part]).wait()
        piece = jnp.concatenate([w[...] for w in weights[begin * split : end * split]], 0)
        term = jnp.dot(
            held[:, begin * half : end * half], piece, preferred_element_type=jnp.float32
        )
        total = term if total is None else total + term
    out_ref[...] = total


def products(total, hidden, weights, places, half):
    split, shards = len(weights[0]), len(weights)
    width = weights[0][0].shape[1]
    operands, layout, at = [places], [], 0
    for part, (row, rows, pieces) in enumerate(hidden):
        first = 0
        for piece in pieces:
            operands.append(piece)
            layout.append((part, at, rows, row, first, piece.shape[1] // half))
            first += piece.shape[1] // half
        at += rows
    flat = [w for shard in weights for w in shard]
    operands += flat
    vmem = pl.BlockSpec(memory_space=pltpu.VMEM)
    in_specs = [pl.BlockSpec(memory_space=pltpu.SMEM)]
    in_specs += [pl.BlockSpec(memory_space=pl.ANY)] * len(layout) + [vmem] * len(flat)
    if total is not None:
        operands.append(total)
        in_specs.append(vmem)
    return pl.pallas_call(
        functools.partial(product_kernel, shards, split, tuple(layout), total is not None),
        out_shape=jax.ShapeDtypeStruct((at, width), jnp.float32),
        in_specs=in_specs,
        out_specs=vmem,
        scratch_shapes=[
            pltpu.VMEM((at, shards * half), jnp.bfloat16),
            pltpu.SemaphoreType.DMA((shards, len(hidden))),
        ],
        compiler_params=pltpu.CompilerParams(vmem_limit_bytes=40 << 20),
        cost_estimate=pl.CostEstimate(
            flops=2 * at * half * width * shards,
            bytes_accessed=shards * 2 * half * (at + width) + 4 * at * width,
            transcendentals=0,
        ),
        name="products",
    )(*operands)


def ring_order(row_count):
    evens = list(range(0, row_count, 2))
    odds = list(range(1, row_count, 2))
    return evens + odds[::-1]


def after(value, other):
    return lax.optimization_barrier((value, other))[0]


def body(passages, kv_weight, new_hidden, queries, lengths, destinations):
    tokens = passages.shape[0]
    requests, steps, half_model = new_hidden.shape
    row_count = lax.axis_size("rows")
    group_count = lax.axis_size("groups")
    row_index = lax.axis_index("rows")
    side = lax.axis_index("groups") % 2
    core = lax.axis_index("tensor")
    depth = kv_weight.shape[0]
    half = depth // 2
    local_heads = kv_weight.shape[2] // HD
    group = queries.shape[2] // kv_weight.shape[2]
    count = requests * steps
    new_padded = -(-count // 16) * 16
    half_rows = row_count // 2

    partners = [(g, g ^ 1) for g in range(group_count)]
    cores = [(0, 1), (1, 0)]
    order = ring_order(row_count)
    onward = [(order[i], order[(i + 1) % row_count]) for i in range(row_count)]
    back = [(b, a) for a, b in onward]
    place = {row: i for i, row in enumerate(order)}
    shard_order = [
        [order[(place[r] + d) % row_count] for r in range(row_count)]
        for k in range(half_rows + 1)
        for d in ([0] if k == 0 else [-k, k] if k < half_rows else [k])
    ]
    owners = lax.dynamic_index_in_dim(jnp.array(shard_order, jnp.int32), row_index, 1, keepdims=False)
    places = ((owners // half_rows) ^ core) * half_rows + owners % half_rows

    chunks = CHUNKS
    chunk_heads = local_heads // chunks
    chunk = chunk_heads * HD
    mine = lax.dynamic_slice_in_dim(kv_weight, side * half, half, 0)
    own = [
        mine[:, :, c * chunk : (c + 1) * chunk].reshape(half, 2 * chunk) for c in range(chunks)
    ]

    sent = [pick_columns(passages, 1 - side, half, at, half_rows // 2) for at in (0, half_rows // 2)]
    got = [lax.ppermute(sent[0], "groups", partners)]

    right, left = [[] for _ in range(chunks)], [[] for _ in range(chunks)]

    def ring_step(c):
        k = len(right[c])
        r, l = (own[c], own[c]) if k == 0 else (right[c][-1], left[c][-1])
        if k == half_rows - 1:
            r, l = r[: half // 2], l[half // 2 :]
        if k == 0 and c == 0:
            r, l = after((r, l), sent[0])
        if k == 0 and c > 0:
            r, l = after((r, l), (right[c - 1][LAG - 1], left[c - 1][LAG - 1]))
        if k == 2 and c == 0:
            r, l = after((r, l), got[0])
        if k == 1 and c == 1:
            r, l = after((r, l), got[1])
        right[c].append(lax.ppermute(r, "rows", onward))
        left[c].append(lax.ppermute(l, "rows", back))
        if k == 1 and c == 0:
            got.append(lax.ppermute(after(sent[1], arrived((0, 1))), "groups", partners))

    def arrived(*steps_done):
        return [side_of[c][k] for c, k in steps_done for side_of in (right, left)]

    for c in range(chunks):
        for k in range(half_rows):
            ring_step(c)

    kept = pick_columns(passages, side, half, 0, half_rows)
    kept_other = lax.ppermute(kept, "tensor", cores)
    got = [
        after(got[0], arrived((0, 1))),
        after(got[1], arrived((0, half_rows - 1), (1, 0))),
    ]
    got_other = [lax.ppermute(piece, "tensor", cores) for piece in got]

    def to_replica(held, start, end):
        moved = lax.all_to_all(after(held, start), "rows", split_axis=0, concat_axis=0, tiled=True)
        return jnp.swapaxes(after(moved, end), 0, 1).reshape(count, -1)

    new_rows = to_replica(new_hidden, (kept, sent), arrived((0, 1)))
    new_rows = jnp.pad(new_rows, ((0, new_padded - count), (0, 0)))
    new_kept = pick_columns(new_rows, side, half, 0, half_rows)
    new_sent = pick_columns(new_rows, 1 - side, half, 0, half_rows)
    new_got = lax.ppermute(new_sent, "groups", partners)
    new_got = after(new_got, arrived((0, 2)))
    new_kept = jnp.concatenate([new_kept, new_got], 0)
    new_other = lax.ppermute(new_kept, "tensor", cores)
    own_hidden = [(0, tokens, (kept, kept_other)), (0, new_padded, (new_kept, new_other))]
    away_hidden = [(0, tokens, (*got, *got_other)), (new_padded, new_padded, (new_kept, new_other))]
    query_rows = to_replica(queries, arrived((1, 1)), arrived((1, half_rows - 1)))

    position, key_info, query_info = token_tables(
        lengths, destinations, row_index, tokens, requests, steps, tokens + new_padded
    )
    cosine, sine = angle_tables(position)

    def project(c, hidden, ready):
        weights = [(own[c],)]
        for k in range(half_rows - 1):
            weights += [(right[c][k],), (left[c][k],)]
        shards, total = len(weights), None
        spots = after(places, ready)
        for at in range(0, shards, MOST_SHARDS):
            some = weights[at : at + MOST_SHARDS]
            total = products(total, hidden, some, spots[at : at + len(some)], half)
        return products(total, hidden, [(right[c][-1], left[c][-1])], spots[shards:], half)

    away = [project(c, away_hidden, ()) for c in range(chunks)]
    away = [(total * RAISE).astype(jnp.float16) for total in away]
    homed = [lax.ppermute(total, "groups", partners) for total in away]
    homed = [total.astype(jnp.float32) * (1.0 / RAISE) for total in homed]

    outs = []
    for c in range(chunks):
        held = project(c, own_hidden, away[c])
        at = c * chunk * group
        query = query_rows[:, at : at + chunk * group]
        outs.append(finish(held, homed[c], cosine, sine, key_info, query_info, query))
    attended = outs[0] if chunks == 1 else jnp.concatenate(outs, 1)
    attended = jnp.swapaxes(attended.reshape(steps, requests, -1), 0, 1)
    return lax.all_to_all(attended, "rows", split_axis=0, concat_axis=0, tiled=True)


def solution(mesh):
    placed = (
        P(("groups", "rows"), "tensor"),
        P("rows", None, "tensor"),
        P(("groups", "rows"), None, "tensor"),
        P(("groups", "rows"), None, "tensor"),
        P("groups", None),
        P("groups", None),
    )
    return jax.shard_map(
        body,
        mesh=mesh,
        in_specs=placed,
        out_specs=P(("groups", "rows"), None, "tensor"),
        check_vma=False,
    )
```

```python
import functools
import math

import jax
import jax.numpy as jnp
from jax import lax
from jax.experimental import pallas as pl
from jax.experimental.pallas import tpu as pltpu
from jax.sharding import PartitionSpec as P

HD = 128
HALF = HD // 2
CHUNKS = 2
MOST_SHARDS = 8
VMEM_BYTES = 56 << 20
MERGED = 4
RAISE = 16.0


def angle_tables(positions):
    index_float = jnp.arange(HALF, dtype=jnp.float32)
    inverse = jnp.exp(index_float * (-2.0 * math.log(1000000.0) / HD))
    angles = positions.astype(jnp.float32)[:, None] * inverse
    return jnp.cos(angles), jnp.sin(angles)


def token_tables(lengths, destinations, row_index, tokens, requests, steps, padded):
    my_lengths = lax.dynamic_index_in_dim(lengths, row_index, 0, keepdims=False)
    my_targets = lax.dynamic_index_in_dim(destinations, row_index, 0, keepdims=False)
    ends = jnp.cumsum(my_lengths)
    starts = ends - my_lengths
    token = jnp.arange(tokens, dtype=jnp.int32)[:, None]
    inside = (starts[None, :] <= token) & (token < ends[None, :])
    token_position = token[:, 0] - jnp.sum(jnp.where(inside, starts[None, :], 0), axis=1)
    token_target = jnp.sum(jnp.where(inside, my_targets[None, :], 0), axis=1)
    row_ids = jnp.arange(requests, dtype=jnp.int32)
    sending = my_targets[None, :] == row_ids[:, None]
    target_length = jnp.sum(jnp.where(sending, my_lengths[None, :], 0), axis=1)
    step = jnp.repeat(jnp.arange(steps, dtype=jnp.int32), requests)
    new_target = jnp.tile(row_ids, steps)
    new_position = jnp.tile(target_length, steps) + step
    spare = jnp.zeros((padded - tokens - requests * steps,), jnp.int32)
    position = jnp.concatenate([token_position, new_position, spare])
    target = jnp.concatenate([token_target, new_target, spare - 1])
    seen_from = jnp.concatenate([jnp.zeros_like(token_target), step, spare])
    query_info = jnp.stack([new_target, step], 1)
    return position, jnp.stack([target, seen_from], 0), query_info


def finish_kernel(heads, group, held_ref, back_ref, cos_ref, sin_ref, keys_ref, rows_ref, query_ref, out_ref):
    cosine, sine = cos_ref[...], sin_ref[...]
    allowed = (keys_ref[0:1, :] == rows_ref[:, 0:1]) & (keys_ref[1:2, :] <= rows_ref[:, 1:2])
    allowed = jnp.concatenate([allowed.astype(jnp.float32)] * group, 0) > 0.5
    queries = query_ref[...].astype(jnp.float32)
    count = queries.shape[0]
    width = heads * HD
    for h in range(heads):
        key_at, value_at = slice(h * HD, (h + 1) * HD), slice(width + h * HD, width + (h + 1) * HD)
        both = held_ref[:, key_at] + back_ref[:, key_at]
        first, second = both[:, :HALF], both[:, HALF:]
        keys = jnp.concatenate(
            [first * cosine - second * sine, second * cosine + first * sine], -1
        ).astype(jnp.bfloat16)
        values = held_ref[:, value_at] + back_ref[:, value_at]
        values = values.astype(jnp.bfloat16)
        at = h * group * HD
        query = jnp.concatenate(
            [queries[:, at + g * HD : at + (g + 1) * HD] for g in range(group)], 0
        ).astype(jnp.bfloat16)
        scores = lax.dot_general(
            query, keys, (((1,), (1,)), ((), ())), preferred_element_type=jnp.float32
        )
        scores = jnp.where(allowed, scores * (1.0 / math.sqrt(HD)), jnp.float32(-1e30))
        raised = jnp.exp(scores - jnp.max(scores, axis=-1, keepdims=True))
        total = jnp.sum(raised, axis=-1, keepdims=True)
        weights = (raised / total).astype(jnp.bfloat16)
        output = jnp.dot(weights, values, preferred_element_type=jnp.float32)
        for g in range(group):
            out_ref[:, at + g * HD : at + (g + 1) * HD] = output[
                g * count : (g + 1) * count
            ].astype(jnp.bfloat16)


def finish(projected, back, cosine, sine, key_info, query_info, queries):
    rows, width = projected.shape
    heads = width // (2 * HD)
    group = queries.shape[1] // (heads * HD)
    count = queries.shape[0]
    whole = pl.BlockSpec(memory_space=pltpu.VMEM)
    return pl.pallas_call(
        functools.partial(finish_kernel, heads, group),
        out_shape=jax.ShapeDtypeStruct(queries.shape, jnp.bfloat16),
        in_specs=[whole] * 7,
        out_specs=whole,
        compiler_params=pltpu.CompilerParams(vmem_limit_bytes=48 << 20),
        cost_estimate=pl.CostEstimate(
            flops=4 * heads * group * count * rows * HD,
            bytes_accessed=projected.size * 8 + 4 * queries.size,
            transcendentals=heads * group * count * rows,
        ),
        name="rotate_attend",
    )(projected, back, cosine, sine, key_info, query_info, queries)


def pick_kernel(half, first, side_ref, source_ref, out_ref, sems):
    rows, width = out_ref.shape
    copies = []
    for j in range(width // half):
        at = pl.multiple_of((2 * j + side_ref[0]) * half, half)
        copies.append(
            pltpu.make_async_copy(
                source_ref.at[first : first + rows, pl.ds(at, half)],
                out_ref.at[:, j * half : (j + 1) * half],
                sems.at[j],
            )
        )
        copies[-1].start()
    for copy in copies:
        copy.wait()


def pick_columns(source, side, half, first, end):
    count = source.shape[1] // (2 * half)
    return pl.pallas_call(
        functools.partial(pick_kernel, half, first),
        out_shape=jax.ShapeDtypeStruct((end - first, count * half), source.dtype),
        in_specs=[pl.BlockSpec(memory_space=pltpu.SMEM), pl.BlockSpec(memory_space=pl.ANY)],
        out_specs=pl.BlockSpec(memory_space=pl.ANY),
        scratch_shapes=[pltpu.SemaphoreType.DMA((count,))],
        compiler_params=pltpu.CompilerParams(vmem_limit_bytes=VMEM_BYTES),
        cost_estimate=pl.CostEstimate(
            flops=0, bytes_accessed=4 * (end - first) * count * half, transcendentals=0
        ),
        name="pick_columns",
    )(side.reshape(1), source)


def product_kernel(depths, layout, column, has_total, *refs):
    place_ref, refs = refs[0], refs[1:]
    hidden, refs = refs[: len(layout)], refs[len(layout) :]
    flat = [depth for pieces in depths for depth in pieces]
    weights, refs = refs[: len(flat)], refs[len(flat) :]
    out_ref, held, piece, sems, piece_sems = refs[-5:]
    shards = len(depths)
    half = held.shape[1] // shards
    spans = sorted({(part, at, rows) for part, at, rows, _, _, _ in layout})
    tops = [sum(flat[:i]) for i in range(len(flat))]
    copies = [
        pltpu.make_async_copy(
            w.at[:, column : column + piece.shape[1]] if w.shape[1] > piece.shape[1] else w,
            piece.at[top : top + depth, :],
            piece_sems.at[i],
        )
        for i, (w, top, depth) in enumerate(zip(weights, tops, flat))
    ]
    done = 0
    for p in range(shards):
        for _ in depths[p]:
            copies[done].start()
            done += 1
        for (part, at, rows, row, first, blocks), source in zip(layout, hidden):
            block = place_ref[p] - first

            @pl.when((block >= 0) & (block < blocks))
            def _():
                columns = pl.ds(pl.multiple_of(block * half, half), half)
                pltpu.make_async_copy(
                    source.at[row : row + rows, columns],
                    held.at[at : at + rows, p * half : (p + 1) * half],
                    sems.at[p, part],
                ).start()

    total = refs[0][...] if has_total else None
    waited = 0
    for begin in range(0, shards, MERGED):
        end = min(begin + MERGED, shards)
        for p in range(begin, end):
            for part, at, rows in spans:
                target = held.at[at : at + rows, p * half : (p + 1) * half]
                pltpu.make_async_copy(target, target, sems.at[p, part]).wait()
            for _ in depths[p]:
                copies[waited].wait()
                waited += 1
        span = slice(begin * half, end * half)
        term = jnp.dot(held[:, span], piece[span, :], preferred_element_type=jnp.float32)
        total = term if total is None else total + term
    out_ref[...] = total


def products(total, hidden, weights, places, column, width):
    shards = len(weights)
    flat = [w for shard in weights for w in shard]
    depths = tuple(tuple(w.shape[0] for w in shard) for shard in weights)
    half = sum(depths[0])
    operands, layout, at = [places], [], 0
    for part, (row, rows, pieces) in enumerate(hidden):
        first = 0
        for piece in pieces:
            operands.append(piece)
            layout.append((part, at, rows, row, first, piece.shape[1] // half))
            first += piece.shape[1] // half
        at += rows
    operands += flat
    vmem = pl.BlockSpec(memory_space=pltpu.VMEM)
    in_specs = [pl.BlockSpec(memory_space=pltpu.SMEM)]
    in_specs += [pl.BlockSpec(memory_space=pl.ANY)] * (len(layout) + len(flat))
    if total is not None:
        operands.append(total)
        in_specs.append(vmem)
    return pl.pallas_call(
        functools.partial(product_kernel, depths, tuple(layout), column, total is not None),
        out_shape=jax.ShapeDtypeStruct((at, width), jnp.float32),
        in_specs=in_specs,
        out_specs=vmem,
        scratch_shapes=[
            pltpu.VMEM((at, shards * half), jnp.bfloat16),
            pltpu.VMEM((shards * half, width), jnp.bfloat16),
            pltpu.SemaphoreType.DMA((shards, len(hidden))),
            pltpu.SemaphoreType.DMA((len(flat),)),
        ],
        compiler_params=pltpu.CompilerParams(vmem_limit_bytes=VMEM_BYTES),
        cost_estimate=pl.CostEstimate(
            flops=2 * at * half * width * shards,
            bytes_accessed=shards * 2 * half * (at + width) + 4 * at * width,
            transcendentals=0,
        ),
        name="products",
    )(*operands)


def ring_order(row_count):
    evens = list(range(0, row_count, 2))
    odds = list(range(1, row_count, 2))
    return evens + odds[::-1]


def fence(*values):
    return lax.optimization_barrier(values)


def body(passages, kv_weight, new_hidden, queries, lengths, destinations):
    tokens = passages.shape[0]
    requests, steps, half_model = new_hidden.shape
    row_count = lax.axis_size("rows")
    group_count = lax.axis_size("groups")
    row_index = lax.axis_index("rows")
    side = lax.axis_index("groups") % 2
    core = lax.axis_index("tensor")
    depth = kv_weight.shape[0]
    half = depth // 2
    local_heads = kv_weight.shape[2] // HD
    group = queries.shape[2] // kv_weight.shape[2]
    count = requests * steps
    new_padded = -(-count // 16) * 16
    half_rows = row_count // 2

    partners = [(g, g ^ 1) for g in range(group_count)]
    cores = [(0, 1), (1, 0)]
    order = ring_order(row_count)
    onward = [(order[i], order[(i + 1) % row_count]) for i in range(row_count)]
    back = [(b, a) for a, b in onward]
    place = {row: i for i, row in enumerate(order)}
    shard_order = [
        [order[(place[r] + d) % row_count] for r in range(row_count)]
        for k in range(half_rows + 1)
        for d in ([0] if k == 0 else [-k, k] if k < half_rows else [k])
    ]
    owners = lax.dynamic_index_in_dim(jnp.array(shard_order, jnp.int32), row_index, 1, keepdims=False)
    places = ((owners // half_rows) ^ core) * half_rows + owners % half_rows

    chunk = kv_weight.shape[2] // CHUNKS
    own = lax.dynamic_slice_in_dim(kv_weight, side * half, half, 0)
    own = own.reshape(half, 2, CHUNKS, chunk).swapaxes(1, 2).reshape(half, -1)
    width = 2 * chunk

    def step(pair):
        return lax.ppermute(pair[0], "rows", onward), lax.ppermute(pair[1], "rows", back)

    third = -(-tokens // 48) * 16
    cuts = (0, third, 2 * third, tokens)
    sent = [pick_columns(passages, 1 - side, half, cuts[0], cuts[1])]
    own, sent[0], passages, new_hidden = fence(own, sent[0], passages, new_hidden)
    got = [lax.ppermute(sent[0], "groups", partners)]
    ring = [step((own, own))]
    sent += [pick_columns(passages, 1 - side, half, *cuts[i : i + 2]) for i in (1, 2)]
    kept = pick_columns(passages, side, half, 0, tokens)
    kept_other = lax.ppermute(kept, "tensor", cores)
    new_hidden, kept = fence(new_hidden, kept)
    moved = lax.all_to_all(new_hidden, "rows", split_axis=0, concat_axis=0, tiled=True)
    ring[0], got[0], moved, kept_other, sent, queries = fence(
        ring[0], got[0], moved, kept_other, sent, queries
    )

    got.append(lax.ppermute(sent[1], "groups", partners))
    ring.append(step(ring[-1]))
    new_rows = jnp.swapaxes(moved, 0, 1).reshape(count, half_model)
    new_rows = jnp.pad(new_rows, ((0, new_padded - count), (0, 0)))
    new_sent = pick_columns(new_rows, 1 - side, half, 0, new_padded)
    new_got = lax.ppermute(new_sent, "groups", partners)
    new_kept = pick_columns(new_rows, side, half, 0, new_padded)
    new_kept = jnp.concatenate([new_kept, new_got], 0)
    new_other = lax.ppermute(new_kept, "tensor", cores)
    got_other = [lax.ppermute(got[0], "tensor", cores)]
    ring[1], got[1], new_other, got_other, places, queries = fence(
        ring[1], got[1], new_other, got_other, places, queries
    )

    def project(hidden, total, begin, end, column, width):
        weights = [(own,)] + [(w,) for pair in ring for w in pair]
        weights = weights[: row_count - 1] + [last[column // width] if last else ()]
        for at in range(begin, end, MOST_SHARDS):
            some = weights[at : min(at + MOST_SHARDS, end)]
            spots = places[at : at + len(some)]
            total = products(total, hidden, some, spots, column, width)
        return total

    def homeward(total):
        return (total * RAISE).astype(jnp.float16)

    last = []
    own_hidden = [(0, tokens, (kept, kept_other)), (0, new_padded, (new_kept, new_other))]
    early = row_count - 3
    for k in range(2, half_rows - 1):
        if k > 2:
            ring[-1] = fence(*ring[-1])
        else:
            got.append(lax.ppermute(sent[2], "groups", partners))
            got_other.append(lax.ppermute(got[1], "tensor", cores))
            moved = lax.all_to_all(queries, "rows", split_axis=0, concat_axis=0, tiled=True)
        ring.append(step(ring[-1]))
    held = project(own_hidden, None, 0, early, 0, 2 * width)
    position, key_info, query_info = token_tables(
        lengths, destinations, row_index, tokens, requests, steps, tokens + new_padded
    )
    cosine, sine = angle_tables(position)

    def halved(c):
        columns = slice(c * width, (c + 1) * width)
        return ring[-1][0][: half // 2, columns], ring[-1][1][half // 2 :, columns]

    ends = [halved(0)]
    ring[-1], got[2], got_other, moved, held, ends, places, cosine, sine = fence(
        ring[-1], got[2], got_other, moved, held, ends, places, cosine, sine
    )
    query_rows = jnp.swapaxes(moved, 0, 1).reshape(count, -1)

    last.append(step(ends[0]))
    got_other.append(lax.ppermute(got[2], "tensor", cores))
    away_hidden = [
        (0, piece.shape[0], (piece, other)) for piece, other in zip(got, got_other)
    ] + [(new_padded, new_padded, (new_kept, new_other))]
    away = [project(away_hidden, None, 0, row_count - 1, 0, width)]
    ends.append(halved(1))
    last[0], away, ends, places = fence(last[0], away, ends, places)

    last.append(step(ends[1]))
    away[0] = homeward(project(away_hidden, away[0], row_count - 1, row_count, 0, width))
    away[0], places = fence(away[0], places)
    homed = [lax.ppermute(away[0], "groups", partners)]
    away.append(project(away_hidden, None, 0, row_count - 1, width, width))
    away[1] = homeward(project(away_hidden, away[1], row_count - 1, row_count, width, width))
    homed[0], away[1], places = fence(homed[0], away[1], places)

    homed.append(lax.ppermute(away[1], "groups", partners))
    outs = []
    for c in range(CHUNKS):
        back_home = homed[c].astype(jnp.float32) * (1.0 / RAISE)
        mine = held[:, c * width : (c + 1) * width]
        mine = project(own_hidden, mine, early, row_count, c * width, width)
        at = c * chunk * group
        query = query_rows[:, at : at + chunk * group]
        outs.append(finish(mine, back_home, cosine, sine, key_info, query_info, query))
    attended = jnp.concatenate(outs, 1)
    attended = jnp.swapaxes(attended.reshape(steps, requests, -1), 0, 1)
    return lax.all_to_all(attended, "rows", split_axis=0, concat_axis=0, tiled=True)


def solution(mesh):
    placed = (
        P(("groups", "rows"), "tensor"),
        P("rows", None, "tensor"),
        P(("groups", "rows"), None, "tensor"),
        P(("groups", "rows"), None, "tensor"),
        P("groups", None),
        P("groups", None),
    )
    return jax.shard_map(
        body,
        mesh=mesh,
        in_specs=placed,
        out_specs=P(("groups", "rows"), None, "tensor"),
        check_vma=False,
    )
```

```python
import functools
import math

import jax
import jax.numpy as jnp
from jax import lax
from jax.experimental import pallas as pl
from jax.experimental.pallas import tpu as pltpu
from jax.sharding import PartitionSpec as P

HD = 128
HALF = HD // 2
CHUNKS = 2
MOST_SHARDS = 8
VMEM_BYTES = 32 << 20
MERGED = 4
RAISE = 16.0


def angle_tables(positions):
    index_float = jnp.arange(HALF, dtype=jnp.float32)
    inverse = jnp.exp(index_float * (-2.0 * math.log(1000000.0) / HD))
    angles = positions.astype(jnp.float32)[:, None] * inverse
    return jnp.cos(angles), jnp.sin(angles)


def token_tables(lengths, destinations, row_index, tokens, requests, steps, padded):
    my_lengths = lax.dynamic_index_in_dim(lengths, row_index, 0, keepdims=False)
    my_targets = lax.dynamic_index_in_dim(destinations, row_index, 0, keepdims=False)
    ends = jnp.cumsum(my_lengths)
    starts = ends - my_lengths
    token = jnp.arange(tokens, dtype=jnp.int32)[:, None]
    inside = (starts[None, :] <= token) & (token < ends[None, :])
    token_position = token[:, 0] - jnp.sum(jnp.where(inside, starts[None, :], 0), axis=1)
    token_target = jnp.sum(jnp.where(inside, my_targets[None, :], 0), axis=1)
    row_ids = jnp.arange(requests, dtype=jnp.int32)
    sending = my_targets[None, :] == row_ids[:, None]
    target_length = jnp.sum(jnp.where(sending, my_lengths[None, :], 0), axis=1)
    step = jnp.repeat(jnp.arange(steps, dtype=jnp.int32), requests)
    new_target = jnp.tile(row_ids, steps)
    new_position = jnp.tile(target_length, steps) + step
    spare = jnp.zeros((padded - tokens - requests * steps,), jnp.int32)
    position = jnp.concatenate([token_position, new_position, spare])
    target = jnp.concatenate([token_target, new_target, spare - 1])
    seen_from = jnp.concatenate([jnp.zeros_like(token_target), step, spare])
    query_info = jnp.stack([new_target, step], 1)
    return position, jnp.stack([target, seen_from], 0), query_info


def finish_kernel(heads, group, held_ref, back_ref, cos_ref, sin_ref, keys_ref, rows_ref, query_ref, out_ref):
    cosine, sine = cos_ref[...], sin_ref[...]
    allowed = (keys_ref[0:1, :] == rows_ref[:, 0:1]) & (keys_ref[1:2, :] <= rows_ref[:, 1:2])
    allowed = jnp.concatenate([allowed.astype(jnp.float32)] * group, 0) > 0.5
    queries = query_ref[...].astype(jnp.float32)
    count = queries.shape[0]
    width = heads * HD
    for h in range(heads):
        key_at, value_at = slice(h * HD, (h + 1) * HD), slice(width + h * HD, width + (h + 1) * HD)
        both = held_ref[:, key_at] + back_ref[:, key_at]
        first, second = both[:, :HALF], both[:, HALF:]
        keys = jnp.concatenate(
            [first * cosine - second * sine, second * cosine + first * sine], -1
        ).astype(jnp.bfloat16)
        values = held_ref[:, value_at] + back_ref[:, value_at]
        values = values.astype(jnp.bfloat16)
        at = h * group * HD
        query = jnp.concatenate(
            [queries[:, at + g * HD : at + (g + 1) * HD] for g in range(group)], 0
        ).astype(jnp.bfloat16)
        scores = lax.dot_general(
            query, keys, (((1,), (1,)), ((), ())), preferred_element_type=jnp.float32
        )
        scores = jnp.where(allowed, scores * (1.0 / math.sqrt(HD)), jnp.float32(-1e30))
        raised = jnp.exp(scores - jnp.max(scores, axis=-1, keepdims=True))
        total = jnp.sum(raised, axis=-1, keepdims=True)
        weights = (raised / total).astype(jnp.bfloat16)
        output = jnp.dot(weights, values, preferred_element_type=jnp.float32)
        for g in range(group):
            out_ref[:, at + g * HD : at + (g + 1) * HD] = output[
                g * count : (g + 1) * count
            ].astype(jnp.bfloat16)


def finish(projected, back, cosine, sine, key_info, query_info, queries):
    rows, width = projected.shape
    heads = width // (2 * HD)
    group = queries.shape[1] // (heads * HD)
    count = queries.shape[0]
    whole = pl.BlockSpec(memory_space=pltpu.VMEM)
    return pl.pallas_call(
        functools.partial(finish_kernel, heads, group),
        out_shape=jax.ShapeDtypeStruct(queries.shape, jnp.bfloat16),
        in_specs=[whole] * 7,
        out_specs=whole,
        compiler_params=pltpu.CompilerParams(vmem_limit_bytes=48 << 20),
        cost_estimate=pl.CostEstimate(
            flops=4 * heads * group * count * rows * HD,
            bytes_accessed=projected.size * 8 + 4 * queries.size,
            transcendentals=heads * group * count * rows,
        ),
        name="rotate_attend",
    )(projected, back, cosine, sine, key_info, query_info, queries)


def pick_kernel(side_ref, source_ref, out_ref):
    out_ref[...] = source_ref[...]


def pick_columns(source, side, half, first, end):
    blocks = source.shape[1] // (2 * half)
    rows = math.gcd(first, end) if first else end
    return pl.pallas_call(
        pick_kernel,
        out_shape=jax.ShapeDtypeStruct((end - first, blocks * half), source.dtype),
        grid_spec=pltpu.PrefetchScalarGridSpec(
            num_scalar_prefetch=1,
            grid=((end - first) // rows, blocks),
            in_specs=[
                pl.BlockSpec((rows, half), lambda i, j, s: (first // rows + i, 2 * j + s[0]))
            ],
            out_specs=pl.BlockSpec((rows, half), lambda i, j, s: (i, j)),
        ),
        compiler_params=pltpu.CompilerParams(vmem_limit_bytes=VMEM_BYTES),
        cost_estimate=pl.CostEstimate(
            flops=0, bytes_accessed=4 * (end - first) * blocks * half, transcendentals=0
        ),
        name="pick_columns",
    )(side.reshape(1), source)


def product_kernel(depths, layout, base, column, has_total, *refs):
    place_ref, refs = refs[0], refs[1:]
    hidden, refs = refs[: 2 * len(layout)], refs[2 * len(layout) :]
    flat = [depth for pieces in depths for depth in pieces]
    weights, refs = refs[: len(flat)], refs[len(flat) :]
    out_ref, held, piece, sems, piece_sems, total_sem = refs[-6:]
    shards, width = len(depths), out_ref.shape[1]
    half = held.shape[1] // shards
    blocks = hidden[0].shape[1] // half

    def window(ref):
        return ref if ref.shape[1] == width else ref.at[:, column : column + width]

    if has_total:
        total_copy = pltpu.make_async_copy(window(refs[0]), out_ref, total_sem)
        total_copy.start()
    tops = [sum(flat[:i]) for i in range(len(flat))]
    copies = [
        pltpu.make_async_copy(window(w), piece.at[top : top + depth, :], piece_sems.at[i])
        for i, (w, top, depth) in enumerate(zip(weights, tops, flat))
    ]
    done = 0
    for p in range(shards):
        for _ in depths[p]:
            copies[done].start()
            done += 1
        place = place_ref[base + p]
        for core in range(2):

            @pl.when(place // blocks == core)
            def _():
                columns = pl.ds(pl.multiple_of((place - core * blocks) * half, half), half)
                for part, (row, at, rows) in enumerate(layout):
                    pltpu.make_async_copy(
                        hidden[2 * part + core].at[row : row + rows, columns],
                        held.at[at : at + rows, p * half : (p + 1) * half],
                        sems.at[p, part],
                    ).start()

    total, waited = None, 0
    for begin in range(0, shards, MERGED):
        end = min(begin + MERGED, shards)
        for p in range(begin, end):
            for part, (_, at, rows) in enumerate(layout):
                target = held.at[at : at + rows, p * half : (p + 1) * half]
                pltpu.make_async_copy(target, target, sems.at[p, part]).wait()
            for _ in depths[p]:
                copies[waited].wait()
                waited += 1
        span = slice(begin * half, end * half)
        term = jnp.dot(held[:, span], piece[span, :], preferred_element_type=jnp.float32)
        total = term if total is None else total + term
    if has_total:
        total_copy.wait()
        total = out_ref[...] + total
    out_ref[...] = total


def products(total, hidden, weights, places, base, column, width):
    shards = len(weights)
    flat = [w for shard in weights for w in shard]
    depths = tuple(tuple(w.shape[0] for w in shard) for shard in weights)
    half = sum(depths[0])
    operands, layout, at = [places], [], 0
    for row, rows, pair in hidden:
        operands += pair
        layout.append((row, at, rows))
        at += rows
    operands += flat
    if total is not None:
        operands.append(total)
    return pl.pallas_call(
        functools.partial(
            product_kernel, depths, tuple(layout), base, column, total is not None
        ),
        out_shape=jax.ShapeDtypeStruct((at, width), jnp.float32),
        in_specs=[pl.BlockSpec(memory_space=pltpu.SMEM)]
        + [pl.BlockSpec(memory_space=pl.ANY)] * (len(operands) - 1),
        out_specs=pl.BlockSpec(memory_space=pltpu.VMEM),
        scratch_shapes=[
            pltpu.VMEM((at, shards * half), jnp.bfloat16),
            pltpu.VMEM((shards * half, width), jnp.bfloat16),
            pltpu.SemaphoreType.DMA((shards, len(hidden))),
            pltpu.SemaphoreType.DMA((len(flat),)),
            pltpu.SemaphoreType.DMA,
        ],
        compiler_params=pltpu.CompilerParams(vmem_limit_bytes=VMEM_BYTES),
        cost_estimate=pl.CostEstimate(
            flops=2 * at * half * width * shards,
            bytes_accessed=shards * 2 * half * (at + width) + 4 * at * width,
            transcendentals=0,
        ),
        name="products",
    )(*operands)


def ring_order(row_count):
    evens = list(range(0, row_count, 2))
    odds = list(range(1, row_count, 2))
    return evens + odds[::-1]


def fence(*values):
    return lax.optimization_barrier(values)


def body(passages, kv_weight, new_hidden, queries, lengths, destinations):
    tokens = passages.shape[0]
    requests, steps, half_model = new_hidden.shape
    row_count = lax.axis_size("rows")
    group_count = lax.axis_size("groups")
    row_index = lax.axis_index("rows")
    side = lax.axis_index("groups") % 2
    core = lax.axis_index("tensor")
    depth = kv_weight.shape[0]
    half = depth // 2
    local_heads = kv_weight.shape[2] // HD
    group = queries.shape[2] // kv_weight.shape[2]
    count = requests * steps
    new_padded = -(-count // 16) * 16
    half_rows = row_count // 2

    partners = [(g, g ^ 1) for g in range(group_count)]
    cores = [(0, 1), (1, 0)]
    order = ring_order(row_count)
    onward = [(order[i], order[(i + 1) % row_count]) for i in range(row_count)]
    back = [(b, a) for a, b in onward]
    place = {row: i for i, row in enumerate(order)}
    shard_order = [
        [order[(place[r] + d) % row_count] for r in range(row_count)]
        for k in range(half_rows + 1)
        for d in ([0] if k == 0 else [-k, k] if k < half_rows else [k])
    ]
    owners = lax.dynamic_index_in_dim(jnp.array(shard_order, jnp.int32), row_index, 1, keepdims=False)
    places = ((owners // half_rows) ^ core) * half_rows + owners % half_rows

    chunk = kv_weight.shape[2] // CHUNKS
    own = lax.dynamic_slice_in_dim(kv_weight, side * half, half, 0)
    own = own.reshape(half, 2, CHUNKS, chunk).swapaxes(1, 2).reshape(half, -1)
    width = 2 * chunk

    def step(pair):
        return lax.ppermute(pair[0], "rows", onward), lax.ppermute(pair[1], "rows", back)

    cuts = (0, 2 * tokens // 5, 4 * tokens // 5, tokens)
    sent = [pick_columns(passages, 1 - side, half, cuts[0], cuts[1])]
    own, sent[0], passages, new_hidden = fence(own, sent[0], passages, new_hidden)
    got = [lax.ppermute(sent[0], "groups", partners)]
    ring = [step((own, own))]
    sent += [pick_columns(passages, 1 - side, half, *cuts[i : i + 2]) for i in (1, 2)]
    kept = pick_columns(passages, side, half, 0, tokens)
    kept_other = lax.ppermute(kept, "tensor", cores)
    new_hidden, kept = fence(new_hidden, kept)
    moved = lax.all_to_all(new_hidden, "rows", split_axis=0, concat_axis=0, tiled=True)
    ring[0], got[0], moved, kept_other, sent, queries = fence(
        ring[0], got[0], moved, kept_other, sent, queries
    )

    got.append(lax.ppermute(sent[1], "groups", partners))
    ring.append(step(ring[-1]))
    new_rows = jnp.swapaxes(moved, 0, 1).reshape(count, half_model)
    new_rows = jnp.pad(new_rows, ((0, new_padded - count), (0, 0)))
    new_sent = pick_columns(new_rows, 1 - side, half, 0, new_padded)
    new_got = lax.ppermute(new_sent, "groups", partners)
    new_kept = pick_columns(new_rows, side, half, 0, new_padded)
    new_kept = jnp.concatenate([new_kept, new_got], 0)
    new_other = lax.ppermute(new_kept, "tensor", cores)
    got_other = [lax.ppermute(got[0], "tensor", cores)]
    moved = lax.all_to_all(queries, "rows", split_axis=0, concat_axis=0, tiled=True)
    ring[1], got[1], new_other, got_other, places, moved = fence(
        ring[1], got[1], new_other, got_other, places, moved
    )
    query_rows = jnp.swapaxes(moved, 0, 1).reshape(count, -1)

    def project(hidden, total, begin, end, column, width):
        weights = [(own,)] + [(w,) for pair in ring for w in pair]
        weights = weights[: row_count - 1] + [last[column // width] if last else ()]
        for at in range(begin, end, MOST_SHARDS):
            some = weights[at : min(at + MOST_SHARDS, end)]
            total = products(total, hidden, some, places, at, column, width)
        return total

    def homeward(total):
        return (total * RAISE).astype(jnp.float16)

    last = []
    own_hidden = [(0, tokens, (kept, kept_other)), (0, new_padded, (new_kept, new_other))]
    early = row_count - 3
    for k in range(2, half_rows - 1):
        if k > 2:
            ring[-1] = fence(*ring[-1])
        else:
            got.append(lax.ppermute(sent[2], "groups", partners))
            got_other.append(lax.ppermute(got[1], "tensor", cores))
        ring.append(step(ring[-1]))
    held = project(own_hidden, None, 0, early, 0, 2 * width)
    position, key_info, query_info = token_tables(
        lengths, destinations, row_index, tokens, requests, steps, tokens + new_padded
    )
    cosine, sine = angle_tables(position)

    def halved(c):
        columns = slice(c * width, (c + 1) * width)
        return ring[-1][0][: half // 2, columns], ring[-1][1][half // 2 :, columns]

    ends = [halved(0)]
    ring[-1], got[2], got_other, held, ends, places, cosine, sine = fence(
        ring[-1], got[2], got_other, held, ends, places, cosine, sine
    )

    last.append(step(ends[0]))
    got_other.append(lax.ppermute(got[2], "tensor", cores))
    away_hidden = [
        (0, piece.shape[0], (piece, other)) for piece, other in zip(got, got_other)
    ] + [(new_padded, new_padded, (new_kept, new_other))]
    away = [project(away_hidden, None, 0, row_count - 1, 0, width)]
    ends.append(halved(1))
    last[0], away, ends, places = fence(last[0], away, ends, places)

    last.append(step(ends[1]))
    away[0] = homeward(project(away_hidden, away[0], row_count - 1, row_count, 0, width))
    away[0], places = fence(away[0], places)
    homed = [lax.ppermute(away[0], "groups", partners)]
    away.append(project(away_hidden, None, 0, row_count - 1, width, width))
    away[1] = homeward(project(away_hidden, away[1], row_count - 1, row_count, width, width))
    homed[0], away[1], places = fence(homed[0], away[1], places)

    homed.append(lax.ppermute(away[1], "groups", partners))
    outs = []
    for c in range(CHUNKS):
        back_home = homed[c].astype(jnp.float32) * (1.0 / RAISE)
        mine = project(own_hidden, held, early, row_count, c * width, width)
        at = c * chunk * group
        query = query_rows[:, at : at + chunk * group]
        outs.append(finish(mine, back_home, cosine, sine, key_info, query_info, query))
    attended = jnp.concatenate(outs, 1)
    attended = jnp.swapaxes(attended.reshape(steps, requests, -1), 0, 1)
    return lax.all_to_all(attended, "rows", split_axis=0, concat_axis=0, tiled=True)


def solution(mesh):
    placed = (
        P(("groups", "rows"), "tensor"),
        P("rows", None, "tensor"),
        P(("groups", "rows"), None, "tensor"),
        P(("groups", "rows"), None, "tensor"),
        P("groups", None),
        P("groups", None),
    )
    return jax.shard_map(
        body,
        mesh=mesh,
        in_specs=placed,
        out_specs=P(("groups", "rows"), None, "tensor"),
        check_vma=False,
    )
```

```python
import functools
import math

import jax
import jax.numpy as jnp
from jax import lax
from jax.experimental import pallas as pl
from jax.experimental.pallas import tpu as pltpu
from jax.sharding import PartitionSpec as P

HD = 128
HALF = HD // 2
CHUNKS = 2
MOST_SHARDS = 8
VMEM_BYTES = 32 << 20
MERGED = 4
RAISE = 16.0


def angle_tables(positions):
    index_float = jnp.arange(HALF, dtype=jnp.float32)
    inverse = jnp.exp(index_float * (-2.0 * math.log(1000000.0) / HD))
    angles = positions.astype(jnp.float32)[:, None] * inverse
    return jnp.cos(angles), jnp.sin(angles)


def token_tables(lengths, destinations, row_index, tokens, requests, steps, padded):
    my_lengths = lax.dynamic_index_in_dim(lengths, row_index, 0, keepdims=False)
    my_targets = lax.dynamic_index_in_dim(destinations, row_index, 0, keepdims=False)
    ends = jnp.cumsum(my_lengths)
    starts = ends - my_lengths
    token = jnp.arange(tokens, dtype=jnp.int32)[:, None]
    inside = (starts[None, :] <= token) & (token < ends[None, :])
    token_position = token[:, 0] - jnp.sum(jnp.where(inside, starts[None, :], 0), axis=1)
    token_target = jnp.sum(jnp.where(inside, my_targets[None, :], 0), axis=1)
    received = jnp.sum(jnp.where(destinations == row_index, lengths, 0), axis=1)
    step = jnp.repeat(jnp.arange(steps, dtype=jnp.int32), requests)
    new_target = jnp.tile(jnp.arange(requests, dtype=jnp.int32), steps)
    new_position = jnp.tile(received, steps) + step
    spare = jnp.zeros((padded - requests * steps,), jnp.int32)
    target = jnp.concatenate([token_target, new_target, spare - 1])
    seen_from = jnp.concatenate([jnp.zeros_like(token_target), step, spare])
    query_info = jnp.stack([new_target, step], 1)
    return token_position, new_position, jnp.stack([target, seen_from], 0), query_info


def rotate(first, second, cosine, sine):
    return [first * cosine - second * sine, second * cosine + first * sine]


def finish_kernel(chunks, group, *refs):
    held, homed, refs = refs[:chunks], refs[chunks : 2 * chunks], refs[2 * chunks :]
    cos_ref, sin_ref, keys_ref, rows_ref, new_ref, query_ref, out_ref = refs
    cosine, sine = cos_ref[...], sin_ref[...]
    allowed = (keys_ref[0:1, :] == rows_ref[:, 0:1]) & (keys_ref[1:2, :] <= rows_ref[:, 1:2])
    allowed = jnp.concatenate([allowed.astype(jnp.float32)] * group, 0) > 0.5
    queries = query_ref[...].astype(jnp.float32)
    count = queries.shape[0]
    width = held[0].shape[1]
    heads = width // (2 * HD)
    for h in range(chunks * heads):
        c, local = h // heads, h % heads
        key_at = slice(local * HD, (local + 1) * HD)
        value_at = slice((heads + local) * HD, (heads + local + 1) * HD)
        new_at = c * width
        both = held[c][:, key_at] + homed[c][:, key_at]
        keys = jnp.concatenate(rotate(both[:, :HALF], both[:, HALF:], cosine, sine), -1)
        values = held[c][:, value_at] + homed[c][:, value_at]
        keys, values = (
            jnp.concatenate(
                [cached.astype(jnp.bfloat16), new_ref[:, new_at + at.start : new_at + at.stop]], 0
            )
            for cached, at in ((keys, key_at), (values, value_at))
        )
        at = h * group * HD
        query = jnp.concatenate(
            [queries[:, at + g * HD : at + (g + 1) * HD] for g in range(group)], 0
        ).astype(jnp.bfloat16)
        scores = lax.dot_general(
            query, keys, (((1,), (1,)), ((), ())), preferred_element_type=jnp.float32
        )
        scores = jnp.where(allowed, scores * (1.0 / math.sqrt(HD)), jnp.float32(-1e30))
        raised = jnp.exp(scores - jnp.max(scores, axis=-1, keepdims=True))
        total = jnp.sum(raised, axis=-1, keepdims=True)
        weights = (raised / total).astype(jnp.bfloat16)
        output = jnp.dot(weights, values, preferred_element_type=jnp.float32)
        for g in range(group):
            out_ref[:, at + g * HD : at + (g + 1) * HD] = output[
                g * count : (g + 1) * count
            ].astype(jnp.bfloat16)


def finish(held, homed, cosine, sine, key_info, query_info, new_pairs, queries):
    rows, width = held[0].shape
    heads = len(held) * width // (2 * HD)
    group = queries.shape[1] // (heads * HD)
    count = queries.shape[0]
    vmem = pl.BlockSpec(memory_space=pltpu.VMEM)
    operands = [*held, *homed, cosine, sine, key_info, query_info, new_pairs, queries]
    return pl.pallas_call(
        functools.partial(finish_kernel, len(held), group),
        out_shape=jax.ShapeDtypeStruct(queries.shape, jnp.bfloat16),
        in_specs=[vmem] * len(operands),
        out_specs=vmem,
        compiler_params=pltpu.CompilerParams(vmem_limit_bytes=VMEM_BYTES),
        cost_estimate=pl.CostEstimate(
            flops=4 * heads * group * count * rows * HD,
            bytes_accessed=8 * len(held) * rows * width + 4 * queries.size,
            transcendentals=heads * group * count * rows,
        ),
        name="rotate_attend",
    )(*operands)


def pick_kernel(side_ref, source_ref, out_ref):
    out_ref[...] = source_ref[...]


def pick_columns(source, side, half, first, end):
    blocks = source.shape[1] // (2 * half)
    rows = math.gcd(first, end) if first else end
    return pl.pallas_call(
        pick_kernel,
        out_shape=jax.ShapeDtypeStruct((end - first, blocks * half), source.dtype),
        grid_spec=pltpu.PrefetchScalarGridSpec(
            num_scalar_prefetch=1,
            grid=((end - first) // rows, blocks),
            in_specs=[
                pl.BlockSpec((rows, half), lambda i, j, s: (first // rows + i, 2 * j + s[0]))
            ],
            out_specs=pl.BlockSpec((rows, half), lambda i, j, s: (i, j)),
        ),
        compiler_params=pltpu.CompilerParams(vmem_limit_bytes=VMEM_BYTES),
        cost_estimate=pl.CostEstimate(
            flops=0, bytes_accessed=4 * (end - first) * blocks * half, transcendentals=0
        ),
        name="pick_columns",
    )(side.reshape(1), source)


def product_kernel(depths, parts, base, column, has_total, *refs):
    place_ref, refs = refs[0], refs[1:]
    hidden, refs = refs[: 2 * parts], refs[2 * parts :]
    weights, out_ref = refs[: sum(len(pieces) for pieces in depths)], refs[-1]
    width = out_ref.shape[1]
    half = sum(depths[0])
    blocks = hidden[0].shape[1] // half

    def window(ref):
        return ref[...] if ref.shape[1] == width else ref[:, column : column + width]

    total, used = window(refs[-2]) if has_total else None, 0
    for p, pieces in enumerate(depths):
        place = place_ref[base + p]
        here = place < blocks
        columns = pl.ds(pl.multiple_of(jnp.where(here, place, place - blocks) * half, half), half)
        rows = [
            jnp.where(here, hidden[2 * q][:, columns], hidden[2 * q + 1][:, columns])
            for q in range(parts)
        ]
        rows = rows[0] if parts == 1 else jnp.concatenate(rows, 0)
        piece = [window(w) for w in weights[used : used + len(pieces)]]
        piece = piece[0] if len(piece) == 1 else jnp.concatenate(piece, 0)
        used += len(pieces)
        term = jnp.dot(rows, piece, preferred_element_type=jnp.float32)
        total = term if total is None else total + term
    out_ref[...] = total


def products(total, hidden, weights, places, base, column, width):
    shards = len(weights)
    flat = [w for shard in weights for w in shard]
    depths = tuple(tuple(w.shape[0] for w in shard) for shard in weights)
    half = sum(depths[0])
    rows = sum(pair[0].shape[0] for pair in hidden)
    operands = [places] + [array for pair in hidden for array in pair] + flat
    if total is not None:
        operands.append(total)
    vmem = pl.BlockSpec(memory_space=pltpu.VMEM)
    return pl.pallas_call(
        functools.partial(
            product_kernel, depths, len(hidden), base, column, total is not None
        ),
        out_shape=jax.ShapeDtypeStruct((rows, width), jnp.float32),
        in_specs=[pl.BlockSpec(memory_space=pltpu.SMEM)] + [vmem] * (len(operands) - 1),
        out_specs=vmem,
        compiler_params=pltpu.CompilerParams(vmem_limit_bytes=VMEM_BYTES),
        cost_estimate=pl.CostEstimate(
            flops=2 * rows * half * width * shards,
            bytes_accessed=shards * 2 * half * (rows + width) + 4 * rows * width,
            transcendentals=0,
        ),
        name="products",
    )(*operands)


def ring_order(row_count):
    evens = list(range(0, row_count, 2))
    odds = list(range(1, row_count, 2))
    return evens + odds[::-1]


def fence(*values):
    return lax.optimization_barrier(values)


def body(passages, kv_weight, new_hidden, queries, lengths, destinations):
    tokens = passages.shape[0]
    requests, steps, half_model = new_hidden.shape
    row_count = lax.axis_size("rows")
    group_count = lax.axis_size("groups")
    row_index = lax.axis_index("rows")
    side = lax.axis_index("groups") % 2
    core = lax.axis_index("tensor")
    depth = kv_weight.shape[0]
    half = depth // 2
    local_heads = kv_weight.shape[2] // HD
    group = queries.shape[2] // kv_weight.shape[2]
    count = requests * steps
    new_padded = -(-count // 16) * 16
    half_rows = row_count // 2

    partners = [(g, g ^ 1) for g in range(group_count)]
    cores = [(0, 1), (1, 0)]
    order = ring_order(row_count)
    onward = [(order[i], order[(i + 1) % row_count]) for i in range(row_count)]
    back = [(b, a) for a, b in onward]
    place = {row: i for i, row in enumerate(order)}
    shard_order = [
        [order[(place[r] + d) % row_count] for r in range(row_count)]
        for k in range(half_rows + 1)
        for d in ([0] if k == 0 else [-k, k] if k < half_rows else [k])
    ]
    owners = lax.dynamic_index_in_dim(jnp.array(shard_order, jnp.int32), row_index, 1, keepdims=False)
    places = ((owners // half_rows) ^ core) * half_rows + owners % half_rows

    chunk = kv_weight.shape[2] // CHUNKS
    own = lax.dynamic_slice_in_dim(kv_weight, side * half, half, 0)
    own = own.reshape(half, 2, CHUNKS, chunk).swapaxes(1, 2).reshape(half, -1)
    width = 2 * chunk

    def step(pair):
        return lax.ppermute(pair[0], "rows", onward), lax.ppermute(pair[1], "rows", back)

    cuts = (0, 2 * tokens // 5, 4 * tokens // 5, tokens)
    sent = [pick_columns(passages, 1 - side, half, cuts[0], cuts[1])]
    own, sent[0], passages, new_hidden = fence(own, sent[0], passages, new_hidden)
    got = [lax.ppermute(sent[0], "groups", partners)]
    ring = [step((own, own))]
    sent += [pick_columns(passages, 1 - side, half, *cuts[i : i + 2]) for i in (1, 2)]
    kept = pick_columns(passages, side, half, 0, tokens)
    new_rows = jnp.swapaxes(new_hidden, 0, 1).reshape(count, half_model)
    new_rows = jnp.pad(new_rows, ((0, new_padded - count), (0, 0)))
    new_sent = pick_columns(new_rows, 1 - side, half, 0, new_padded)
    new_kept = pick_columns(new_rows, side, half, 0, new_padded)
    ring[0], got[0], sent, kept, new_sent, new_kept, lengths, destinations = fence(
        ring[0], got[0], sent, kept, new_sent, new_kept, lengths, destinations
    )

    got.append(lax.ppermute(sent[1], "groups", partners))
    ring.append(step(ring[-1]))
    kept_other = lax.ppermute(kept, "tensor", cores)
    new_got = lax.ppermute(new_sent, "groups", partners)
    position, new_position, key_info, query_info = token_tables(
        lengths, destinations, row_index, tokens, requests, steps, new_padded
    )
    cosine, sine = angle_tables(position)
    new_cosine, new_sine = angle_tables(new_position)
    tables = (cosine, sine, new_cosine, new_sine, key_info, query_info)
    ring[1], got[1], kept_other, new_got, tables, places = fence(
        ring[1], got[1], kept_other, new_got, tables, places
    )

    def project(hidden, total, begin, end, column, width):
        weights = [(own,)] + [(w,) for pair in ring for w in pair]
        weights = weights[: row_count - 1] + [last[column // width] if last else ()]
        for at in range(begin, end, MOST_SHARDS):
            some = weights[at : min(at + MOST_SHARDS, end)]
            total = products(total, hidden, some, places, at, column, width)
        return total

    def homeward(total):
        tokens_total = (total[:tokens] * RAISE).astype(jnp.float16)
        return tokens_total, total[tokens + new_padded :], total[tokens : tokens + count]

    last = []
    own_hidden = [(kept, kept_other)]
    early = row_count - 3
    got_other = []
    for k in range(2, half_rows - 1):
        if k > 2:
            ring[-1] = fence(*ring[-1])
        else:
            got.append(lax.ppermute(sent[2], "groups", partners))
            got_other += [lax.ppermute(piece, "tensor", cores) for piece in got[:2]]
        ring.append(step(ring[-1]))
    held = project(own_hidden, None, 0, early, 0, 2 * width)
    new_kept = jnp.concatenate([new_kept, new_got], 0)

    def halved(c):
        columns = slice(c * width, (c + 1) * width)
        return ring[-1][0][: half // 2, columns], ring[-1][1][half // 2 :, columns]

    ends = [halved(0)]
    ring[-1], got[2], got_other, new_kept, held, ends, places = fence(
        ring[-1], got[2], got_other, new_kept, held, ends, places
    )

    last.append(step(ends[0]))
    got_other.append(lax.ppermute(got[2], "tensor", cores))
    new_other = lax.ppermute(new_kept, "tensor", cores)
    away_hidden = list(zip(got, got_other)) + [(new_kept, new_other)]
    away = project(away_hidden, None, 0, row_count - 1, 0, width)
    ends.append(halved(1))
    last[0], away, ends, places = fence(last[0], away, ends, places)

    last.append(step(ends[1]))
    away = project(away_hidden, away, row_count - 1, row_count, 0, width)
    away, places = fence(homeward(away), places)
    homed = [lax.ppermute(away[0], "groups", partners)]
    new_totals = [away[2] + lax.ppermute(away[1], "groups", partners)[:count]]
    away = project(away_hidden, None, 0, row_count - 1, width, width)
    away = homeward(project(away_hidden, away, row_count - 1, row_count, width, width))
    new_totals.append(away[2] + lax.ppermute(away[1], "groups", partners)[:count])
    mine = [project(own_hidden, held, early, row_count, 0, width)]
    homed[0], away, mine, new_totals, held, queries, places = fence(
        homed[0], away, mine, new_totals, held, queries, places
    )

    homed.append(lax.ppermute(away[0], "groups", partners))
    cosine, sine, new_cosine, new_sine, key_info, query_info = tables
    moved = [jnp.swapaxes(queries, 0, 1).reshape(count, -1)]
    for total in new_totals:
        pairs = total.reshape(count, 2, -1, 2, HALF)
        keys = rotate(
            pairs[:, 0, :, 0], pairs[:, 0, :, 1], new_cosine[:, None, :], new_sine[:, None, :]
        )
        keys = jnp.stack(keys, 2).reshape(count, chunk)
        moved += [keys.astype(jnp.bfloat16), total[:, chunk:].astype(jnp.bfloat16)]
    moved = jnp.concatenate(moved, 1).reshape(steps, requests, -1)
    moved = jnp.swapaxes(moved, 0, 1)
    moved = lax.all_to_all(moved, "rows", split_axis=0, concat_axis=0, tiled=True)
    moved = jnp.swapaxes(moved, 0, 1).reshape(count, -1)
    heads_width = queries.shape[2]
    query_rows, new_pairs = moved[:, :heads_width], moved[:, heads_width:]
    new_pairs = jnp.pad(new_pairs, ((0, new_padded - count), (0, 0)))
    mine.append(project(own_hidden, held, early, row_count, width, width))
    homed = [total.astype(jnp.float32) * (1.0 / RAISE) for total in homed]
    attended = finish(mine, homed, cosine, sine, key_info, query_info, new_pairs, query_rows)
    attended = jnp.swapaxes(attended.reshape(steps, requests, -1), 0, 1)
    return lax.all_to_all(attended, "rows", split_axis=0, concat_axis=0, tiled=True)


def solution(mesh):
    placed = (
        P(("groups", "rows"), "tensor"),
        P("rows", None, "tensor"),
        P(("groups", "rows"), None, "tensor"),
        P(("groups", "rows"), None, "tensor"),
        P("groups", None),
        P("groups", None),
    )
    return jax.shard_map(
        body,
        mesh=mesh,
        in_specs=placed,
        out_specs=P(("groups", "rows"), None, "tensor"),
        check_vma=False,
    )
```

```python
import functools
import math

import jax
import jax.numpy as jnp
from jax import lax
from jax.experimental import pallas as pl
from jax.experimental.pallas import tpu as pltpu
from jax.sharding import PartitionSpec as P

HD = 128
HALF = HD // 2
CHUNKS = 2
MOST_SHARDS = 8
VMEM_BYTES = 32 << 20
MERGED = 4
RAISE = 16.0


def angle_tables(positions):
    index_float = jnp.arange(HALF, dtype=jnp.float32)
    inverse = jnp.exp(index_float * (-2.0 * math.log(1000000.0) / HD))
    angles = positions.astype(jnp.float32)[:, None] * inverse
    return jnp.cos(angles), jnp.sin(angles)


def token_tables(lengths, destinations, row_index, tokens, requests, steps, padded):
    my_lengths = lax.dynamic_index_in_dim(lengths, row_index, 0, keepdims=False)
    my_targets = lax.dynamic_index_in_dim(destinations, row_index, 0, keepdims=False)
    ends = jnp.cumsum(my_lengths)
    starts = ends - my_lengths
    token = jnp.arange(tokens, dtype=jnp.int32)[:, None]
    inside = (starts[None, :] <= token) & (token < ends[None, :])
    token_position = token[:, 0] - jnp.sum(jnp.where(inside, starts[None, :], 0), axis=1)
    token_target = jnp.sum(jnp.where(inside, my_targets[None, :], 0), axis=1)
    received = jnp.sum(jnp.where(destinations == row_index, lengths, 0), axis=1)
    step = jnp.repeat(jnp.arange(steps, dtype=jnp.int32), requests)
    new_target = jnp.tile(jnp.arange(requests, dtype=jnp.int32), steps)
    new_position = jnp.tile(received, steps) + step
    spare = jnp.zeros((padded - requests * steps,), jnp.int32)
    target = jnp.concatenate([token_target, new_target, spare - 1])
    seen_from = jnp.concatenate([jnp.zeros_like(token_target), step, spare])
    query_info = jnp.stack([new_target, step], 1)
    return token_position, new_position, jnp.stack([target, seen_from], 0), query_info


def rotate(first, second, cosine, sine):
    return [first * cosine - second * sine, second * cosine + first * sine]


def finish_kernel(chunks, group, *refs):
    held, homed, refs = refs[:chunks], refs[chunks : 2 * chunks], refs[2 * chunks :]
    cos_ref, sin_ref, keys_ref, rows_ref, new_ref, query_ref, out_ref = refs
    cosine, sine = cos_ref[...], sin_ref[...]
    allowed = (keys_ref[0:1, :] == rows_ref[:, 0:1]) & (keys_ref[1:2, :] <= rows_ref[:, 1:2])
    allowed = jnp.concatenate([allowed.astype(jnp.float32)] * group, 0) > 0.5
    queries = query_ref[...].astype(jnp.float32)
    count = queries.shape[0]
    width = held[0].shape[1]
    heads = width // (2 * HD)
    for h in range(chunks * heads):
        c, local = h // heads, h % heads
        key_at = slice(local * HD, (local + 1) * HD)
        value_at = slice((heads + local) * HD, (heads + local + 1) * HD)
        new_at = c * width
        both = held[c][:, key_at] + homed[c][:, key_at]
        keys = jnp.concatenate(rotate(both[:, :HALF], both[:, HALF:], cosine, sine), -1)
        values = held[c][:, value_at] + homed[c][:, value_at]
        keys, values = (
            jnp.concatenate(
                [cached.astype(jnp.bfloat16), new_ref[:, new_at + at.start : new_at + at.stop]], 0
            )
            for cached, at in ((keys, key_at), (values, value_at))
        )
        at = h * group * HD
        query = jnp.concatenate(
            [queries[:, at + g * HD : at + (g + 1) * HD] for g in range(group)], 0
        ).astype(jnp.bfloat16)
        scores = lax.dot_general(
            query, keys, (((1,), (1,)), ((), ())), preferred_element_type=jnp.float32
        )
        scores = jnp.where(allowed, scores * (1.0 / math.sqrt(HD)), jnp.float32(-1e30))
        raised = jnp.exp(scores - jnp.max(scores, axis=-1, keepdims=True))
        total = jnp.sum(raised, axis=-1, keepdims=True)
        weights = (raised / total).astype(jnp.bfloat16)
        output = jnp.dot(weights, values, preferred_element_type=jnp.float32)
        for g in range(group):
            out_ref[:, at + g * HD : at + (g + 1) * HD] = output[
                g * count : (g + 1) * count
            ].astype(jnp.bfloat16)


def finish(held, homed, cosine, sine, key_info, query_info, new_pairs, queries):
    rows, width = held[0].shape
    heads = len(held) * width // (2 * HD)
    group = queries.shape[1] // (heads * HD)
    count = queries.shape[0]
    vmem = pl.BlockSpec(memory_space=pltpu.VMEM)
    operands = [*held, *homed, cosine, sine, key_info, query_info, new_pairs, queries]
    return pl.pallas_call(
        functools.partial(finish_kernel, len(held), group),
        out_shape=jax.ShapeDtypeStruct(queries.shape, jnp.bfloat16),
        in_specs=[vmem] * len(operands),
        out_specs=vmem,
        compiler_params=pltpu.CompilerParams(vmem_limit_bytes=VMEM_BYTES),
        cost_estimate=pl.CostEstimate(
            flops=4 * heads * group * count * rows * HD,
            bytes_accessed=8 * len(held) * rows * width + 4 * queries.size,
            transcendentals=heads * group * count * rows,
        ),
        name="rotate_attend",
    )(*operands)


def own_kernel(side_ref, weight_ref, out_ref):
    chunk = out_ref.shape[1] // (2 * CHUNKS)
    for kind in range(2):
        columns = weight_ref[:, kind, :]
        for c in range(CHUNKS):
            at = (2 * c + kind) * chunk
            out_ref[:, at : at + chunk] = columns[:, c * chunk : (c + 1) * chunk]


def own_half(weight, side):
    depth, kinds, width = weight.shape
    half = depth // 2
    return pl.pallas_call(
        own_kernel,
        out_shape=jax.ShapeDtypeStruct((half, kinds * width), weight.dtype),
        grid_spec=pltpu.PrefetchScalarGridSpec(
            num_scalar_prefetch=1,
            grid=(2,),
            in_specs=[
                pl.BlockSpec((half // 2, kinds, width), lambda i, s: (2 * s[0] + i, 0, 0))
            ],
            out_specs=pl.BlockSpec((half // 2, kinds * width), lambda i, s: (i, 0)),
        ),
        compiler_params=pltpu.CompilerParams(vmem_limit_bytes=VMEM_BYTES),
        cost_estimate=pl.CostEstimate(
            flops=0, bytes_accessed=8 * half * width * kinds, transcendentals=0
        ),
        name="own_half",
    )(side.reshape(1), weight)


def pack_kernel(chunks, own_ref, *refs):
    owns, (got_ref, cos_ref, sin_ref, query_ref, out_ref) = (own_ref, *refs[: chunks - 1]), refs[chunks - 1 :]
    cosine, sine = cos_ref[...], sin_ref[...]
    count, base = query_ref.shape
    width = owns[0].shape[1]
    half = width // 2
    out_ref[:, :base] = query_ref[...]
    for c in range(chunks):
        for h in range(half // HD):
            at = h * HD
            both = owns[c][:, at : at + HD] + got_ref[:count, c * width + at : c * width + at + HD]
            both = jnp.concatenate(rotate(both[:, :HALF], both[:, HALF:], cosine, sine), -1)
            at += base + c * width
            out_ref[:, at : at + HD] = both.astype(jnp.bfloat16)
        values = owns[c][:, half:] + got_ref[:count, c * width + half : (c + 1) * width]
        at = base + c * width + half
        out_ref[:, at : at + half] = values.astype(jnp.bfloat16)


def pack(owns, got, cosine, sine, queries):
    vmem = pl.BlockSpec(memory_space=pltpu.VMEM)
    width = queries.shape[1] + got.shape[1]
    return pl.pallas_call(
        functools.partial(pack_kernel, len(owns)),
        out_shape=jax.ShapeDtypeStruct((queries.shape[0], width), jnp.bfloat16),
        in_specs=[vmem] * (len(owns) + 4),
        out_specs=vmem,
        compiler_params=pltpu.CompilerParams(vmem_limit_bytes=VMEM_BYTES),
        cost_estimate=pl.CostEstimate(
            flops=0, bytes_accessed=4 * queries.size + 10 * got.size, transcendentals=0
        ),
        name="pack_new",
    )(*owns, got, cosine, sine, queries)


def pick_kernel(side_ref, source_ref, out_ref):
    out_ref[...] = source_ref[...]


def pick_columns(source, side, half, first, end):
    blocks = source.shape[1] // (2 * half)
    rows = math.gcd(first, end) if first else end
    return pl.pallas_call(
        pick_kernel,
        out_shape=jax.ShapeDtypeStruct((end - first, blocks * half), source.dtype),
        grid_spec=pltpu.PrefetchScalarGridSpec(
            num_scalar_prefetch=1,
            grid=((end - first) // rows, blocks),
            in_specs=[
                pl.BlockSpec((rows, half), lambda i, j, s: (first // rows + i, 2 * j + s[0]))
            ],
            out_specs=pl.BlockSpec((rows, half), lambda i, j, s: (i, j)),
        ),
        compiler_params=pltpu.CompilerParams(vmem_limit_bytes=VMEM_BYTES),
        cost_estimate=pl.CostEstimate(
            flops=0, bytes_accessed=4 * (end - first) * blocks * half, transcendentals=0
        ),
        name="pick_columns",
    )(side.reshape(1), source)


def product_kernel(depths, parts, base, column, has_total, *refs):
    place_ref, refs = refs[0], refs[1:]
    hidden, refs = refs[: 2 * parts], refs[2 * parts :]
    weights, out_ref = refs[: sum(len(pieces) for pieces in depths)], refs[-1]
    width = out_ref.shape[1]
    half = sum(depths[0])
    blocks = hidden[0].shape[1] // half

    def window(ref):
        return ref[...] if ref.shape[1] == width else ref[:, column : column + width]

    total, used = window(refs[-2]) if has_total else None, 0
    for p, pieces in enumerate(depths):
        place = place_ref[base + p]
        here = place < blocks
        columns = pl.ds(pl.multiple_of(jnp.where(here, place, place - blocks) * half, half), half)
        rows = [
            jnp.where(here, hidden[2 * q][:, columns], hidden[2 * q + 1][:, columns])
            for q in range(parts)
        ]
        rows = rows[0] if parts == 1 else jnp.concatenate(rows, 0)
        piece = [window(w) for w in weights[used : used + len(pieces)]]
        piece = piece[0] if len(piece) == 1 else jnp.concatenate(piece, 0)
        used += len(pieces)
        term = jnp.dot(rows, piece, preferred_element_type=jnp.float32)
        total = term if total is None else total + term
    out_ref[...] = total


def products(total, hidden, weights, places, base, column, width):
    shards = len(weights)
    flat = [w for shard in weights for w in shard]
    depths = tuple(tuple(w.shape[0] for w in shard) for shard in weights)
    half = sum(depths[0])
    rows = sum(pair[0].shape[0] for pair in hidden)
    operands = [places] + [array for pair in hidden for array in pair] + flat
    if total is not None:
        operands.append(total)
    vmem = pl.BlockSpec(memory_space=pltpu.VMEM)
    return pl.pallas_call(
        functools.partial(
            product_kernel, depths, len(hidden), base, column, total is not None
        ),
        out_shape=jax.ShapeDtypeStruct((rows, width), jnp.float32),
        in_specs=[pl.BlockSpec(memory_space=pltpu.SMEM)] + [vmem] * (len(operands) - 1),
        out_specs=vmem,
        compiler_params=pltpu.CompilerParams(vmem_limit_bytes=VMEM_BYTES),
        cost_estimate=pl.CostEstimate(
            flops=2 * rows * half * width * shards,
            bytes_accessed=shards * 2 * half * (rows + width) + 4 * rows * width,
            transcendentals=0,
        ),
        name="products",
    )(*operands)


def ring_order(row_count):
    evens = list(range(0, row_count, 2))
    odds = list(range(1, row_count, 2))
    return evens + odds[::-1]


def fence(*values):
    return lax.optimization_barrier(values)


def body(passages, kv_weight, new_hidden, queries, lengths, destinations):
    tokens = passages.shape[0]
    requests, steps, half_model = new_hidden.shape
    row_count = lax.axis_size("rows")
    group_count = lax.axis_size("groups")
    row_index = lax.axis_index("rows")
    side = lax.axis_index("groups") % 2
    core = lax.axis_index("tensor")
    depth = kv_weight.shape[0]
    half = depth // 2
    local_heads = kv_weight.shape[2] // HD
    group = queries.shape[2] // kv_weight.shape[2]
    count = requests * steps
    new_padded = -(-count // 16) * 16
    half_rows = row_count // 2

    partners = [(g, g ^ 1) for g in range(group_count)]
    cores = [(0, 1), (1, 0)]
    order = ring_order(row_count)
    onward = [(order[i], order[(i + 1) % row_count]) for i in range(row_count)]
    back = [(b, a) for a, b in onward]
    place = {row: i for i, row in enumerate(order)}
    shard_order = [
        [order[(place[r] + d) % row_count] for r in range(row_count)]
        for k in range(half_rows + 1)
        for d in ([0] if k == 0 else [-k, k] if k < half_rows else [k])
    ]
    owners = lax.dynamic_index_in_dim(jnp.array(shard_order, jnp.int32), row_index, 1, keepdims=False)
    places = ((owners // half_rows) ^ core) * half_rows + owners % half_rows

    chunk = kv_weight.shape[2] // CHUNKS
    width = 2 * chunk
    own = own_half(kv_weight, side)

    def step(pair):
        return lax.ppermute(pair[0], "rows", onward), lax.ppermute(pair[1], "rows", back)

    cuts = (0, 2 * tokens // 5, 4 * tokens // 5, tokens)
    sent = [pick_columns(passages, 1 - side, half, cuts[0], cuts[1])]
    own, passages_later, new_hidden = fence(own, passages, new_hidden)
    got = [lax.ppermute(sent[0], "groups", partners)]
    ring = [step((own, own))]
    passages = passages_later
    sent += [pick_columns(passages, 1 - side, half, *cuts[i : i + 2]) for i in (1, 2)]
    kept = pick_columns(passages, side, half, 0, tokens)
    new_rows = jnp.swapaxes(new_hidden, 0, 1).reshape(count, half_model)
    new_rows = jnp.pad(new_rows, ((0, new_padded - count), (0, 0)))
    new_sent = pick_columns(new_rows, 1 - side, half, 0, new_padded)
    new_kept = pick_columns(new_rows, side, half, 0, new_padded)
    ring[0], got[0], sent, kept, new_sent, new_kept, lengths, destinations = fence(
        ring[0], got[0], sent, kept, new_sent, new_kept, lengths, destinations
    )

    got.append(lax.ppermute(sent[1], "groups", partners))
    ring.append(step(ring[-1]))
    kept_other = lax.ppermute(kept, "tensor", cores)
    got_other = [lax.ppermute(got[0], "tensor", cores)]
    position, new_position, key_info, query_info = token_tables(
        lengths, destinations, row_index, tokens, requests, steps, new_padded
    )
    cosine, sine = angle_tables(position)
    new_cosine, new_sine = angle_tables(new_position)
    tables = (cosine, sine, new_cosine, new_sine, key_info, query_info)
    ring[1], got[1], kept_other, got_other, tables, places = fence(
        ring[1], got[1], kept_other, got_other, tables, places
    )

    def project(hidden, total, begin, end, column, width):
        weights = [(own,)] + [(w,) for pair in ring for w in pair]
        weights = weights[: row_count - 1] + [last[column // width] if last else ()]
        for at in range(begin, end, MOST_SHARDS):
            some = weights[at : min(at + MOST_SHARDS, end)]
            total = products(total, hidden, some, places, at, column, width)
        return total

    def homeward(total):
        tokens_total = (total[:tokens] * RAISE).astype(jnp.float16)
        return tokens_total, total[tokens + new_padded :], total[tokens : tokens + count]

    last = []
    own_hidden = [(kept, kept_other)]
    early = row_count - 3
    for k in range(2, half_rows - 1):
        if k > 2:
            ring[-1] = fence(*ring[-1])
        else:
            got.append(lax.ppermute(sent[2], "groups", partners))
            got_other.append(lax.ppermute(got[1], "tensor", cores))
            new_got = lax.ppermute(new_sent, "groups", partners)
        ring.append(step(ring[-1]))
    held = project(own_hidden, None, 0, early, 0, 2 * width)
    new_kept = jnp.concatenate([new_kept, new_got], 0)

    def halved(c):
        columns = slice(c * width, (c + 1) * width)
        return ring[-1][0][: half // 2, columns], ring[-1][1][half // 2 :, columns]

    ends = [halved(0)]
    ring[-1], got[2], got_other, new_kept, held, ends, places = fence(
        ring[-1], got[2], got_other, new_kept, held, ends, places
    )

    last.append(step(ends[0]))
    got_other.append(lax.ppermute(got[2], "tensor", cores))
    new_other = lax.ppermute(new_kept, "tensor", cores)
    away_hidden = list(zip(got, got_other)) + [(new_kept, new_other)]
    away = project(away_hidden, None, 0, row_count - 1, 0, width)
    ends.append(halved(1))
    last[0], away, ends, places = fence(last[0], away, ends, places)

    last.append(step(ends[1]))
    away = project(away_hidden, away, row_count - 1, row_count, 0, width)
    away, places = fence(homeward(away), places)
    homed = [lax.ppermute(away[0], "groups", partners)]
    new_own, new_away = [away[2]], [away[1]]
    away = project(away_hidden, None, 0, row_count - 1, width, width)
    away = homeward(project(away_hidden, away, row_count - 1, row_count, width, width))
    new_own.append(away[2])
    new_away.append(away[1])
    new_back = lax.ppermute(jnp.concatenate(new_away, 1), "groups", partners)
    mine = [project(own_hidden, held, early, row_count, c * width, width) for c in range(CHUNKS)]
    queries = jnp.swapaxes(queries, 0, 1).reshape(count, -1)
    homed[0], away, mine, new_own, new_back, queries = fence(
        homed[0], away, mine, new_own, new_back, queries
    )

    homed.append(lax.ppermute(away[0], "groups", partners))
    cosine, sine, new_cosine, new_sine, key_info, query_info = tables
    moved = pack(new_own, new_back, new_cosine, new_sine, queries)
    moved = moved.reshape(steps, requests, -1)
    moved = jnp.swapaxes(moved, 0, 1)
    moved = lax.all_to_all(moved, "rows", split_axis=0, concat_axis=0, tiled=True)
    moved = jnp.swapaxes(moved, 0, 1).reshape(count, -1)
    heads_width = queries.shape[1]
    query_rows, new_pairs = moved[:, :heads_width], moved[:, heads_width:]
    new_pairs = jnp.pad(new_pairs, ((0, new_padded - count), (0, 0)))
    homed = [total.astype(jnp.float32) * (1.0 / RAISE) for total in homed]
    attended = finish(mine, homed, cosine, sine, key_info, query_info, new_pairs, query_rows)
    attended = jnp.swapaxes(attended.reshape(steps, requests, -1), 0, 1)
    return lax.all_to_all(attended, "rows", split_axis=0, concat_axis=0, tiled=True)


def solution(mesh):
    placed = (
        P(("groups", "rows"), "tensor"),
        P("rows", None, "tensor"),
        P(("groups", "rows"), None, "tensor"),
        P(("groups", "rows"), None, "tensor"),
        P("groups", None),
        P("groups", None),
    )
    return jax.shard_map(
        body,
        mesh=mesh,
        in_specs=placed,
        out_specs=P(("groups", "rows"), None, "tensor"),
        check_vma=False,
    )
```

```python
import functools
import math

import jax
import jax.numpy as jnp
from jax import lax
from jax.experimental import pallas as pl
from jax.experimental.pallas import tpu as pltpu
from jax.sharding import PartitionSpec as P

HD = 128
HALF = HD // 2
CHUNKS = 2
MOST_SHARDS = 8
VMEM_BYTES = 32 << 20
MERGED = 4
RAISE = 16.0


def angle_tables(positions):
    index_float = jnp.arange(HALF, dtype=jnp.float32)
    inverse = jnp.exp(index_float * (-2.0 * math.log(1000000.0) / HD))
    angles = positions.astype(jnp.float32)[:, None] * inverse
    return jnp.cos(angles), jnp.sin(angles)


def token_tables(lengths, destinations, row_index, tokens, requests, steps, padded):
    my_lengths = lax.dynamic_index_in_dim(lengths, row_index, 0, keepdims=False)
    my_targets = lax.dynamic_index_in_dim(destinations, row_index, 0, keepdims=False)
    ends = jnp.cumsum(my_lengths)
    starts = ends - my_lengths
    token = jnp.arange(tokens, dtype=jnp.int32)[:, None]
    inside = (starts[None, :] <= token) & (token < ends[None, :])
    token_position = token[:, 0] - jnp.sum(jnp.where(inside, starts[None, :], 0), axis=1)
    token_target = jnp.sum(jnp.where(inside, my_targets[None, :], 0), axis=1)
    received = jnp.sum(jnp.where(destinations == row_index, lengths, 0), axis=1)
    step = jnp.repeat(jnp.arange(steps, dtype=jnp.int32), requests)
    new_target = jnp.tile(jnp.arange(requests, dtype=jnp.int32), steps)
    new_position = jnp.tile(received, steps) + step
    spare = jnp.zeros((padded - requests * steps,), jnp.int32)
    target = jnp.concatenate([token_target, new_target, spare - 1])
    seen_from = jnp.concatenate([jnp.zeros_like(token_target), step, spare])
    query_info = jnp.stack([new_target, step], 1)
    return token_position, new_position, jnp.stack([target, seen_from], 0), query_info


def rotate(first, second, cosine, sine):
    return [first * cosine - second * sine, second * cosine + first * sine]


def finish_kernel(chunks, group, *refs):
    held, homed, refs = refs[:chunks], refs[chunks : 2 * chunks], refs[2 * chunks :]
    cos_ref, sin_ref, keys_ref, rows_ref, new_ref, query_ref, out_ref = refs
    cosine, sine = cos_ref[...], sin_ref[...]
    allowed = (keys_ref[0:1, :] == rows_ref[:, 0:1]) & (keys_ref[1:2, :] <= rows_ref[:, 1:2])
    allowed = jnp.concatenate([allowed.astype(jnp.float32)] * group, 0) > 0.5
    queries = query_ref[...].astype(jnp.float32)
    count = queries.shape[0]
    width = held[0].shape[1]
    heads = width // (2 * HD)
    for h in range(chunks * heads):
        c, local = h // heads, h % heads
        key_at = slice(local * HD, (local + 1) * HD)
        value_at = slice((heads + local) * HD, (heads + local + 1) * HD)
        new_at = c * width
        both = held[c][:, key_at] + homed[c][:, key_at]
        keys = jnp.concatenate(rotate(both[:, :HALF], both[:, HALF:], cosine, sine), -1)
        values = held[c][:, value_at] + homed[c][:, value_at]
        keys, values = (
            jnp.concatenate(
                [cached.astype(jnp.bfloat16), new_ref[:, new_at + at.start : new_at + at.stop]], 0
            )
            for cached, at in ((keys, key_at), (values, value_at))
        )
        at = h * group * HD
        query = jnp.concatenate(
            [queries[:, at + g * HD : at + (g + 1) * HD] for g in range(group)], 0
        ).astype(jnp.bfloat16)
        scores = lax.dot_general(
            query, keys, (((1,), (1,)), ((), ())), preferred_element_type=jnp.float32
        )
        scores = jnp.where(allowed, scores * (1.0 / math.sqrt(HD)), jnp.float32(-1e30))
        raised = jnp.exp(scores - jnp.max(scores, axis=-1, keepdims=True))
        total = jnp.sum(raised, axis=-1, keepdims=True)
        weights = (raised / total).astype(jnp.bfloat16)
        output = jnp.dot(weights, values, preferred_element_type=jnp.float32)
        for g in range(group):
            out_ref[:, at + g * HD : at + (g + 1) * HD] = output[
                g * count : (g + 1) * count
            ].astype(jnp.bfloat16)


def finish(held, homed, cosine, sine, key_info, query_info, new_pairs, queries):
    rows, width = held[0].shape
    heads = len(held) * width // (2 * HD)
    group = queries.shape[1] // (heads * HD)
    count = queries.shape[0]
    vmem = pl.BlockSpec(memory_space=pltpu.VMEM)
    operands = [*held, *homed, cosine, sine, key_info, query_info, new_pairs, queries]
    return pl.pallas_call(
        functools.partial(finish_kernel, len(held), group),
        out_shape=jax.ShapeDtypeStruct(queries.shape, jnp.bfloat16),
        in_specs=[vmem] * len(operands),
        out_specs=vmem,
        compiler_params=pltpu.CompilerParams(vmem_limit_bytes=VMEM_BYTES),
        cost_estimate=pl.CostEstimate(
            flops=4 * heads * group * count * rows * HD,
            bytes_accessed=8 * len(held) * rows * width + 4 * queries.size,
            transcendentals=heads * group * count * rows,
        ),
        name="rotate_attend",
    )(*operands)


def own_kernel(side_ref, weight_ref, *out_refs):
    chunk = out_refs[0].shape[1] // 2
    for kind in range(2):
        columns = weight_ref[:, kind, :]
        for c, out_ref in enumerate(out_refs):
            out_ref[:, kind * chunk : (kind + 1) * chunk] = columns[:, c * chunk : (c + 1) * chunk]


def own_half(weight, side):
    depth, kinds, width = weight.shape
    half = depth // 2
    chunk = kinds * width // CHUNKS
    return pl.pallas_call(
        own_kernel,
        out_shape=[jax.ShapeDtypeStruct((half, chunk), weight.dtype)] * CHUNKS,
        grid_spec=pltpu.PrefetchScalarGridSpec(
            num_scalar_prefetch=1,
            grid=(2,),
            in_specs=[
                pl.BlockSpec((half // 2, kinds, width), lambda i, s: (2 * s[0] + i, 0, 0))
            ],
            out_specs=[pl.BlockSpec((half // 2, chunk), lambda i, s: (i, 0))] * CHUNKS,
        ),
        compiler_params=pltpu.CompilerParams(vmem_limit_bytes=VMEM_BYTES),
        cost_estimate=pl.CostEstimate(
            flops=0, bytes_accessed=8 * half * width * kinds, transcendentals=0
        ),
        name="own_half",
    )(side.reshape(1), weight)


def pack_kernel(chunks, own_ref, *refs):
    owns, (got_ref, cos_ref, sin_ref, query_ref, out_ref) = (own_ref, *refs[: chunks - 1]), refs[chunks - 1 :]
    cosine, sine = cos_ref[...], sin_ref[...]
    count, base = query_ref.shape
    width = owns[0].shape[1]
    half = width // 2
    out_ref[:, :base] = query_ref[...]
    for c in range(chunks):
        for h in range(half // HD):
            at = h * HD
            both = owns[c][:, at : at + HD] + got_ref[:count, c * width + at : c * width + at + HD]
            both = jnp.concatenate(rotate(both[:, :HALF], both[:, HALF:], cosine, sine), -1)
            at += base + c * width
            out_ref[:, at : at + HD] = both.astype(jnp.bfloat16)
        values = owns[c][:, half:] + got_ref[:count, c * width + half : (c + 1) * width]
        at = base + c * width + half
        out_ref[:, at : at + half] = values.astype(jnp.bfloat16)


def pack(owns, got, cosine, sine, queries):
    vmem = pl.BlockSpec(memory_space=pltpu.VMEM)
    width = queries.shape[1] + got.shape[1]
    return pl.pallas_call(
        functools.partial(pack_kernel, len(owns)),
        out_shape=jax.ShapeDtypeStruct((queries.shape[0], width), jnp.bfloat16),
        in_specs=[vmem] * (len(owns) + 4),
        out_specs=vmem,
        compiler_params=pltpu.CompilerParams(vmem_limit_bytes=VMEM_BYTES),
        cost_estimate=pl.CostEstimate(
            flops=0, bytes_accessed=4 * queries.size + 10 * got.size, transcendentals=0
        ),
        name="pack_new",
    )(*owns, got, cosine, sine, queries)


def pick_kernel(first, side_ref, source_ref, out_ref):
    out_ref[...] = source_ref[first : first + out_ref.shape[0], :]


def pick_columns(source, side, half, first, end):
    rows, blocks = source.shape[0], source.shape[1] // (2 * half)
    return pl.pallas_call(
        functools.partial(pick_kernel, first),
        out_shape=jax.ShapeDtypeStruct((end - first, blocks * half), source.dtype),
        grid_spec=pltpu.PrefetchScalarGridSpec(
            num_scalar_prefetch=1,
            grid=(blocks,),
            in_specs=[pl.BlockSpec((rows, half), lambda j, s: (0, 2 * j + s[0]))],
            out_specs=pl.BlockSpec((end - first, half), lambda j, s: (0, j)),
        ),
        compiler_params=pltpu.CompilerParams(vmem_limit_bytes=VMEM_BYTES),
        cost_estimate=pl.CostEstimate(
            flops=0, bytes_accessed=4 * (end - first) * blocks * half, transcendentals=0
        ),
        name="pick_columns",
    )(side.reshape(1), source)


def product_kernel(depths, parts, base, has_total, *refs):
    place_ref, refs = refs[0], refs[1:]
    hidden, refs = refs[: 2 * parts], refs[2 * parts :]
    weights, out_ref = refs[: sum(len(pieces) for pieces in depths)], refs[-1]
    half = sum(depths[0])
    blocks = hidden[0].shape[1] // half

    total, used = refs[-2][...] if has_total else None, 0
    for p, pieces in enumerate(depths):
        place = place_ref[base + p]
        here = place < blocks
        columns = pl.ds(pl.multiple_of(jnp.where(here, place, place - blocks) * half, half), half)
        rows = [
            jnp.where(here, hidden[2 * q][:, columns], hidden[2 * q + 1][:, columns])
            for q in range(parts)
        ]
        rows = rows[0] if parts == 1 else jnp.concatenate(rows, 0)
        piece = [w[...] for w in weights[used : used + len(pieces)]]
        piece = piece[0] if len(piece) == 1 else jnp.concatenate(piece, 0)
        used += len(pieces)
        term = jnp.dot(rows, piece, preferred_element_type=jnp.float32)
        total = term if total is None else total + term
    out_ref[...] = total


def products(total, hidden, weights, places, base):
    shards = len(weights)
    flat = [w for shard in weights for w in shard]
    depths = tuple(tuple(w.shape[0] for w in shard) for shard in weights)
    half, width = sum(depths[0]), flat[0].shape[1]
    rows = sum(pair[0].shape[0] for pair in hidden)
    operands = [places] + [array for pair in hidden for array in pair] + flat
    if total is not None:
        operands.append(total)
    vmem = pl.BlockSpec(memory_space=pltpu.VMEM)
    return pl.pallas_call(
        functools.partial(
            product_kernel, depths, len(hidden), base, total is not None
        ),
        out_shape=jax.ShapeDtypeStruct((rows, width), jnp.float32),
        in_specs=[pl.BlockSpec(memory_space=pltpu.SMEM)] + [vmem] * (len(operands) - 1),
        out_specs=vmem,
        compiler_params=pltpu.CompilerParams(vmem_limit_bytes=VMEM_BYTES),
        cost_estimate=pl.CostEstimate(
            flops=2 * rows * half * width * shards,
            bytes_accessed=shards * 2 * half * (rows + width) + 4 * rows * width,
            transcendentals=0,
        ),
        name="products",
    )(*operands)


def ring_order(row_count):
    evens = list(range(0, row_count, 2))
    odds = list(range(1, row_count, 2))
    return evens + odds[::-1]


def fence(*values):
    return lax.optimization_barrier(values)


def body(passages, kv_weight, new_hidden, queries, lengths, destinations):
    tokens = passages.shape[0]
    requests, steps, half_model = new_hidden.shape
    row_count = lax.axis_size("rows")
    group_count = lax.axis_size("groups")
    row_index = lax.axis_index("rows")
    side = lax.axis_index("groups") % 2
    core = lax.axis_index("tensor")
    depth = kv_weight.shape[0]
    half = depth // 2
    local_heads = kv_weight.shape[2] // HD
    group = queries.shape[2] // kv_weight.shape[2]
    count = requests * steps
    new_padded = -(-count // 16) * 16
    half_rows = row_count // 2

    partners = [(g, g ^ 1) for g in range(group_count)]
    cores = [(0, 1), (1, 0)]
    order = ring_order(row_count)
    onward = [(order[i], order[(i + 1) % row_count]) for i in range(row_count)]
    back = [(b, a) for a, b in onward]
    place = {row: i for i, row in enumerate(order)}
    shard_order = [
        [order[(place[r] + d) % row_count] for r in range(row_count)]
        for k in range(half_rows + 1)
        for d in ([0] if k == 0 else [-k, k] if k < half_rows else [k])
    ]
    owners = lax.dynamic_index_in_dim(jnp.array(shard_order, jnp.int32), row_index, 1, keepdims=False)
    places = ((owners // half_rows) ^ core) * half_rows + owners % half_rows

    own = own_half(kv_weight, side)

    ring, ends = [[(piece, piece)] for piece in own], [None, None]

    def halved(pair):
        return pair[0][: half // 2], pair[1][half // 2 :]

    def step(c):
        pair = ring[c][-1]
        if len(ring[c]) == half_rows:
            pair = ends[c]
        ring[c].append((lax.ppermute(pair[0], "rows", onward), lax.ppermute(pair[1], "rows", back)))

    def fence_with(c, *others):
        ring[c][-1], others = fence(ring[c][-1], others)
        return others

    def project(c, hidden, total, begin, end):
        weights = [(own[c],)] + [(w,) for pair in ring[c][1:half_rows] for w in pair]
        weights += ring[c][half_rows:]
        for at in range(begin, end, MOST_SHARDS):
            some = weights[at : min(at + MOST_SHARDS, end)]
            total = products(total, hidden, some, places, at)
        return total

    def homeward(total):
        tokens_total = (total[:tokens] * RAISE).astype(jnp.float16)
        return tokens_total, total[tokens + new_padded :], total[tokens : tokens + count]

    cuts = (0, tokens // 10, tokens // 20 * 11, tokens)
    sent = [pick_columns(passages, 1 - side, half, cuts[0], cuts[1])]
    (passages_later, new_hidden) = fence_with(0, passages, new_hidden)
    got = [lax.ppermute(sent[0], "groups", partners)]
    step(0)
    passages = passages_later
    sent += [pick_columns(passages, 1 - side, half, *cuts[i : i + 2]) for i in (1, 2)]
    kept = pick_columns(passages, side, half, 0, tokens)
    new_rows = jnp.swapaxes(new_hidden, 0, 1).reshape(count, half_model)
    new_rows = jnp.pad(new_rows, ((0, new_padded - count), (0, 0)))
    new_sent = pick_columns(new_rows, 1 - side, half, 0, new_padded)
    new_kept = pick_columns(new_rows, side, half, 0, new_padded)
    new_got = lax.ppermute(new_sent, "groups", partners)
    got[0], sent, kept, new_got, new_kept, lengths, destinations = fence_with(
        0, got[0], sent, kept, new_got, new_kept, lengths, destinations
    )
    new_kept = jnp.concatenate([new_kept, new_got], 0)

    got.append(lax.ppermute(sent[1], "groups", partners))
    step(0)
    kept_other = lax.ppermute(kept, "tensor", cores)
    got_other = [lax.ppermute(got[0], "tensor", cores)]
    kept_other, got_other = fence_with(1, kept_other, got_other)
    step(1)
    position, new_position, key_info, query_info = token_tables(
        lengths, destinations, row_index, tokens, requests, steps, new_padded
    )
    cosine, sine = angle_tables(position)
    new_cosine, new_sine = angle_tables(new_position)
    tables = (cosine, sine, new_cosine, new_sine, key_info, query_info)
    got[1], tables, places, ring[1][-1] = fence_with(0, got[1], tables, places, ring[1][-1])

    own_hidden = [(kept, kept_other)]
    early = row_count - 3
    got.append(lax.ppermute(sent[2], "groups", partners))
    step(0)
    got_other.append(lax.ppermute(got[1], "tensor", cores))
    (got_other[1],) = fence_with(1, got_other[1])
    step(1)
    for k in range(3, half_rows - 1):
        (ring[1][-1],) = fence_with(0, ring[1][-1])
        step(0)
        step(1)
    held = [project(0, own_hidden, None, 0, early)]
    ends[0] = halved(ring[0][-1])
    got[2], new_kept, held, places, ring[1][-1], ends[0] = fence_with(
        0, got[2], new_kept, held, places, ring[1][-1], ends[0]
    )

    step(0)
    got_other.append(lax.ppermute(got[2], "tensor", cores))
    new_other = lax.ppermute(new_kept, "tensor", cores)
    new_other, got_other[2] = fence_with(1, new_other, got_other[2])
    step(1)
    away_hidden = list(zip(got, got_other)) + [(new_kept, new_other)]
    held.append(project(1, own_hidden, None, 0, early))
    places, held = fence(places, held)
    away = project(0, away_hidden, None, 0, row_count)
    away, places = fence(homeward(away), places)
    (places,) = fence_with(1, places)
    ends[1] = halved(ring[1][-1])
    step(1)
    homed = [lax.ppermute(away[0], "groups", partners)]
    new_own, new_away = [away[2]], [away[1]]
    away = project(1, away_hidden, None, 0, row_count - 1)
    away = homeward(project(1, away_hidden, away, row_count - 1, row_count))
    new_own.append(away[2])
    new_away.append(away[1])
    new_back = lax.ppermute(jnp.concatenate(new_away, 1), "groups", partners)
    held[0] = project(0, own_hidden, held[0], early, row_count)
    queries = jnp.swapaxes(queries, 0, 1).reshape(count, -1)
    homed[0], away, held, new_own, new_back, queries, places = fence(
        homed[0], away, held, new_own, new_back, queries, places
    )

    homed.append(lax.ppermute(away[0], "groups", partners))
    held[1] = project(1, own_hidden, held[1], early, row_count)
    cosine, sine, new_cosine, new_sine, key_info, query_info = tables
    moved = pack(new_own, new_back, new_cosine, new_sine, queries)
    moved = moved.reshape(steps, requests, -1)
    moved = jnp.swapaxes(moved, 0, 1)
    moved = lax.all_to_all(moved, "rows", split_axis=0, concat_axis=0, tiled=True)
    moved = jnp.swapaxes(moved, 0, 1).reshape(count, -1)
    heads_width = queries.shape[1]
    query_rows, new_pairs = moved[:, :heads_width], moved[:, heads_width:]
    new_pairs = jnp.pad(new_pairs, ((0, new_padded - count), (0, 0)))
    homed = [total.astype(jnp.float32) * (1.0 / RAISE) for total in homed]
    attended = finish(held, homed, cosine, sine, key_info, query_info, new_pairs, query_rows)
    attended = jnp.swapaxes(attended.reshape(steps, requests, -1), 0, 1)
    return lax.all_to_all(attended, "rows", split_axis=0, concat_axis=0, tiled=True)


def solution(mesh):
    placed = (
        P(("groups", "rows"), "tensor"),
        P("rows", None, "tensor"),
        P(("groups", "rows"), None, "tensor"),
        P(("groups", "rows"), None, "tensor"),
        P("groups", None),
        P("groups", None),
    )
    return jax.shard_map(
        body,
        mesh=mesh,
        in_specs=placed,
        out_specs=P(("groups", "rows"), None, "tensor"),
        check_vma=False,
    )
```

```python
import functools
import math

import jax
import jax.numpy as jnp
from jax import lax
from jax.experimental import pallas as pl
from jax.experimental.pallas import tpu as pltpu
from jax.sharding import PartitionSpec as P

HD = 128
HALF = HD // 2
CHUNKS = 2
MOST_SHARDS = 8
VMEM_BYTES = 20 << 20
MERGED = 4
RAISE = 16.0


def angle_tables(positions):
    index_float = jnp.arange(HALF, dtype=jnp.float32)
    inverse = jnp.exp(index_float * (-2.0 * math.log(1000000.0) / HD))
    angles = positions.astype(jnp.float32)[:, None] * inverse
    return jnp.cos(angles), jnp.sin(angles)


def token_tables(lengths, destinations, row_index, tokens, requests, steps, padded):
    my_lengths = lax.dynamic_index_in_dim(lengths, row_index, 0, keepdims=False)
    my_targets = lax.dynamic_index_in_dim(destinations, row_index, 0, keepdims=False)
    ends = jnp.cumsum(my_lengths)
    starts = ends - my_lengths
    token = jnp.arange(tokens, dtype=jnp.int32)[:, None]
    inside = (starts[None, :] <= token) & (token < ends[None, :])
    token_position = token[:, 0] - jnp.sum(jnp.where(inside, starts[None, :], 0), axis=1)
    token_target = jnp.sum(jnp.where(inside, my_targets[None, :], 0), axis=1)
    received = jnp.sum(jnp.where(destinations == row_index, lengths, 0), axis=1)
    step = jnp.repeat(jnp.arange(steps, dtype=jnp.int32), requests)
    new_target = jnp.tile(jnp.arange(requests, dtype=jnp.int32), steps)
    new_position = jnp.tile(received, steps) + step
    spare = jnp.zeros((padded - requests * steps,), jnp.int32)
    target = jnp.concatenate([token_target, new_target, spare - 1])
    seen_from = jnp.concatenate([jnp.zeros_like(token_target), step, spare])
    query_info = jnp.stack([new_target, step], 1)
    return token_position, new_position, jnp.stack([target, seen_from], 0), query_info


def rotate(first, second, cosine, sine):
    return [first * cosine - second * sine, second * cosine + first * sine]


def finish_kernel(chunks, group, *refs):
    held, homed, refs = refs[:chunks], refs[chunks : 2 * chunks], refs[2 * chunks :]
    cos_ref, sin_ref, keys_ref, rows_ref, new_ref, query_ref, out_ref = refs
    cosine, sine = cos_ref[...], sin_ref[...]
    allowed = (keys_ref[0:1, :] == rows_ref[:, 0:1]) & (keys_ref[1:2, :] <= rows_ref[:, 1:2])
    allowed = jnp.concatenate([allowed.astype(jnp.float32)] * group, 0) > 0.5
    queries = query_ref[...].astype(jnp.float32)
    count = queries.shape[0]
    width = held[0].shape[1]
    heads = width // (2 * HD)
    for h in range(chunks * heads):
        c, local = h // heads, h % heads
        key_at = slice(local * HD, (local + 1) * HD)
        value_at = slice((heads + local) * HD, (heads + local + 1) * HD)
        new_at = c * width
        both = held[c][:, key_at] + homed[c][:, key_at]
        keys = jnp.concatenate(rotate(both[:, :HALF], both[:, HALF:], cosine, sine), -1)
        values = held[c][:, value_at] + homed[c][:, value_at]
        keys, values = (
            jnp.concatenate(
                [cached.astype(jnp.bfloat16), new_ref[:, new_at + at.start : new_at + at.stop]], 0
            )
            for cached, at in ((keys, key_at), (values, value_at))
        )
        at = h * group * HD
        query = jnp.concatenate(
            [queries[:, at + g * HD : at + (g + 1) * HD] for g in range(group)], 0
        ).astype(jnp.bfloat16)
        scores = lax.dot_general(
            query, keys, (((1,), (1,)), ((), ())), preferred_element_type=jnp.float32
        )
        scores = jnp.where(allowed, scores * (1.0 / math.sqrt(HD)), jnp.float32(-1e30))
        raised = jnp.exp(scores - jnp.max(scores, axis=-1, keepdims=True))
        total = jnp.sum(raised, axis=-1, keepdims=True)
        weights = (raised / total).astype(jnp.bfloat16)
        output = jnp.dot(weights, values, preferred_element_type=jnp.float32)
        for g in range(group):
            out_ref[:, at + g * HD : at + (g + 1) * HD] = output[
                g * count : (g + 1) * count
            ].astype(jnp.bfloat16)


def finish(held, homed, cosine, sine, key_info, query_info, new_pairs, queries):
    rows, width = held[0].shape
    heads = len(held) * width // (2 * HD)
    group = queries.shape[1] // (heads * HD)
    count = queries.shape[0]
    vmem = pl.BlockSpec(memory_space=pltpu.VMEM)
    operands = [*held, *homed, cosine, sine, key_info, query_info, new_pairs, queries]
    return pl.pallas_call(
        functools.partial(finish_kernel, len(held), group),
        out_shape=jax.ShapeDtypeStruct(queries.shape, jnp.bfloat16),
        in_specs=[vmem] * len(operands),
        out_specs=vmem,
        compiler_params=pltpu.CompilerParams(vmem_limit_bytes=VMEM_BYTES),
        cost_estimate=pl.CostEstimate(
            flops=4 * heads * group * count * rows * HD,
            bytes_accessed=8 * len(held) * rows * width + 4 * queries.size,
            transcendentals=heads * group * count * rows,
        ),
        name="rotate_attend",
    )(*operands)


def own_kernel(side_ref, weight_ref, *out_refs):
    chunk = out_refs[0].shape[1] // 2
    for kind in range(2):
        columns = weight_ref[:, kind, :]
        for c, out_ref in enumerate(out_refs):
            out_ref[:, kind * chunk : (kind + 1) * chunk] = columns[:, c * chunk : (c + 1) * chunk]


def own_half(weight, side):
    depth, kinds, width = weight.shape
    half = depth // 2
    chunk = kinds * width // CHUNKS
    return pl.pallas_call(
        own_kernel,
        out_shape=[jax.ShapeDtypeStruct((half, chunk), weight.dtype)] * CHUNKS,
        grid_spec=pltpu.PrefetchScalarGridSpec(
            num_scalar_prefetch=1,
            grid=(2,),
            in_specs=[
                pl.BlockSpec((half // 2, kinds, width), lambda i, s: (2 * s[0] + i, 0, 0))
            ],
            out_specs=[pl.BlockSpec((half // 2, chunk), lambda i, s: (i, 0))] * CHUNKS,
        ),
        compiler_params=pltpu.CompilerParams(vmem_limit_bytes=VMEM_BYTES),
        cost_estimate=pl.CostEstimate(
            flops=0, bytes_accessed=8 * half * width * kinds, transcendentals=0
        ),
        name="own_half",
    )(side.reshape(1), weight)


def pack_kernel(chunks, own_ref, *refs):
    owns, (got_ref, cos_ref, sin_ref, query_ref, out_ref) = (own_ref, *refs[: chunks - 1]), refs[chunks - 1 :]
    cosine, sine = cos_ref[...], sin_ref[...]
    count, base = query_ref.shape
    width = owns[0].shape[1]
    half = width // 2
    out_ref[:, :base] = query_ref[...]
    for c in range(chunks):
        for h in range(half // HD):
            at = h * HD
            both = owns[c][:, at : at + HD] + got_ref[:count, c * width + at : c * width + at + HD]
            both = jnp.concatenate(rotate(both[:, :HALF], both[:, HALF:], cosine, sine), -1)
            at += base + c * width
            out_ref[:, at : at + HD] = both.astype(jnp.bfloat16)
        values = owns[c][:, half:] + got_ref[:count, c * width + half : (c + 1) * width]
        at = base + c * width + half
        out_ref[:, at : at + half] = values.astype(jnp.bfloat16)


def pack(owns, got, cosine, sine, queries):
    vmem = pl.BlockSpec(memory_space=pltpu.VMEM)
    width = queries.shape[1] + got.shape[1]
    return pl.pallas_call(
        functools.partial(pack_kernel, len(owns)),
        out_shape=jax.ShapeDtypeStruct((queries.shape[0], width), jnp.bfloat16),
        in_specs=[vmem] * (len(owns) + 4),
        out_specs=vmem,
        compiler_params=pltpu.CompilerParams(vmem_limit_bytes=VMEM_BYTES),
        cost_estimate=pl.CostEstimate(
            flops=0, bytes_accessed=4 * queries.size + 10 * got.size, transcendentals=0
        ),
        name="pack_new",
    )(*owns, got, cosine, sine, queries)


def pick_kernel(first, side_ref, source_ref, out_ref):
    out_ref[...] = source_ref[first : first + out_ref.shape[0], :]


def pick_columns(source, side, half, first, end):
    rows, blocks = source.shape[0], source.shape[1] // (2 * half)
    return pl.pallas_call(
        functools.partial(pick_kernel, first),
        out_shape=jax.ShapeDtypeStruct((end - first, blocks * half), source.dtype),
        grid_spec=pltpu.PrefetchScalarGridSpec(
            num_scalar_prefetch=1,
            grid=(blocks,),
            in_specs=[pl.BlockSpec((rows, half), lambda j, s: (0, 2 * j + s[0]))],
            out_specs=pl.BlockSpec((end - first, half), lambda j, s: (0, j)),
        ),
        compiler_params=pltpu.CompilerParams(vmem_limit_bytes=VMEM_BYTES),
        cost_estimate=pl.CostEstimate(
            flops=0, bytes_accessed=4 * (end - first) * blocks * half, transcendentals=0
        ),
        name="pick_columns",
    )(side.reshape(1), source)


def product_kernel(depths, parts, base, has_total, *refs):
    place_ref, refs = refs[0], refs[1:]
    hidden, refs = refs[: 2 * parts], refs[2 * parts :]
    weights, out_ref = refs[: sum(len(pieces) for pieces in depths)], refs[-1]
    half = sum(depths[0])
    blocks = hidden[0].shape[1] // half

    total, used = refs[-2][...] if has_total else None, 0
    for p, pieces in enumerate(depths):
        place = place_ref[base + p]
        here = place < blocks
        columns = pl.ds(pl.multiple_of(jnp.where(here, place, place - blocks) * half, half), half)
        rows = [
            jnp.where(here, hidden[2 * q][:, columns], hidden[2 * q + 1][:, columns])
            for q in range(parts)
        ]
        rows = rows[0] if parts == 1 else jnp.concatenate(rows, 0)
        piece = [w[...] for w in weights[used : used + len(pieces)]]
        piece = piece[0] if len(piece) == 1 else jnp.concatenate(piece, 0)
        used += len(pieces)
        term = jnp.dot(rows, piece, preferred_element_type=jnp.float32)
        total = term if total is None else total + term
    out_ref[...] = total


def products(total, hidden, weights, places, base):
    shards = len(weights)
    flat = [w for shard in weights for w in shard]
    depths = tuple(tuple(w.shape[0] for w in shard) for shard in weights)
    half, width = sum(depths[0]), flat[0].shape[1]
    rows = sum(pair[0].shape[0] for pair in hidden)
    operands = [places] + [array for pair in hidden for array in pair] + flat
    if total is not None:
        operands.append(total)
    vmem = pl.BlockSpec(memory_space=pltpu.VMEM)
    return pl.pallas_call(
        functools.partial(
            product_kernel, depths, len(hidden), base, total is not None
        ),
        out_shape=jax.ShapeDtypeStruct((rows, width), jnp.float32),
        in_specs=[pl.BlockSpec(memory_space=pltpu.SMEM)] + [vmem] * (len(operands) - 1),
        out_specs=vmem,
        compiler_params=pltpu.CompilerParams(vmem_limit_bytes=VMEM_BYTES),
        cost_estimate=pl.CostEstimate(
            flops=2 * rows * half * width * shards,
            bytes_accessed=shards * 2 * half * (rows + width) + 4 * rows * width,
            transcendentals=0,
        ),
        name="products",
    )(*operands)


def ring_order(row_count):
    evens = list(range(0, row_count, 2))
    odds = list(range(1, row_count, 2))
    return evens + odds[::-1]


def fence(*values):
    return lax.optimization_barrier(values)


def body(passages, kv_weight, new_hidden, queries, lengths, destinations):
    tokens = passages.shape[0]
    requests, steps, half_model = new_hidden.shape
    row_count = lax.axis_size("rows")
    group_count = lax.axis_size("groups")
    row_index = lax.axis_index("rows")
    side = lax.axis_index("groups") % 2
    core = lax.axis_index("tensor")
    depth = kv_weight.shape[0]
    half = depth // 2
    local_heads = kv_weight.shape[2] // HD
    group = queries.shape[2] // kv_weight.shape[2]
    count = requests * steps
    new_padded = -(-count // 16) * 16
    half_rows = row_count // 2

    partners = [(g, g ^ 1) for g in range(group_count)]
    cores = [(0, 1), (1, 0)]
    order = ring_order(row_count)
    onward = [(order[i], order[(i + 1) % row_count]) for i in range(row_count)]
    back = [(b, a) for a, b in onward]
    place = {row: i for i, row in enumerate(order)}
    shard_order = [
        [order[(place[r] + d) % row_count] for r in range(row_count)]
        for k in range(half_rows + 1)
        for d in ([0] if k == 0 else [-k, k] if k < half_rows else [k])
    ]
    owners = lax.dynamic_index_in_dim(jnp.array(shard_order, jnp.int32), row_index, 1, keepdims=False)
    places = ((owners // half_rows) ^ core) * half_rows + owners % half_rows

    own = own_half(kv_weight, side)

    ring, ends = [[(piece, piece)] for piece in own], [None, None]

    def halved(pair):
        return pair[0][: half // 2], pair[1][half // 2 :]

    def step(c):
        pair = ring[c][-1]
        if len(ring[c]) == half_rows:
            pair = ends[c]
        ring[c].append((lax.ppermute(pair[0], "rows", onward), lax.ppermute(pair[1], "rows", back)))

    def fence_with(c, *others):
        ring[c][-1], others = fence(ring[c][-1], others)
        return others

    def project(c, hidden, total, begin, end):
        weights = [(own[c],)] + [(w,) for pair in ring[c][1:half_rows] for w in pair]
        weights += ring[c][half_rows:]
        for at in range(begin, end, MOST_SHARDS):
            some = weights[at : min(at + MOST_SHARDS, end)]
            total = products(total, hidden, some, places, at)
        return total

    def homeward(total):
        tokens_total = (total[:tokens] * RAISE).astype(jnp.float16)
        return tokens_total, total[tokens + new_padded :], total[tokens : tokens + count]

    cuts = (0, 3 * tokens // 20, 23 * tokens // 40, tokens)
    sent = [pick_columns(passages, 1 - side, half, cuts[0], cuts[1])]
    (passages_later, new_hidden) = fence_with(0, passages, new_hidden)
    got = [lax.ppermute(sent[0], "groups", partners)]
    step(0)
    passages = passages_later
    sent += [pick_columns(passages, 1 - side, half, *cuts[i : i + 2]) for i in (1, 2)]
    kept = pick_columns(passages, side, half, 0, tokens)
    new_rows = jnp.swapaxes(new_hidden, 0, 1).reshape(count, half_model)
    new_rows = jnp.pad(new_rows, ((0, new_padded - count), (0, 0)))
    new_sent = pick_columns(new_rows, 1 - side, half, 0, new_padded)
    new_kept = pick_columns(new_rows, side, half, 0, new_padded)
    got[0], sent, kept, new_sent, new_kept, lengths, destinations = fence_with(
        0, got[0], sent, kept, new_sent, new_kept, lengths, destinations
    )

    got.append(lax.ppermute(sent[1], "groups", partners))
    step(0)
    kept_other = lax.ppermute(kept, "tensor", cores)
    got_other = [lax.ppermute(got[0], "tensor", cores)]
    kept_other, got_other = fence_with(1, kept_other, got_other)
    step(1)
    position, new_position, key_info, query_info = token_tables(
        lengths, destinations, row_index, tokens, requests, steps, new_padded
    )
    cosine, sine = angle_tables(position)
    new_cosine, new_sine = angle_tables(new_position)
    tables = (cosine, sine, new_cosine, new_sine, key_info, query_info)
    got[1], tables, places, ring[1][-1] = fence_with(0, got[1], tables, places, ring[1][-1])

    own_hidden = [(kept, kept_other)]
    early = row_count - 3
    got.append(lax.ppermute(sent[2], "groups", partners))
    step(0)
    got_other.append(lax.ppermute(got[1], "tensor", cores))
    (got_other[1],) = fence_with(1, got_other[1])
    step(1)
    for k in range(3, half_rows - 1):
        (ring[1][-1],) = fence_with(0, ring[1][-1])
        step(0)
        step(1)
    held = [project(0, own_hidden, None, 0, early)]
    ends[0] = halved(ring[0][-1])
    got[2], new_sent, held, places, ring[1][-1], ends[0] = fence_with(
        0, got[2], new_sent, held, places, ring[1][-1], ends[0]
    )

    step(0)
    got_other.append(lax.ppermute(got[2], "tensor", cores))
    new_kept = jnp.concatenate([new_kept, lax.ppermute(new_sent, "groups", partners)], 0)
    new_other = lax.ppermute(new_kept, "tensor", cores)
    (got_other[2],) = fence_with(1, got_other[2])
    step(1)
    away_hidden = list(zip(got, got_other)) + [(new_kept, new_other)]
    held.append(project(1, own_hidden, None, 0, early))
    places, held = fence(places, held)
    away = project(0, away_hidden, None, 0, row_count)
    away, places = fence(homeward(away), places)
    (places,) = fence_with(1, places)
    ends[1] = halved(ring[1][-1])
    step(1)
    homed = [lax.ppermute(away[0], "groups", partners)]
    new_own, new_away = [away[2]], [away[1]]
    away = project(1, away_hidden, None, 0, row_count - 1)
    away = homeward(project(1, away_hidden, away, row_count - 1, row_count))
    new_own.append(away[2])
    new_away.append(away[1])
    new_back = lax.ppermute(jnp.concatenate(new_away, 1), "groups", partners)
    held[0] = project(0, own_hidden, held[0], early, row_count)
    queries = jnp.swapaxes(queries, 0, 1).reshape(count, -1)
    held, queries, places = fence(held, queries, places)
    homed.append(lax.ppermute(away[0], "groups", partners))
    cosine, sine, new_cosine, new_sine, key_info, query_info = tables
    moved = pack(new_own, new_back, new_cosine, new_sine, queries)
    moved, places = fence(moved, places)
    held[1] = project(1, own_hidden, held[1], early, row_count)
    moved = moved.reshape(steps, requests, -1)
    moved = jnp.swapaxes(moved, 0, 1)
    moved = lax.all_to_all(moved, "rows", split_axis=0, concat_axis=0, tiled=True)
    moved = jnp.swapaxes(moved, 0, 1).reshape(count, -1)
    heads_width = queries.shape[1]
    query_rows, new_pairs = moved[:, :heads_width], moved[:, heads_width:]
    new_pairs = jnp.pad(new_pairs, ((0, new_padded - count), (0, 0)))
    homed = [total.astype(jnp.float32) * (1.0 / RAISE) for total in homed]
    attended = finish(held, homed, cosine, sine, key_info, query_info, new_pairs, query_rows)
    attended = jnp.swapaxes(attended.reshape(steps, requests, -1), 0, 1)
    return lax.all_to_all(attended, "rows", split_axis=0, concat_axis=0, tiled=True)


def solution(mesh):
    placed = (
        P(("groups", "rows"), "tensor"),
        P("rows", None, "tensor"),
        P(("groups", "rows"), None, "tensor"),
        P(("groups", "rows"), None, "tensor"),
        P("groups", None),
        P("groups", None),
    )
    return jax.shard_map(
        body,
        mesh=mesh,
        in_specs=placed,
        out_specs=P(("groups", "rows"), None, "tensor"),
        check_vma=False,
    )
```

```python
import functools
import math

import jax
import jax.numpy as jnp
from jax import lax
from jax.experimental import pallas as pl
from jax.experimental.pallas import tpu as pltpu
from jax.sharding import PartitionSpec as P

HD = 128
HALF = HD // 2
CHUNKS = 2
MOST_SHARDS = 8
VMEM_BYTES = 20 << 20
MERGED = 4
RAISE = 16.0


def angle_table(positions):
    index_float = jnp.arange(HALF, dtype=jnp.float32)
    inverse = jnp.exp(index_float * (-2.0 * math.log(1000000.0) / HD))
    angles = positions.astype(jnp.float32)[:, None] * inverse
    return jnp.concatenate([jnp.cos(angles), jnp.sin(angles)], 1)


def token_tables(lengths, destinations, row_index, tokens, requests, steps, padded):
    my_lengths = lax.dynamic_index_in_dim(lengths, row_index, 0, keepdims=False)
    my_targets = lax.dynamic_index_in_dim(destinations, row_index, 0, keepdims=False)
    ends = jnp.cumsum(my_lengths)
    starts = ends - my_lengths
    token = jnp.arange(tokens, dtype=jnp.int32)[:, None]
    inside = (starts[None, :] <= token) & (token < ends[None, :])
    token_position = token[:, 0] - jnp.sum(jnp.where(inside, starts[None, :], 0), axis=1)
    token_target = jnp.sum(jnp.where(inside, my_targets[None, :], 0), axis=1)
    received = jnp.sum(jnp.where(destinations == row_index, lengths, 0), axis=1)
    step = jnp.repeat(jnp.arange(steps, dtype=jnp.int32), requests)
    new_target = jnp.tile(jnp.arange(requests, dtype=jnp.int32), steps)
    new_position = jnp.tile(received, steps) + step
    spare = jnp.zeros((padded - requests * steps,), jnp.int32)
    target = jnp.concatenate([token_target, new_target, spare - 1])
    seen_from = jnp.concatenate([jnp.zeros_like(token_target), step, spare])
    query_info = jnp.stack([new_target, step], 1)
    return token_position, new_position, jnp.stack([target, seen_from], 0), query_info


def rotate(first, second, cosine, sine):
    return [first * cosine - second * sine, second * cosine + first * sine]


def finish_kernel(chunks, group, *refs):
    held, homed, refs = refs[:chunks], refs[chunks : 2 * chunks], refs[2 * chunks :]
    angle_ref, keys_ref, rows_ref, new_ref, query_ref, out_ref = refs
    cosine, sine = angle_ref[:, :HALF], angle_ref[:, HALF:]
    allowed = (keys_ref[0:1, :] == rows_ref[:, 0:1]) & (keys_ref[1:2, :] <= rows_ref[:, 1:2])
    allowed = jnp.concatenate([allowed.astype(jnp.float32)] * group, 0) > 0.5
    queries = query_ref[...].astype(jnp.float32)
    count = queries.shape[0]
    width = held[0].shape[1]
    heads = width // (2 * HD)
    for h in range(chunks * heads):
        c, local = h // heads, h % heads
        key_at = slice(local * HD, (local + 1) * HD)
        value_at = slice((heads + local) * HD, (heads + local + 1) * HD)
        new_at = c * width
        both = held[c][:, key_at] + homed[c][:, key_at]
        keys = jnp.concatenate(rotate(both[:, :HALF], both[:, HALF:], cosine, sine), -1)
        values = held[c][:, value_at] + homed[c][:, value_at]
        keys, values = (
            jnp.concatenate(
                [cached.astype(jnp.bfloat16), new_ref[:, new_at + at.start : new_at + at.stop]], 0
            )
            for cached, at in ((keys, key_at), (values, value_at))
        )
        at = h * group * HD
        query = jnp.concatenate(
            [queries[:, at + g * HD : at + (g + 1) * HD] for g in range(group)], 0
        ).astype(jnp.bfloat16)
        scores = lax.dot_general(
            query, keys, (((1,), (1,)), ((), ())), preferred_element_type=jnp.float32
        )
        scores = jnp.where(allowed, scores * (1.0 / math.sqrt(HD)), jnp.float32(-1e30))
        raised = jnp.exp(scores - jnp.max(scores, axis=-1, keepdims=True))
        total = jnp.sum(raised, axis=-1, keepdims=True)
        weights = (raised / total).astype(jnp.bfloat16)
        output = jnp.dot(weights, values, preferred_element_type=jnp.float32)
        for g in range(group):
            out_ref[:, at + g * HD : at + (g + 1) * HD] = output[
                g * count : (g + 1) * count
            ].astype(jnp.bfloat16)


def finish(held, homed, angles, key_info, query_info, new_pairs, queries):
    rows, width = held[0].shape
    heads = len(held) * width // (2 * HD)
    group = queries.shape[1] // (heads * HD)
    count = queries.shape[0]
    vmem = pl.BlockSpec(memory_space=pltpu.VMEM)
    operands = [*held, *homed, angles, key_info, query_info, new_pairs, queries]
    return pl.pallas_call(
        functools.partial(finish_kernel, len(held), group),
        out_shape=jax.ShapeDtypeStruct(queries.shape, jnp.bfloat16),
        in_specs=[vmem] * len(operands),
        out_specs=vmem,
        compiler_params=pltpu.CompilerParams(vmem_limit_bytes=VMEM_BYTES),
        cost_estimate=pl.CostEstimate(
            flops=4 * heads * group * count * rows * HD,
            bytes_accessed=8 * len(held) * rows * width + 4 * queries.size,
            transcendentals=heads * group * count * rows,
        ),
        name="rotate_attend",
    )(*operands)


def own_kernel(side_ref, weight_ref, *out_refs):
    chunk = out_refs[0].shape[1] // 2
    for kind in range(2):
        columns = weight_ref[:, kind, :]
        for c, out_ref in enumerate(out_refs):
            out_ref[:, kind * chunk : (kind + 1) * chunk] = columns[:, c * chunk : (c + 1) * chunk]


def own_half(weight, side):
    depth, kinds, width = weight.shape
    half = depth // 2
    chunk = kinds * width // CHUNKS
    return pl.pallas_call(
        own_kernel,
        out_shape=[jax.ShapeDtypeStruct((half, chunk), weight.dtype)] * CHUNKS,
        grid_spec=pltpu.PrefetchScalarGridSpec(
            num_scalar_prefetch=1,
            grid=(2,),
            in_specs=[
                pl.BlockSpec((half // 2, kinds, width), lambda i, s: (2 * s[0] + i, 0, 0))
            ],
            out_specs=[pl.BlockSpec((half // 2, chunk), lambda i, s: (i, 0))] * CHUNKS,
        ),
        compiler_params=pltpu.CompilerParams(vmem_limit_bytes=VMEM_BYTES),
        cost_estimate=pl.CostEstimate(
            flops=0, bytes_accessed=8 * half * width * kinds, transcendentals=0
        ),
        name="own_half",
    )(side.reshape(1), weight)


def pack_kernel(chunks, own_ref, *refs):
    owns, (got_ref, angle_ref, query_ref, out_ref) = (own_ref, *refs[: chunks - 1]), refs[chunks - 1 :]
    cosine, sine = angle_ref[:, :HALF], angle_ref[:, HALF:]
    count, base = query_ref.shape
    width = owns[0].shape[1]
    half = width // 2
    out_ref[:, :base] = query_ref[...]
    for c in range(chunks):
        for h in range(half // HD):
            at = h * HD
            both = owns[c][:, at : at + HD] + got_ref[:count, c * width + at : c * width + at + HD]
            both = jnp.concatenate(rotate(both[:, :HALF], both[:, HALF:], cosine, sine), -1)
            at += base + c * width
            out_ref[:, at : at + HD] = both.astype(jnp.bfloat16)
        values = owns[c][:, half:] + got_ref[:count, c * width + half : (c + 1) * width]
        at = base + c * width + half
        out_ref[:, at : at + half] = values.astype(jnp.bfloat16)


def pack(owns, got, angles, queries):
    vmem = pl.BlockSpec(memory_space=pltpu.VMEM)
    width = queries.shape[1] + got.shape[1]
    return pl.pallas_call(
        functools.partial(pack_kernel, len(owns)),
        out_shape=jax.ShapeDtypeStruct((queries.shape[0], width), jnp.bfloat16),
        in_specs=[vmem] * (len(owns) + 3),
        out_specs=vmem,
        compiler_params=pltpu.CompilerParams(vmem_limit_bytes=VMEM_BYTES),
        cost_estimate=pl.CostEstimate(
            flops=0, bytes_accessed=4 * queries.size + 10 * got.size, transcendentals=0
        ),
        name="pack_new",
    )(*owns, got, angles, queries)


def pick_kernel(first, side_ref, source_ref, out_ref):
    out_ref[...] = source_ref[first : first + out_ref.shape[0], :]


def pick_columns(source, side, half, first, end):
    rows, blocks = source.shape[0], source.shape[1] // (2 * half)
    return pl.pallas_call(
        functools.partial(pick_kernel, first),
        out_shape=jax.ShapeDtypeStruct((end - first, blocks * half), source.dtype),
        grid_spec=pltpu.PrefetchScalarGridSpec(
            num_scalar_prefetch=1,
            grid=(blocks,),
            in_specs=[pl.BlockSpec((rows, half), lambda j, s: (0, 2 * j + s[0]))],
            out_specs=pl.BlockSpec((end - first, half), lambda j, s: (0, j)),
        ),
        compiler_params=pltpu.CompilerParams(vmem_limit_bytes=VMEM_BYTES),
        cost_estimate=pl.CostEstimate(
            flops=0, bytes_accessed=4 * (end - first) * blocks * half, transcendentals=0
        ),
        name="pick_columns",
    )(side.reshape(1), source)


def product_kernel(depths, parts, base, has_total, *refs):
    place_ref, refs = refs[0], refs[1:]
    hidden, refs = refs[: 2 * parts], refs[2 * parts :]
    weights, out_ref = refs[: sum(len(pieces) for pieces in depths)], refs[-1]
    half = sum(depths[0])
    blocks = hidden[0].shape[1] // half

    total, used = refs[-2][...] if has_total else None, 0
    for p, pieces in enumerate(depths):
        place = place_ref[base + p]
        here = place < blocks
        columns = pl.ds(pl.multiple_of(jnp.where(here, place, place - blocks) * half, half), half)
        rows = [
            jnp.where(here, hidden[2 * q][:, columns], hidden[2 * q + 1][:, columns])
            for q in range(parts)
        ]
        rows = rows[0] if parts == 1 else jnp.concatenate(rows, 0)
        piece = [w[...] for w in weights[used : used + len(pieces)]]
        piece = piece[0] if len(piece) == 1 else jnp.concatenate(piece, 0)
        used += len(pieces)
        term = jnp.dot(rows, piece, preferred_element_type=jnp.float32)
        total = term if total is None else total + term
    out_ref[...] = total


def products(total, hidden, weights, places, base):
    shards = len(weights)
    flat = [w for shard in weights for w in shard]
    depths = tuple(tuple(w.shape[0] for w in shard) for shard in weights)
    half, width = sum(depths[0]), flat[0].shape[1]
    rows = sum(pair[0].shape[0] for pair in hidden)
    operands = [places] + [array for pair in hidden for array in pair] + flat
    if total is not None:
        operands.append(total)
    vmem = pl.BlockSpec(memory_space=pltpu.VMEM)
    return pl.pallas_call(
        functools.partial(
            product_kernel, depths, len(hidden), base, total is not None
        ),
        out_shape=jax.ShapeDtypeStruct((rows, width), jnp.float32),
        in_specs=[pl.BlockSpec(memory_space=pltpu.SMEM)] + [vmem] * (len(operands) - 1),
        out_specs=vmem,
        compiler_params=pltpu.CompilerParams(vmem_limit_bytes=VMEM_BYTES),
        cost_estimate=pl.CostEstimate(
            flops=2 * rows * half * width * shards,
            bytes_accessed=shards * 2 * half * (rows + width) + 4 * rows * width,
            transcendentals=0,
        ),
        name="products",
    )(*operands)


def ring_order(row_count):
    evens = list(range(0, row_count, 2))
    odds = list(range(1, row_count, 2))
    return evens + odds[::-1]


def fence(*values):
    return lax.optimization_barrier(values)


def body(passages, kv_weight, new_hidden, queries, lengths, destinations):
    tokens = passages.shape[0]
    requests, steps, half_model = new_hidden.shape
    row_count = lax.axis_size("rows")
    group_count = lax.axis_size("groups")
    row_index = lax.axis_index("rows")
    side = lax.axis_index("groups") % 2
    core = lax.axis_index("tensor")
    depth = kv_weight.shape[0]
    half = depth // 2
    local_heads = kv_weight.shape[2] // HD
    group = queries.shape[2] // kv_weight.shape[2]
    count = requests * steps
    new_padded = -(-count // 16) * 16
    half_rows = row_count // 2

    partners = [(g, g ^ 1) for g in range(group_count)]
    cores = [(0, 1), (1, 0)]
    order = ring_order(row_count)
    onward = [(order[i], order[(i + 1) % row_count]) for i in range(row_count)]
    back = [(b, a) for a, b in onward]
    place = {row: i for i, row in enumerate(order)}
    shard_order = [
        [order[(place[r] + d) % row_count] for r in range(row_count)]
        for k in range(half_rows + 1)
        for d in ([0] if k == 0 else [-k, k] if k < half_rows else [k])
    ]
    owners = lax.dynamic_index_in_dim(jnp.array(shard_order, jnp.int32), row_index, 1, keepdims=False)
    places = ((owners // half_rows) ^ core) * half_rows + owners % half_rows

    own = own_half(kv_weight, side)

    ring, ends = [[(piece, piece)] for piece in own], [None, None]

    def halved(pair):
        return pair[0][: half // 2], pair[1][half // 2 :]

    def step(c):
        pair = ring[c][-1]
        if len(ring[c]) == half_rows:
            pair = ends[c]
        ring[c].append((lax.ppermute(pair[0], "rows", onward), lax.ppermute(pair[1], "rows", back)))

    def fence_with(c, *others):
        ring[c][-1], others = fence(ring[c][-1], others)
        return others

    def project(c, hidden, total, begin, end):
        weights = [(own[c],)] + [(w,) for pair in ring[c][1:half_rows] for w in pair]
        weights += ring[c][half_rows:]
        for at in range(begin, end, MOST_SHARDS):
            some = weights[at : min(at + MOST_SHARDS, end)]
            total = products(total, hidden, some, places, at)
        return total

    def homeward(total):
        tokens_total = (total[:tokens] * RAISE).astype(jnp.float16)
        return tokens_total, total[tokens + new_padded :], total[tokens : tokens + count]

    cuts = (0, 3 * tokens // 20, 23 * tokens // 40, tokens)
    sent = [pick_columns(passages, 1 - side, half, cuts[0], cuts[1])]
    (passages_later, new_hidden) = fence_with(0, passages, new_hidden)
    got = [lax.ppermute(sent[0], "groups", partners)]
    step(0)
    passages = passages_later
    sent += [pick_columns(passages, 1 - side, half, *cuts[i : i + 2]) for i in (1, 2)]
    kept = pick_columns(passages, side, half, 0, tokens)
    new_rows = jnp.swapaxes(new_hidden, 0, 1).reshape(count, half_model)
    new_rows = jnp.pad(new_rows, ((0, new_padded - count), (0, 0)))
    new_sent = pick_columns(new_rows, 1 - side, half, 0, new_padded)
    new_kept = pick_columns(new_rows, side, half, 0, new_padded)
    got[0], sent, kept, new_sent, new_kept, lengths, destinations = fence_with(
        0, got[0], sent, kept, new_sent, new_kept, lengths, destinations
    )

    got.append(lax.ppermute(sent[1], "groups", partners))
    step(0)
    kept_other = lax.ppermute(kept, "tensor", cores)
    got_other = [lax.ppermute(got[0], "tensor", cores)]
    kept_other, got_other = fence_with(1, kept_other, got_other)
    step(1)
    position, new_position, key_info, query_info = token_tables(
        lengths, destinations, row_index, tokens, requests, steps, new_padded
    )
    angles, new_angles = angle_table(position), angle_table(new_position)
    tables = (angles, new_angles, key_info, query_info)
    got[1], tables, places, ring[1][-1] = fence_with(0, got[1], tables, places, ring[1][-1])

    own_hidden = [(kept, kept_other)]
    early = row_count - 3
    got.append(lax.ppermute(sent[2], "groups", partners))
    step(0)
    got_other.append(lax.ppermute(got[1], "tensor", cores))
    (got_other[1],) = fence_with(1, got_other[1])
    step(1)
    for k in range(3, half_rows - 1):
        (ring[1][-1],) = fence_with(0, ring[1][-1])
        step(0)
        step(1)
    held = [project(0, own_hidden, None, 0, early)]
    ends[0] = halved(ring[0][-1])
    got[2], new_sent, held, places, ring[1][-1], ends[0] = fence_with(
        0, got[2], new_sent, held, places, ring[1][-1], ends[0]
    )

    step(0)
    got_other.append(lax.ppermute(got[2], "tensor", cores))
    new_kept = jnp.concatenate([new_kept, lax.ppermute(new_sent, "groups", partners)], 0)
    new_other = lax.ppermute(new_kept, "tensor", cores)
    (got_other[2],) = fence_with(1, got_other[2])
    step(1)
    away_hidden = list(zip(got, got_other)) + [(new_kept, new_other)]
    held.append(project(1, own_hidden, None, 0, early))
    places, held = fence(places, held)
    away = project(0, away_hidden, None, 0, row_count)
    away, places = fence(homeward(away), places)
    (places,) = fence_with(1, places)
    ends[1] = halved(ring[1][-1])
    step(1)
    homed = [lax.ppermute(away[0], "groups", partners)]
    new_own, new_away = [away[2]], [away[1]]
    away = project(1, away_hidden, None, 0, row_count - 1)
    away = homeward(project(1, away_hidden, away, row_count - 1, row_count))
    new_own.append(away[2])
    new_away.append(away[1])
    new_back = lax.ppermute(jnp.concatenate(new_away, 1), "groups", partners)
    held[0] = project(0, own_hidden, held[0], early, row_count)
    queries = jnp.swapaxes(queries, 0, 1).reshape(count, -1)
    held, queries, places, away, new_back, homed[0] = fence(
        held, queries, places, away, new_back, homed[0]
    )
    homed.append(lax.ppermute(away[0], "groups", partners))
    angles, new_angles, key_info, query_info = tables
    moved = pack(new_own, new_back, new_angles, queries)
    moved, places = fence(moved, places)
    held[1] = project(1, own_hidden, held[1], early, row_count)
    moved = moved.reshape(steps, requests, -1)
    moved = jnp.swapaxes(moved, 0, 1)
    moved = lax.all_to_all(moved, "rows", split_axis=0, concat_axis=0, tiled=True)
    moved = jnp.swapaxes(moved, 0, 1).reshape(count, -1)
    heads_width = queries.shape[1]
    query_rows, new_pairs = moved[:, :heads_width], moved[:, heads_width:]
    new_pairs = jnp.pad(new_pairs, ((0, new_padded - count), (0, 0)))
    homed = [total.astype(jnp.float32) * (1.0 / RAISE) for total in homed]
    attended = finish(held, homed, angles, key_info, query_info, new_pairs, query_rows)
    attended = jnp.swapaxes(attended.reshape(steps, requests, -1), 0, 1)
    return lax.all_to_all(attended, "rows", split_axis=0, concat_axis=0, tiled=True)


def solution(mesh):
    placed = (
        P(("groups", "rows"), "tensor"),
        P("rows", None, "tensor"),
        P(("groups", "rows"), None, "tensor"),
        P(("groups", "rows"), None, "tensor"),
        P("groups", None),
        P("groups", None),
    )
    return jax.shard_map(
        body,
        mesh=mesh,
        in_specs=placed,
        out_specs=P(("groups", "rows"), None, "tensor"),
        check_vma=False,
    )
```

```python
import functools
import math

import jax
import jax.numpy as jnp
from jax import lax
from jax.experimental import pallas as pl
from jax.experimental.pallas import tpu as pltpu
from jax.sharding import PartitionSpec as P

HD = 128
HALF = HD // 2
CHUNKS = 2
MOST_SHARDS = 8
VMEM_BYTES = 20 << 20
MERGED = 4
RAISE = 16.0


def angle_table(positions):
    index_float = jnp.arange(HALF, dtype=jnp.float32)
    inverse = jnp.exp(index_float * (-2.0 * math.log(1000000.0) / HD))
    angles = positions.astype(jnp.float32)[:, None] * inverse
    return jnp.concatenate([jnp.cos(angles), jnp.sin(angles)], 1)


def token_tables(lengths, destinations, row_index, tokens, requests, steps, padded):
    my_lengths = lax.dynamic_index_in_dim(lengths, row_index, 0, keepdims=False)
    my_targets = lax.dynamic_index_in_dim(destinations, row_index, 0, keepdims=False)
    ends = jnp.cumsum(my_lengths)
    starts = ends - my_lengths
    token = jnp.arange(tokens, dtype=jnp.int32)[:, None]
    inside = (starts[None, :] <= token) & (token < ends[None, :])
    token_position = token[:, 0] - jnp.sum(jnp.where(inside, starts[None, :], 0), axis=1)
    token_target = jnp.sum(jnp.where(inside, my_targets[None, :], 0), axis=1)
    received = jnp.sum(jnp.where(destinations == row_index, lengths, 0), axis=1)
    step = jnp.repeat(jnp.arange(steps, dtype=jnp.int32), requests)
    new_target = jnp.tile(jnp.arange(requests, dtype=jnp.int32), steps)
    new_position = jnp.tile(received, steps) + step
    spare = jnp.zeros((padded - requests * steps,), jnp.int32)
    target = jnp.concatenate([token_target, new_target, spare - 1])
    seen_from = jnp.concatenate([jnp.zeros_like(token_target), step, spare])
    query_info = jnp.stack([new_target, step], 1)
    return token_position, new_position, jnp.stack([target, seen_from], 0), query_info


def rotate(first, second, cosine, sine):
    return [first * cosine - second * sine, second * cosine + first * sine]


def finish_kernel(chunks, group, *refs):
    held, homed, refs = refs[:chunks], refs[chunks : 2 * chunks], refs[2 * chunks :]
    angle_ref, keys_ref, rows_ref, new_ref, query_ref, out_ref = refs
    cosine, sine = angle_ref[:, :HALF], angle_ref[:, HALF:]
    allowed = (keys_ref[0:1, :] == rows_ref[:, 0:1]) & (keys_ref[1:2, :] <= rows_ref[:, 1:2])
    allowed = jnp.concatenate([allowed.astype(jnp.float32)] * group, 0) > 0.5
    queries = query_ref[...].astype(jnp.float32)
    count = queries.shape[0]
    width = held[0].shape[1]
    heads = width // (2 * HD)
    for h in range(chunks * heads):
        c, local = h // heads, h % heads
        key_at = slice(local * HD, (local + 1) * HD)
        value_at = slice((heads + local) * HD, (heads + local + 1) * HD)
        new_at = c * width
        both = held[c][:, key_at] + homed[c][:, key_at]
        keys = jnp.concatenate(rotate(both[:, :HALF], both[:, HALF:], cosine, sine), -1)
        values = held[c][:, value_at] + homed[c][:, value_at]
        keys, values = (
            jnp.concatenate(
                [cached.astype(jnp.bfloat16), new_ref[:, new_at + at.start : new_at + at.stop]], 0
            )
            for cached, at in ((keys, key_at), (values, value_at))
        )
        at = h * group * HD
        query = jnp.concatenate(
            [queries[:, at + g * HD : at + (g + 1) * HD] for g in range(group)], 0
        ).astype(jnp.bfloat16)
        scores = lax.dot_general(
            query, keys, (((1,), (1,)), ((), ())), preferred_element_type=jnp.float32
        )
        scores = jnp.where(allowed, scores * (1.0 / math.sqrt(HD)), jnp.float32(-1e30))
        raised = jnp.exp(scores - jnp.max(scores, axis=-1, keepdims=True))
        total = jnp.sum(raised, axis=-1, keepdims=True)
        weights = (raised / total).astype(jnp.bfloat16)
        output = jnp.dot(weights, values, preferred_element_type=jnp.float32)
        for g in range(group):
            out_ref[:, at + g * HD : at + (g + 1) * HD] = output[
                g * count : (g + 1) * count
            ].astype(jnp.bfloat16)


def finish(held, homed, angles, key_info, query_info, new_pairs, queries):
    rows, width = held[0].shape
    heads = len(held) * width // (2 * HD)
    group = queries.shape[1] // (heads * HD)
    count = queries.shape[0]
    vmem = pl.BlockSpec(memory_space=pltpu.VMEM)
    operands = [*held, *homed, angles, key_info, query_info, new_pairs, queries]
    return pl.pallas_call(
        functools.partial(finish_kernel, len(held), group),
        out_shape=jax.ShapeDtypeStruct(queries.shape, jnp.bfloat16),
        in_specs=[vmem] * len(operands),
        out_specs=vmem,
        compiler_params=pltpu.CompilerParams(vmem_limit_bytes=VMEM_BYTES),
        cost_estimate=pl.CostEstimate(
            flops=4 * heads * group * count * rows * HD,
            bytes_accessed=8 * len(held) * rows * width + 4 * queries.size,
            transcendentals=heads * group * count * rows,
        ),
        name="rotate_attend",
    )(*operands)


def own_kernel(side_ref, weight_ref, *out_refs):
    chunk = out_refs[0].shape[1] // 2
    for kind in range(2):
        columns = weight_ref[:, kind, :]
        for c, out_ref in enumerate(out_refs):
            out_ref[:, kind * chunk : (kind + 1) * chunk] = columns[:, c * chunk : (c + 1) * chunk]


def own_half(weight, side):
    depth, kinds, width = weight.shape
    half = depth // 2
    chunk = kinds * width // CHUNKS
    return pl.pallas_call(
        own_kernel,
        out_shape=[jax.ShapeDtypeStruct((half, chunk), weight.dtype)] * CHUNKS,
        grid_spec=pltpu.PrefetchScalarGridSpec(
            num_scalar_prefetch=1,
            grid=(2,),
            in_specs=[
                pl.BlockSpec((half // 2, kinds, width), lambda i, s: (2 * s[0] + i, 0, 0))
            ],
            out_specs=[pl.BlockSpec((half // 2, chunk), lambda i, s: (i, 0))] * CHUNKS,
        ),
        compiler_params=pltpu.CompilerParams(vmem_limit_bytes=VMEM_BYTES),
        cost_estimate=pl.CostEstimate(
            flops=0, bytes_accessed=8 * half * width * kinds, transcendentals=0
        ),
        name="own_half",
    )(side.reshape(1), weight)


def pack_kernel(chunks, own_ref, *refs):
    owns, (got_ref, angle_ref, query_ref, out_ref) = (own_ref, *refs[: chunks - 1]), refs[chunks - 1 :]
    cosine, sine = angle_ref[:, :HALF], angle_ref[:, HALF:]
    count, base = query_ref.shape
    width = owns[0].shape[1]
    half = width // 2
    out_ref[:, :base] = query_ref[...]
    for c in range(chunks):
        for h in range(half // HD):
            at = h * HD
            both = owns[c][:, at : at + HD] + got_ref[:count, c * width + at : c * width + at + HD]
            both = jnp.concatenate(rotate(both[:, :HALF], both[:, HALF:], cosine, sine), -1)
            at += base + c * width
            out_ref[:, at : at + HD] = both.astype(jnp.bfloat16)
        values = owns[c][:, half:] + got_ref[:count, c * width + half : (c + 1) * width]
        at = base + c * width + half
        out_ref[:, at : at + half] = values.astype(jnp.bfloat16)


def pack(owns, got, angles, queries):
    vmem = pl.BlockSpec(memory_space=pltpu.VMEM)
    width = queries.shape[1] + got.shape[1]
    return pl.pallas_call(
        functools.partial(pack_kernel, len(owns)),
        out_shape=jax.ShapeDtypeStruct((queries.shape[0], width), jnp.bfloat16),
        in_specs=[vmem] * (len(owns) + 3),
        out_specs=vmem,
        compiler_params=pltpu.CompilerParams(vmem_limit_bytes=VMEM_BYTES),
        cost_estimate=pl.CostEstimate(
            flops=0, bytes_accessed=4 * queries.size + 10 * got.size, transcendentals=0
        ),
        name="pack_new",
    )(*owns, got, angles, queries)


def pick_kernel(first, side_ref, source_ref, out_ref):
    out_ref[...] = source_ref[first : first + out_ref.shape[0], :]


def pick_columns(source, side, half, first, end):
    rows, blocks = source.shape[0], source.shape[1] // (2 * half)
    return pl.pallas_call(
        functools.partial(pick_kernel, first),
        out_shape=jax.ShapeDtypeStruct((end - first, blocks * half), source.dtype),
        grid_spec=pltpu.PrefetchScalarGridSpec(
            num_scalar_prefetch=1,
            grid=(blocks,),
            in_specs=[pl.BlockSpec((rows, half), lambda j, s: (0, 2 * j + s[0]))],
            out_specs=pl.BlockSpec((end - first, half), lambda j, s: (0, j)),
        ),
        compiler_params=pltpu.CompilerParams(vmem_limit_bytes=VMEM_BYTES),
        cost_estimate=pl.CostEstimate(
            flops=0, bytes_accessed=4 * (end - first) * blocks * half, transcendentals=0
        ),
        name="pick_columns",
    )(side.reshape(1), source)


def product_kernel(depths, parts, base, has_total, *refs):
    place_ref, refs = refs[0], refs[1:]
    hidden, refs = refs[: 2 * parts], refs[2 * parts :]
    weights, out_ref = refs[: sum(len(pieces) for pieces in depths)], refs[-1]
    half = sum(depths[0])
    blocks = hidden[0].shape[1] // half

    total, used = refs[-2][...] if has_total else None, 0
    for p, pieces in enumerate(depths):
        place = place_ref[base + p]
        here = place < blocks
        columns = pl.ds(pl.multiple_of(jnp.where(here, place, place - blocks) * half, half), half)
        rows = [
            jnp.where(here, hidden[2 * q][:, columns], hidden[2 * q + 1][:, columns])
            for q in range(parts)
        ]
        rows = rows[0] if parts == 1 else jnp.concatenate(rows, 0)
        piece = [w[...] for w in weights[used : used + len(pieces)]]
        piece = piece[0] if len(piece) == 1 else jnp.concatenate(piece, 0)
        used += len(pieces)
        term = jnp.dot(rows, piece, preferred_element_type=jnp.float32)
        total = term if total is None else total + term
    out_ref[...] = total


def products(total, hidden, weights, places, base):
    shards = len(weights)
    flat = [w for shard in weights for w in shard]
    depths = tuple(tuple(w.shape[0] for w in shard) for shard in weights)
    half, width = sum(depths[0]), flat[0].shape[1]
    rows = sum(pair[0].shape[0] for pair in hidden)
    operands = [places] + [array for pair in hidden for array in pair] + flat
    if total is not None:
        operands.append(total)
    vmem = pl.BlockSpec(memory_space=pltpu.VMEM)
    return pl.pallas_call(
        functools.partial(
            product_kernel, depths, len(hidden), base, total is not None
        ),
        out_shape=jax.ShapeDtypeStruct((rows, width), jnp.float32),
        in_specs=[pl.BlockSpec(memory_space=pltpu.SMEM)] + [vmem] * (len(operands) - 1),
        out_specs=vmem,
        compiler_params=pltpu.CompilerParams(vmem_limit_bytes=VMEM_BYTES),
        cost_estimate=pl.CostEstimate(
            flops=2 * rows * half * width * shards,
            bytes_accessed=shards * 2 * half * (rows + width) + 4 * rows * width,
            transcendentals=0,
        ),
        name="products",
    )(*operands)


def ring_order(row_count):
    evens = list(range(0, row_count, 2))
    odds = list(range(1, row_count, 2))
    return evens + odds[::-1]


def fence(*values):
    return lax.optimization_barrier(values)


def body(passages, kv_weight, new_hidden, queries, lengths, destinations):
    tokens = passages.shape[0]
    requests, steps, half_model = new_hidden.shape
    row_count = lax.axis_size("rows")
    group_count = lax.axis_size("groups")
    row_index = lax.axis_index("rows")
    side = lax.axis_index("groups") % 2
    core = lax.axis_index("tensor")
    depth = kv_weight.shape[0]
    half = depth // 2
    local_heads = kv_weight.shape[2] // HD
    group = queries.shape[2] // kv_weight.shape[2]
    count = requests * steps
    new_padded = -(-count // 16) * 16
    half_rows = row_count // 2

    partners = [(g, g ^ 1) for g in range(group_count)]
    cores = [(0, 1), (1, 0)]
    order = ring_order(row_count)
    onward = [(order[i], order[(i + 1) % row_count]) for i in range(row_count)]
    back = [(b, a) for a, b in onward]
    place = {row: i for i, row in enumerate(order)}
    shard_order = [
        [order[(place[r] + d) % row_count] for r in range(row_count)]
        for k in range(half_rows + 1)
        for d in ([0] if k == 0 else [-k, k] if k < half_rows else [k])
    ]
    owners = lax.dynamic_index_in_dim(jnp.array(shard_order, jnp.int32), row_index, 1, keepdims=False)
    places = ((owners // half_rows) ^ core) * half_rows + owners % half_rows

    own = own_half(kv_weight, side)

    ring, ends = [[(piece, piece)] for piece in own], [None, None]

    def halved(pair):
        return pair[0][: half // 2], pair[1][half // 2 :]

    def step(c):
        pair = ring[c][-1]
        if len(ring[c]) == half_rows:
            pair = ends[c]
        ring[c].append((lax.ppermute(pair[0], "rows", onward), lax.ppermute(pair[1], "rows", back)))

    def fence_with(c, *others):
        ring[c][-1], others = fence(ring[c][-1], others)
        return others

    def project(c, hidden, total, begin, end):
        weights = [(own[c],)] + [(w,) for pair in ring[c][1:half_rows] for w in pair]
        weights += ring[c][half_rows:]
        for at in range(begin, end, MOST_SHARDS):
            some = weights[at : min(at + MOST_SHARDS, end)]
            total = products(total, hidden, some, places, at)
        return total

    def homeward(total):
        tokens_total = (total[:tokens] * RAISE).astype(jnp.float16)
        return tokens_total, total[tokens + new_padded :], total[tokens : tokens + count]

    cuts = (0, 3 * tokens // 20, 23 * tokens // 40, tokens)
    sent = [pick_columns(passages, 1 - side, half, cuts[0], cuts[1])]
    (passages_later, new_hidden) = fence_with(0, passages, new_hidden)
    got = [lax.ppermute(sent[0], "groups", partners)]
    step(0)
    passages = passages_later
    sent += [pick_columns(passages, 1 - side, half, *cuts[i : i + 2]) for i in (1, 2)]
    kept = pick_columns(passages, side, half, 0, tokens)
    new_rows = jnp.swapaxes(new_hidden, 0, 1).reshape(count, half_model)
    new_rows = jnp.pad(new_rows, ((0, new_padded - count), (0, 0)))
    new_sent = pick_columns(new_rows, 1 - side, half, 0, new_padded)
    new_kept = pick_columns(new_rows, side, half, 0, new_padded)
    got[0], sent, kept, new_sent, new_kept, lengths, destinations = fence_with(
        0, got[0], sent, kept, new_sent, new_kept, lengths, destinations
    )

    got.append(lax.ppermute(sent[1], "groups", partners))
    step(0)
    kept_other = lax.ppermute(kept, "tensor", cores)
    got_other = [lax.ppermute(got[0], "tensor", cores)]
    kept_other, got_other = fence_with(1, kept_other, got_other)
    step(1)
    position, new_position, key_info, query_info = token_tables(
        lengths, destinations, row_index, tokens, requests, steps, new_padded
    )
    angles, new_angles = angle_table(position), angle_table(new_position)
    tables = (angles, new_angles, key_info, query_info)
    own_hidden = [(kept, kept_other)]
    first, early = 5, row_count - 3
    held = [project(0, own_hidden, None, 0, first)]
    got[1], tables, places, held, ring[1][-1] = fence_with(
        0, got[1], tables, places, held, ring[1][-1]
    )

    got.append(lax.ppermute(sent[2], "groups", partners))
    step(0)
    got_other.append(lax.ppermute(got[1], "tensor", cores))
    (got_other[1],) = fence_with(1, got_other[1])
    step(1)
    for k in range(3, half_rows - 1):
        (ring[1][-1],) = fence_with(0, ring[1][-1])
        step(0)
        step(1)
    held[0] = project(0, own_hidden, held[0], first, row_count - 1)
    held.append(project(1, own_hidden, None, 0, early - 2))
    ends[0] = halved(ring[0][-1])
    got[2], new_sent, held, places, ring[1][-1], ends[0] = fence_with(
        0, got[2], new_sent, held, places, ring[1][-1], ends[0]
    )

    step(0)
    got_other.append(lax.ppermute(got[2], "tensor", cores))
    new_kept = jnp.concatenate([new_kept, lax.ppermute(new_sent, "groups", partners)], 0)
    new_other = lax.ppermute(new_kept, "tensor", cores)
    (got_other[2],) = fence_with(1, got_other[2])
    step(1)
    away_hidden = list(zip(got, got_other)) + [(new_kept, new_other)]
    away = project(0, away_hidden, None, 0, row_count)
    away, places, held = fence(homeward(away), places, held)
    (places,) = fence_with(1, places)
    ends[1] = halved(ring[1][-1])
    step(1)
    homed = [lax.ppermute(away[0], "groups", partners)]
    new_own, new_away = [away[2]], [away[1]]
    away = project(1, away_hidden, None, 0, row_count - 1)
    away = homeward(project(1, away_hidden, away, row_count - 1, row_count))
    new_own.append(away[2])
    new_away.append(away[1])
    new_back = lax.ppermute(jnp.concatenate(new_away, 1), "groups", partners)
    held[0] = project(0, own_hidden, held[0], row_count - 1, row_count)
    held[1] = project(1, own_hidden, held[1], early - 2, early)
    queries = jnp.swapaxes(queries, 0, 1).reshape(count, -1)
    held, queries, places, away, new_back, homed[0] = fence(
        held, queries, places, away, new_back, homed[0]
    )
    homed.append(lax.ppermute(away[0], "groups", partners))
    angles, new_angles, key_info, query_info = tables
    moved = pack(new_own, new_back, new_angles, queries)
    moved, places = fence(moved, places)
    held[1] = project(1, own_hidden, held[1], early, row_count)
    moved = moved.reshape(steps, requests, -1)
    moved = jnp.swapaxes(moved, 0, 1)
    moved = lax.all_to_all(moved, "rows", split_axis=0, concat_axis=0, tiled=True)
    moved = jnp.swapaxes(moved, 0, 1).reshape(count, -1)
    heads_width = queries.shape[1]
    query_rows, new_pairs = moved[:, :heads_width], moved[:, heads_width:]
    new_pairs = jnp.pad(new_pairs, ((0, new_padded - count), (0, 0)))
    homed = [total.astype(jnp.float32) * (1.0 / RAISE) for total in homed]
    attended = finish(held, homed, angles, key_info, query_info, new_pairs, query_rows)
    attended = jnp.swapaxes(attended.reshape(steps, requests, -1), 0, 1)
    return lax.all_to_all(attended, "rows", split_axis=0, concat_axis=0, tiled=True)


def solution(mesh):
    placed = (
        P(("groups", "rows"), "tensor"),
        P("rows", None, "tensor"),
        P(("groups", "rows"), None, "tensor"),
        P(("groups", "rows"), None, "tensor"),
        P("groups", None),
        P("groups", None),
    )
    return jax.shard_map(
        body,
        mesh=mesh,
        in_specs=placed,
        out_specs=P(("groups", "rows"), None, "tensor"),
        check_vma=False,
    )
```

```python
import functools
import math

import jax
import jax.numpy as jnp
from jax import lax
from jax.experimental import pallas as pl
from jax.experimental.pallas import tpu as pltpu
from jax.sharding import PartitionSpec as P

HD = 128
HALF = HD // 2
CHUNKS = 2
MOST_SHARDS = 8
VMEM_BYTES = 20 << 20
FIRST_VMEM_BYTES = 60 << 20
MERGED = 4
RAISE = 16.0


def angle_table(positions):
    index_float = jnp.arange(HALF, dtype=jnp.float32)
    inverse = jnp.exp(index_float * (-2.0 * math.log(1000000.0) / HD))
    angles = positions.astype(jnp.float32)[:, None] * inverse
    return jnp.concatenate([jnp.cos(angles), jnp.sin(angles)], 1)


def token_tables(lengths, destinations, row_index, tokens, requests, steps, padded):
    my_lengths = lax.dynamic_index_in_dim(lengths, row_index, 0, keepdims=False)
    my_targets = lax.dynamic_index_in_dim(destinations, row_index, 0, keepdims=False)
    ends = jnp.cumsum(my_lengths)
    starts = ends - my_lengths
    token = jnp.arange(tokens, dtype=jnp.int32)[:, None]
    inside = (starts[None, :] <= token) & (token < ends[None, :])
    token_position = token[:, 0] - jnp.sum(jnp.where(inside, starts[None, :], 0), axis=1)
    token_target = jnp.sum(jnp.where(inside, my_targets[None, :], 0), axis=1)
    received = jnp.sum(jnp.where(destinations == row_index, lengths, 0), axis=1)
    step = jnp.repeat(jnp.arange(steps, dtype=jnp.int32), requests)
    new_target = jnp.tile(jnp.arange(requests, dtype=jnp.int32), steps)
    new_position = jnp.tile(received, steps) + step
    spare = jnp.zeros((padded - requests * steps,), jnp.int32)
    target = jnp.concatenate([token_target, new_target, spare - 1])
    seen_from = jnp.concatenate([jnp.zeros_like(token_target), step, spare])
    query_info = jnp.stack([new_target, step], 1)
    return token_position, new_position, jnp.stack([target, seen_from], 0), query_info


def rotate(first, second, cosine, sine):
    return [first * cosine - second * sine, second * cosine + first * sine]


def finish_kernel(chunks, group, *refs):
    held, homed, refs = refs[:chunks], refs[chunks : 2 * chunks], refs[2 * chunks :]
    angle_ref, keys_ref, rows_ref, new_ref, query_ref, out_ref = refs
    cosine, sine = angle_ref[:, :HALF], angle_ref[:, HALF:]
    allowed = (keys_ref[0:1, :] == rows_ref[:, 0:1]) & (keys_ref[1:2, :] <= rows_ref[:, 1:2])
    allowed = jnp.concatenate([allowed.astype(jnp.float32)] * group, 0) > 0.5
    queries = query_ref[...].astype(jnp.float32)
    count = queries.shape[0]
    width = held[0].shape[1]
    heads = width // (2 * HD)
    for h in range(chunks * heads):
        c, local = h // heads, h % heads
        key_at = slice(local * HD, (local + 1) * HD)
        value_at = slice((heads + local) * HD, (heads + local + 1) * HD)
        new_at = c * width
        both = held[c][:, key_at] + homed[c][:, key_at]
        keys = jnp.concatenate(rotate(both[:, :HALF], both[:, HALF:], cosine, sine), -1)
        values = held[c][:, value_at] + homed[c][:, value_at]
        keys, values = (
            jnp.concatenate(
                [cached.astype(jnp.bfloat16), new_ref[:, new_at + at.start : new_at + at.stop]], 0
            )
            for cached, at in ((keys, key_at), (values, value_at))
        )
        at = h * group * HD
        query = jnp.concatenate(
            [queries[:, at + g * HD : at + (g + 1) * HD] for g in range(group)], 0
        ).astype(jnp.bfloat16)
        scores = lax.dot_general(
            query, keys, (((1,), (1,)), ((), ())), preferred_element_type=jnp.float32
        )
        scores = jnp.where(allowed, scores * (1.0 / math.sqrt(HD)), jnp.float32(-1e30))
        raised = jnp.exp(scores - jnp.max(scores, axis=-1, keepdims=True))
        total = jnp.sum(raised, axis=-1, keepdims=True)
        weights = (raised / total).astype(jnp.bfloat16)
        output = jnp.dot(weights, values, preferred_element_type=jnp.float32)
        for g in range(group):
            out_ref[:, at + g * HD : at + (g + 1) * HD] = output[
                g * count : (g + 1) * count
            ].astype(jnp.bfloat16)


def finish(held, homed, angles, key_info, query_info, new_pairs, queries):
    rows, width = held[0].shape
    heads = len(held) * width // (2 * HD)
    group = queries.shape[1] // (heads * HD)
    count = queries.shape[0]
    vmem = pl.BlockSpec(memory_space=pltpu.VMEM)
    operands = [*held, *homed, angles, key_info, query_info, new_pairs, queries]
    return pl.pallas_call(
        functools.partial(finish_kernel, len(held), group),
        out_shape=jax.ShapeDtypeStruct(queries.shape, jnp.bfloat16),
        in_specs=[vmem] * len(operands),
        out_specs=vmem,
        compiler_params=pltpu.CompilerParams(vmem_limit_bytes=VMEM_BYTES),
        cost_estimate=pl.CostEstimate(
            flops=4 * heads * group * count * rows * HD,
            bytes_accessed=8 * len(held) * rows * width + 4 * queries.size,
            transcendentals=heads * group * count * rows,
        ),
        name="rotate_attend",
    )(*operands)


def own_kernel(side_ref, weight_ref, *out_refs):
    chunk = out_refs[0].shape[1] // 2
    for kind in range(2):
        columns = weight_ref[:, kind, :]
        for c, out_ref in enumerate(out_refs):
            out_ref[:, kind * chunk : (kind + 1) * chunk] = columns[:, c * chunk : (c + 1) * chunk]


def own_half(weight, side):
    depth, kinds, width = weight.shape
    half = depth // 2
    chunk = kinds * width // CHUNKS
    return pl.pallas_call(
        own_kernel,
        out_shape=[jax.ShapeDtypeStruct((half, chunk), weight.dtype)] * CHUNKS,
        grid_spec=pltpu.PrefetchScalarGridSpec(
            num_scalar_prefetch=1,
            grid=(2,),
            in_specs=[
                pl.BlockSpec((half // 2, kinds, width), lambda i, s: (2 * s[0] + i, 0, 0))
            ],
            out_specs=[pl.BlockSpec((half // 2, chunk), lambda i, s: (i, 0))] * CHUNKS,
        ),
        compiler_params=pltpu.CompilerParams(vmem_limit_bytes=FIRST_VMEM_BYTES),
        cost_estimate=pl.CostEstimate(
            flops=0, bytes_accessed=8 * half * width * kinds, transcendentals=0
        ),
        name="own_half",
    )(side.reshape(1), weight)


def pack_kernel(chunks, own_ref, *refs):
    owns, (got_ref, angle_ref, query_ref, out_ref) = (own_ref, *refs[: chunks - 1]), refs[chunks - 1 :]
    cosine, sine = angle_ref[:, :HALF], angle_ref[:, HALF:]
    count, base = query_ref.shape
    width = owns[0].shape[1]
    half = width // 2
    out_ref[:, :base] = query_ref[...]
    for c in range(chunks):
        for h in range(half // HD):
            at = h * HD
            both = owns[c][:, at : at + HD] + got_ref[:count, c * width + at : c * width + at + HD]
            both = jnp.concatenate(rotate(both[:, :HALF], both[:, HALF:], cosine, sine), -1)
            at += base + c * width
            out_ref[:, at : at + HD] = both.astype(jnp.bfloat16)
        values = owns[c][:, half:] + got_ref[:count, c * width + half : (c + 1) * width]
        at = base + c * width + half
        out_ref[:, at : at + half] = values.astype(jnp.bfloat16)


def pack(owns, got, angles, queries):
    vmem = pl.BlockSpec(memory_space=pltpu.VMEM)
    width = queries.shape[1] + got.shape[1]
    return pl.pallas_call(
        functools.partial(pack_kernel, len(owns)),
        out_shape=jax.ShapeDtypeStruct((queries.shape[0], width), jnp.bfloat16),
        in_specs=[vmem] * (len(owns) + 3),
        out_specs=vmem,
        compiler_params=pltpu.CompilerParams(vmem_limit_bytes=VMEM_BYTES),
        cost_estimate=pl.CostEstimate(
            flops=0, bytes_accessed=4 * queries.size + 10 * got.size, transcendentals=0
        ),
        name="pack_new",
    )(*owns, got, angles, queries)


def pick_kernel(first, side_ref, source_ref, out_ref):
    out_ref[...] = source_ref[first : first + out_ref.shape[0], :]


def pick_columns(source, side, half, first, end, vmem_bytes=VMEM_BYTES):
    rows, blocks = source.shape[0] if first else end, source.shape[1] // (2 * half)
    return pl.pallas_call(
        functools.partial(pick_kernel, first),
        out_shape=jax.ShapeDtypeStruct((end - first, blocks * half), source.dtype),
        grid_spec=pltpu.PrefetchScalarGridSpec(
            num_scalar_prefetch=1,
            grid=(blocks,),
            in_specs=[pl.BlockSpec((rows, half), lambda j, s: (0, 2 * j + s[0]))],
            out_specs=pl.BlockSpec((end - first, half), lambda j, s: (0, j)),
        ),
        compiler_params=pltpu.CompilerParams(vmem_limit_bytes=vmem_bytes),
        cost_estimate=pl.CostEstimate(
            flops=0, bytes_accessed=4 * (end - first) * blocks * half, transcendentals=0
        ),
        name="pick_columns",
    )(side.reshape(1), source)


def product_kernel(depths, parts, base, has_total, *refs):
    place_ref, refs = refs[0], refs[1:]
    hidden, refs = refs[: 2 * parts], refs[2 * parts :]
    weights, out_ref = refs[: sum(len(pieces) for pieces in depths)], refs[-1]
    half = sum(depths[0])
    blocks = hidden[0].shape[1] // half

    total, used = refs[-2][...] if has_total else None, 0
    for p, pieces in enumerate(depths):
        place = place_ref[base + p]
        here = place < blocks
        columns = pl.ds(pl.multiple_of(jnp.where(here, place, place - blocks) * half, half), half)
        rows = [
            jnp.where(here, hidden[2 * q][:, columns], hidden[2 * q + 1][:, columns])
            for q in range(parts)
        ]
        rows = rows[0] if parts == 1 else jnp.concatenate(rows, 0)
        piece = [w[...] for w in weights[used : used + len(pieces)]]
        piece = piece[0] if len(piece) == 1 else jnp.concatenate(piece, 0)
        used += len(pieces)
        term = jnp.dot(rows, piece, preferred_element_type=jnp.float32)
        total = term if total is None else total + term
    out_ref[...] = total


def products(total, hidden, weights, places, base):
    shards = len(weights)
    flat = [w for shard in weights for w in shard]
    depths = tuple(tuple(w.shape[0] for w in shard) for shard in weights)
    half, width = sum(depths[0]), flat[0].shape[1]
    rows = sum(pair[0].shape[0] for pair in hidden)
    operands = [places] + [array for pair in hidden for array in pair] + flat
    if total is not None:
        operands.append(total)
    vmem = pl.BlockSpec(memory_space=pltpu.VMEM)
    return pl.pallas_call(
        functools.partial(
            product_kernel, depths, len(hidden), base, total is not None
        ),
        out_shape=jax.ShapeDtypeStruct((rows, width), jnp.float32),
        in_specs=[pl.BlockSpec(memory_space=pltpu.SMEM)] + [vmem] * (len(operands) - 1),
        out_specs=vmem,
        compiler_params=pltpu.CompilerParams(vmem_limit_bytes=VMEM_BYTES),
        cost_estimate=pl.CostEstimate(
            flops=2 * rows * half * width * shards,
            bytes_accessed=shards * 2 * half * (rows + width) + 4 * rows * width,
            transcendentals=0,
        ),
        name="products",
    )(*operands)


def ring_order(row_count):
    evens = list(range(0, row_count, 2))
    odds = list(range(1, row_count, 2))
    return evens + odds[::-1]


def fence(*values):
    return lax.optimization_barrier(values)


def body(passages, kv_weight, new_hidden, queries, lengths, destinations):
    tokens = passages.shape[0]
    requests, steps, half_model = new_hidden.shape
    row_count = lax.axis_size("rows")
    group_count = lax.axis_size("groups")
    row_index = lax.axis_index("rows")
    side = lax.axis_index("groups") % 2
    core = lax.axis_index("tensor")
    depth = kv_weight.shape[0]
    half = depth // 2
    local_heads = kv_weight.shape[2] // HD
    group = queries.shape[2] // kv_weight.shape[2]
    count = requests * steps
    new_padded = -(-count // 16) * 16
    half_rows = row_count // 2

    partners = [(g, g ^ 1) for g in range(group_count)]
    cores = [(0, 1), (1, 0)]
    order = ring_order(row_count)
    onward = [(order[i], order[(i + 1) % row_count]) for i in range(row_count)]
    back = [(b, a) for a, b in onward]
    place = {row: i for i, row in enumerate(order)}
    shard_order = [
        [order[(place[r] + d) % row_count] for r in range(row_count)]
        for k in range(half_rows + 1)
        for d in ([0] if k == 0 else [-k, k] if k < half_rows else [k])
    ]
    owners = lax.dynamic_index_in_dim(jnp.array(shard_order, jnp.int32), row_index, 1, keepdims=False)
    places = ((owners // half_rows) ^ core) * half_rows + owners % half_rows

    cuts = (0, tokens // 4, tokens // 8 * 5, tokens)
    sent = [pick_columns(passages, 1 - side, half, cuts[0], cuts[1], FIRST_VMEM_BYTES)]
    kv_weight, sent[0], passages = fence(kv_weight, sent[0], passages)
    got = [lax.ppermute(sent[0], "groups", partners)]
    own = own_half(kv_weight, side)

    ring, ends = [[(piece, piece)] for piece in own], [None, None]

    def halved(pair):
        return pair[0][: half // 2], pair[1][half // 2 :]

    def step(c):
        pair = ring[c][-1]
        if len(ring[c]) == half_rows:
            pair = ends[c]
        ring[c].append((lax.ppermute(pair[0], "rows", onward), lax.ppermute(pair[1], "rows", back)))

    def fence_with(c, *others):
        ring[c][-1], others = fence(ring[c][-1], others)
        return others

    def project(c, hidden, total, begin, end):
        weights = [(own[c],)] + [(w,) for pair in ring[c][1:half_rows] for w in pair]
        weights += ring[c][half_rows:]
        for at in range(begin, end, MOST_SHARDS):
            some = weights[at : min(at + MOST_SHARDS, end)]
            total = products(total, hidden, some, places, at)
        return total

    def homeward(total):
        tokens_total = (total[:tokens] * RAISE).astype(jnp.float16)
        return tokens_total, total[tokens + new_padded :], total[tokens : tokens + count]

    passages, new_hidden = fence_with(0, passages, new_hidden)
    step(0)
    sent += [pick_columns(passages, 1 - side, half, *cuts[i : i + 2]) for i in (1, 2)]
    kept = pick_columns(passages, side, half, 0, tokens)
    new_rows = jnp.swapaxes(new_hidden, 0, 1).reshape(count, half_model)
    new_rows = jnp.pad(new_rows, ((0, new_padded - count), (0, 0)))
    new_sent = pick_columns(new_rows, 1 - side, half, 0, new_padded)
    new_kept = pick_columns(new_rows, side, half, 0, new_padded)
    new_got = lax.ppermute(new_sent, "groups", partners)
    got[0], sent, kept, new_got, new_kept, lengths, destinations = fence_with(
        0, got[0], sent, kept, new_got, new_kept, lengths, destinations
    )
    new_kept = jnp.concatenate([new_kept, new_got], 0)

    got.append(lax.ppermute(sent[1], "groups", partners))
    step(0)
    kept_other = lax.ppermute(kept, "tensor", cores)
    got_other = [lax.ppermute(got[0], "tensor", cores)]
    kept_other, got_other = fence_with(1, kept_other, got_other)
    step(1)
    position, new_position, key_info, query_info = token_tables(
        lengths, destinations, row_index, tokens, requests, steps, new_padded
    )
    angles, new_angles = angle_table(position), angle_table(new_position)
    tables = (angles, new_angles, key_info, query_info)
    own_hidden = [(kept, kept_other)]
    first, early = 5, row_count - 3
    held = [project(0, own_hidden, None, 0, first)]
    got[1], tables, places, held, ring[1][-1] = fence_with(
        0, got[1], tables, places, held, ring[1][-1]
    )

    got.append(lax.ppermute(sent[2], "groups", partners))
    step(0)
    got_other.append(lax.ppermute(got[1], "tensor", cores))
    (got_other[1],) = fence_with(1, got_other[1])
    step(1)
    for k in range(3, half_rows - 1):
        (ring[1][-1],) = fence_with(0, ring[1][-1])
        step(0)
        step(1)
    held[0] = project(0, own_hidden, held[0], first, early)
    ends[0] = halved(ring[0][-1])
    got[2], new_kept, held, places, ring[1][-1], ends[0] = fence_with(
        0, got[2], new_kept, held, places, ring[1][-1], ends[0]
    )

    step(0)
    got_other.append(lax.ppermute(got[2], "tensor", cores))
    new_other = lax.ppermute(new_kept, "tensor", cores)
    (got_other[2],) = fence_with(1, got_other[2])
    step(1)
    away_hidden = list(zip(got, got_other)) + [(new_kept, new_other)]
    held.append(project(1, own_hidden, None, 0, early))
    places, held = fence(places, held)
    away = project(0, away_hidden, None, 0, row_count)
    away, places = fence(homeward(away), places)
    (places,) = fence_with(1, places)
    ends[1] = halved(ring[1][-1])
    step(1)
    homed = [lax.ppermute(away[0], "groups", partners)]
    new_own, new_away = [away[2]], [away[1]]
    away = project(1, away_hidden, None, 0, row_count - 1)
    away = homeward(project(1, away_hidden, away, row_count - 1, row_count))
    new_own.append(away[2])
    new_away.append(away[1])
    new_back = lax.ppermute(jnp.concatenate(new_away, 1), "groups", partners)
    held[0] = project(0, own_hidden, held[0], early, row_count)
    queries = jnp.swapaxes(queries, 0, 1).reshape(count, -1)
    held, queries, places, away, new_back, homed[0] = fence(
        held, queries, places, away, new_back, homed[0]
    )
    homed.append(lax.ppermute(away[0], "groups", partners))
    angles, new_angles, key_info, query_info = tables
    moved = pack(new_own, new_back, new_angles, queries)
    moved, places = fence(moved, places)
    held[1] = project(1, own_hidden, held[1], early, row_count)
    moved = moved.reshape(steps, requests, -1)
    moved = jnp.swapaxes(moved, 0, 1)
    moved = lax.all_to_all(moved, "rows", split_axis=0, concat_axis=0, tiled=True)
    moved = jnp.swapaxes(moved, 0, 1).reshape(count, -1)
    heads_width = queries.shape[1]
    query_rows, new_pairs = moved[:, :heads_width], moved[:, heads_width:]
    new_pairs = jnp.pad(new_pairs, ((0, new_padded - count), (0, 0)))
    homed = [total.astype(jnp.float32) * (1.0 / RAISE) for total in homed]
    attended = finish(held, homed, angles, key_info, query_info, new_pairs, query_rows)
    attended = jnp.swapaxes(attended.reshape(steps, requests, -1), 0, 1)
    return lax.all_to_all(attended, "rows", split_axis=0, concat_axis=0, tiled=True)


def solution(mesh):
    placed = (
        P(("groups", "rows"), "tensor"),
        P("rows", None, "tensor"),
        P(("groups", "rows"), None, "tensor"),
        P(("groups", "rows"), None, "tensor"),
        P("groups", None),
        P("groups", None),
    )
    return jax.shard_map(
        body,
        mesh=mesh,
        in_specs=placed,
        out_specs=P(("groups", "rows"), None, "tensor"),
        check_vma=False,
    )
```

```python
import functools
import math

import jax
import jax.numpy as jnp
from jax import lax
from jax.experimental import pallas as pl
from jax.experimental.pallas import tpu as pltpu
from jax.sharding import PartitionSpec as P

HD = 128
HALF = HD // 2
CHUNKS = 2
MOST_SHARDS = 8
VMEM_BYTES = 20 << 20
MERGED = 4
RAISE = 16.0


def angle_table(positions):
    index_float = jnp.arange(HALF, dtype=jnp.float32)
    inverse = jnp.exp(index_float * (-2.0 * math.log(1000000.0) / HD))
    angles = positions.astype(jnp.float32)[:, None] * inverse
    return jnp.concatenate([jnp.cos(angles), jnp.sin(angles)], 1)


def token_tables(lengths, destinations, row_index, tokens, requests, steps, padded):
    my_lengths = lax.dynamic_index_in_dim(lengths, row_index, 0, keepdims=False)
    my_targets = lax.dynamic_index_in_dim(destinations, row_index, 0, keepdims=False)
    ends = jnp.cumsum(my_lengths)
    starts = ends - my_lengths
    token = jnp.arange(tokens, dtype=jnp.int32)[:, None]
    inside = (starts[None, :] <= token) & (token < ends[None, :])
    token_position = token[:, 0] - jnp.sum(jnp.where(inside, starts[None, :], 0), axis=1)
    token_target = jnp.sum(jnp.where(inside, my_targets[None, :], 0), axis=1)
    received = jnp.sum(jnp.where(destinations == row_index, lengths, 0), axis=1)
    step = jnp.repeat(jnp.arange(steps, dtype=jnp.int32), requests)
    new_target = jnp.tile(jnp.arange(requests, dtype=jnp.int32), steps)
    new_position = jnp.tile(received, steps) + step
    spare = jnp.zeros((padded - requests * steps,), jnp.int32)
    target = jnp.concatenate([token_target, new_target, spare - 1])
    seen_from = jnp.concatenate([jnp.zeros_like(token_target), step, spare])
    query_info = jnp.stack([new_target, step], 1)
    return token_position, new_position, jnp.stack([target, seen_from], 0), query_info


def rotate(first, second, cosine, sine):
    return [first * cosine - second * sine, second * cosine + first * sine]


def finish_kernel(chunks, group, *refs):
    held, homed, refs = refs[:chunks], refs[chunks : 2 * chunks], refs[2 * chunks :]
    angle_ref, keys_ref, rows_ref, new_ref, query_ref, out_ref = refs
    cosine, sine = angle_ref[:, :HALF], angle_ref[:, HALF:]
    allowed = (keys_ref[0:1, :] == rows_ref[:, 0:1]) & (keys_ref[1:2, :] <= rows_ref[:, 1:2])
    allowed = jnp.concatenate([allowed.astype(jnp.float32)] * group, 0) > 0.5
    queries = query_ref[...].astype(jnp.float32)
    count = queries.shape[0]
    width = held[0].shape[1]
    heads = width // (2 * HD)
    for h in range(chunks * heads):
        c, local = h // heads, h % heads
        key_at = slice(local * HD, (local + 1) * HD)
        value_at = slice((heads + local) * HD, (heads + local + 1) * HD)
        new_at = c * width
        both = held[c][:, key_at] + homed[c][:, key_at]
        keys = jnp.concatenate(rotate(both[:, :HALF], both[:, HALF:], cosine, sine), -1)
        values = held[c][:, value_at] + homed[c][:, value_at]
        keys, values = (
            jnp.concatenate(
                [cached.astype(jnp.bfloat16), new_ref[:, new_at + at.start : new_at + at.stop]], 0
            )
            for cached, at in ((keys, key_at), (values, value_at))
        )
        at = h * group * HD
        query = jnp.concatenate(
            [queries[:, at + g * HD : at + (g + 1) * HD] for g in range(group)], 0
        ).astype(jnp.bfloat16)
        scores = lax.dot_general(
            query, keys, (((1,), (1,)), ((), ())), preferred_element_type=jnp.float32
        )
        scores = jnp.where(allowed, scores * (1.0 / math.sqrt(HD)), jnp.float32(-1e30))
        raised = jnp.exp(scores - jnp.max(scores, axis=-1, keepdims=True))
        total = jnp.sum(raised, axis=-1, keepdims=True)
        weights = (raised / total).astype(jnp.bfloat16)
        output = jnp.dot(weights, values, preferred_element_type=jnp.float32)
        for g in range(group):
            out_ref[:, at + g * HD : at + (g + 1) * HD] = output[
                g * count : (g + 1) * count
            ].astype(jnp.bfloat16)


def finish(held, homed, angles, key_info, query_info, new_pairs, queries):
    rows, width = held[0].shape
    heads = len(held) * width // (2 * HD)
    group = queries.shape[1] // (heads * HD)
    count = queries.shape[0]
    vmem = pl.BlockSpec(memory_space=pltpu.VMEM)
    operands = [*held, *homed, angles, key_info, query_info, new_pairs, queries]
    return pl.pallas_call(
        functools.partial(finish_kernel, len(held), group),
        out_shape=jax.ShapeDtypeStruct(queries.shape, jnp.bfloat16),
        in_specs=[vmem] * len(operands),
        out_specs=vmem,
        compiler_params=pltpu.CompilerParams(vmem_limit_bytes=VMEM_BYTES),
        cost_estimate=pl.CostEstimate(
            flops=4 * heads * group * count * rows * HD,
            bytes_accessed=8 * len(held) * rows * width + 4 * queries.size,
            transcendentals=heads * group * count * rows,
        ),
        name="rotate_attend",
    )(*operands)


def own_kernel(side_ref, weight_ref, *out_refs):
    chunk = out_refs[0].shape[1] // 2
    for kind in range(2):
        columns = weight_ref[:, kind, :]
        for c, out_ref in enumerate(out_refs):
            out_ref[:, kind * chunk : (kind + 1) * chunk] = columns[:, c * chunk : (c + 1) * chunk]


def own_half(weight, side):
    depth, kinds, width = weight.shape
    half = depth // 2
    chunk = kinds * width // CHUNKS
    return pl.pallas_call(
        own_kernel,
        out_shape=[jax.ShapeDtypeStruct((half, chunk), weight.dtype)] * CHUNKS,
        grid_spec=pltpu.PrefetchScalarGridSpec(
            num_scalar_prefetch=1,
            grid=(2,),
            in_specs=[
                pl.BlockSpec((half // 2, kinds, width), lambda i, s: (2 * s[0] + i, 0, 0))
            ],
            out_specs=[pl.BlockSpec((half // 2, chunk), lambda i, s: (i, 0))] * CHUNKS,
        ),
        compiler_params=pltpu.CompilerParams(vmem_limit_bytes=VMEM_BYTES),
        cost_estimate=pl.CostEstimate(
            flops=0, bytes_accessed=8 * half * width * kinds, transcendentals=0
        ),
        name="own_half",
    )(side.reshape(1), weight)


def pack_kernel(chunks, own_ref, *refs):
    owns, (got_ref, angle_ref, query_ref, out_ref) = (own_ref, *refs[: chunks - 1]), refs[chunks - 1 :]
    cosine, sine = angle_ref[:, :HALF], angle_ref[:, HALF:]
    count, base = query_ref.shape
    width = owns[0].shape[1]
    half = width // 2
    out_ref[:, :base] = query_ref[...]
    for c in range(chunks):
        for h in range(half // HD):
            at = h * HD
            both = owns[c][:, at : at + HD] + got_ref[:count, c * width + at : c * width + at + HD]
            both = jnp.concatenate(rotate(both[:, :HALF], both[:, HALF:], cosine, sine), -1)
            at += base + c * width
            out_ref[:, at : at + HD] = both.astype(jnp.bfloat16)
        values = owns[c][:, half:] + got_ref[:count, c * width + half : (c + 1) * width]
        at = base + c * width + half
        out_ref[:, at : at + half] = values.astype(jnp.bfloat16)


def pack(owns, got, angles, queries):
    vmem = pl.BlockSpec(memory_space=pltpu.VMEM)
    width = queries.shape[1] + got.shape[1]
    return pl.pallas_call(
        functools.partial(pack_kernel, len(owns)),
        out_shape=jax.ShapeDtypeStruct((queries.shape[0], width), jnp.bfloat16),
        in_specs=[vmem] * (len(owns) + 3),
        out_specs=vmem,
        compiler_params=pltpu.CompilerParams(vmem_limit_bytes=VMEM_BYTES),
        cost_estimate=pl.CostEstimate(
            flops=0, bytes_accessed=4 * queries.size + 10 * got.size, transcendentals=0
        ),
        name="pack_new",
    )(*owns, got, angles, queries)


def pick_kernel(first, side_ref, source_ref, out_ref):
    out_ref[...] = source_ref[first : first + out_ref.shape[0], :]


def pick_columns(source, side, half, first, end):
    rows, blocks = source.shape[0], source.shape[1] // (2 * half)
    return pl.pallas_call(
        functools.partial(pick_kernel, first),
        out_shape=jax.ShapeDtypeStruct((end - first, blocks * half), source.dtype),
        grid_spec=pltpu.PrefetchScalarGridSpec(
            num_scalar_prefetch=1,
            grid=(blocks,),
            in_specs=[pl.BlockSpec((rows, half), lambda j, s: (0, 2 * j + s[0]))],
            out_specs=pl.BlockSpec((end - first, half), lambda j, s: (0, j)),
        ),
        compiler_params=pltpu.CompilerParams(vmem_limit_bytes=VMEM_BYTES),
        cost_estimate=pl.CostEstimate(
            flops=0, bytes_accessed=4 * (end - first) * blocks * half, transcendentals=0
        ),
        name="pick_columns",
    )(side.reshape(1), source)


def product_kernel(depths, parts, base, has_total, outs, *refs):
    place_ref, refs = refs[0], refs[1:]
    hidden, refs = refs[: 2 * parts], refs[2 * parts :]
    refs, out_refs = refs[:-outs], refs[-outs:]
    weights = refs[: sum(len(pieces) for pieces in depths)]
    half = sum(depths[0])
    blocks = hidden[0].shape[1] // half

    total, used = refs[-1][...] if has_total else None, 0
    for p, pieces in enumerate(depths):
        place = place_ref[base + p]
        here = place < blocks
        columns = pl.ds(pl.multiple_of(jnp.where(here, place, place - blocks) * half, half), half)
        rows = [
            jnp.where(here, hidden[2 * q][:, columns], hidden[2 * q + 1][:, columns])
            for q in range(parts)
        ]
        rows = rows[0] if parts == 1 else jnp.concatenate(rows, 0)
        piece = [w[...] for w in weights[used : used + len(pieces)]]
        piece = piece[0] if len(piece) == 1 else jnp.concatenate(piece, 0)
        used += len(pieces)
        term = jnp.dot(rows, piece, preferred_element_type=jnp.float32)
        total = term if total is None else total + term
    at = 0
    for out_ref in out_refs:
        out_ref[...] = total[at : at + out_ref.shape[0], :]
        at += out_ref.shape[0]


def products(total, hidden, weights, places, base, cut=None):
    shards = len(weights)
    flat = [w for shard in weights for w in shard]
    depths = tuple(tuple(w.shape[0] for w in shard) for shard in weights)
    half, width = sum(depths[0]), flat[0].shape[1]
    rows = sum(pair[0].shape[0] for pair in hidden)
    operands = [places] + [array for pair in hidden for array in pair] + flat
    if total is not None:
        operands.append(total)
    vmem = pl.BlockSpec(memory_space=pltpu.VMEM)
    return pl.pallas_call(
        functools.partial(
            product_kernel, depths, len(hidden), base, total is not None, 2 if cut else 1
        ),
        out_shape=jax.ShapeDtypeStruct((rows, width), jnp.float32)
        if cut is None
        else [jax.ShapeDtypeStruct((n, width), jnp.float32) for n in (cut, rows - cut)],
        in_specs=[pl.BlockSpec(memory_space=pltpu.SMEM)] + [vmem] * (len(operands) - 1),
        out_specs=vmem if cut is None else [vmem, vmem],
        compiler_params=pltpu.CompilerParams(vmem_limit_bytes=VMEM_BYTES),
        cost_estimate=pl.CostEstimate(
            flops=2 * rows * half * width * shards,
            bytes_accessed=shards * 2 * half * (rows + width) + 4 * rows * width,
            transcendentals=0,
        ),
        name="products",
    )(*operands)


def ring_order(row_count):
    evens = list(range(0, row_count, 2))
    odds = list(range(1, row_count, 2))
    return evens + odds[::-1]


def fence(*values):
    return lax.optimization_barrier(values)


def body(passages, kv_weight, new_hidden, queries, lengths, destinations):
    tokens = passages.shape[0]
    requests, steps, half_model = new_hidden.shape
    row_count = lax.axis_size("rows")
    group_count = lax.axis_size("groups")
    row_index = lax.axis_index("rows")
    side = lax.axis_index("groups") % 2
    core = lax.axis_index("tensor")
    depth = kv_weight.shape[0]
    half = depth // 2
    local_heads = kv_weight.shape[2] // HD
    group = queries.shape[2] // kv_weight.shape[2]
    count = requests * steps
    new_padded = -(-count // 16) * 16
    half_rows = row_count // 2

    partners = [(g, g ^ 1) for g in range(group_count)]
    cores = [(0, 1), (1, 0)]
    order = ring_order(row_count)
    onward = [(order[i], order[(i + 1) % row_count]) for i in range(row_count)]
    back = [(b, a) for a, b in onward]
    place = {row: i for i, row in enumerate(order)}
    shard_order = [
        [order[(place[r] + d) % row_count] for r in range(row_count)]
        for k in range(half_rows + 1)
        for d in ([0] if k == 0 else [-k, k] if k < half_rows else [k])
    ]
    owners = lax.dynamic_index_in_dim(jnp.array(shard_order, jnp.int32), row_index, 1, keepdims=False)
    places = ((owners // half_rows) ^ core) * half_rows + owners % half_rows

    own = own_half(kv_weight, side)

    ring, ends = [[(piece, piece)] for piece in own], [None, None]

    def halved(pair):
        return pair[0][: half // 2], pair[1][half // 2 :]

    def step(c):
        pair = ring[c][-1]
        if len(ring[c]) == half_rows:
            pair = ends[c]
        ring[c].append((lax.ppermute(pair[0], "rows", onward), lax.ppermute(pair[1], "rows", back)))

    def fence_with(c, *others):
        ring[c][-1], others = fence(ring[c][-1], others)
        return others

    def project(c, hidden, total, begin, end, cut=None):
        weights = [(own[c],)] + [(w,) for pair in ring[c][1:half_rows] for w in pair]
        weights += ring[c][half_rows:]
        for at in range(begin, end, MOST_SHARDS):
            some = weights[at : min(at + MOST_SHARDS, end)]
            total = products(total, hidden, some, places, at, cut if at + len(some) == end else None)
        return total

    def homeward(total):
        total, new = total
        return (total * RAISE).astype(jnp.float16), new[new_padded:], new[:count]

    cuts = (0, 3 * tokens // 20, 23 * tokens // 40, tokens)
    sent = [pick_columns(passages[: cuts[1]], 1 - side, half, cuts[0], cuts[1])]
    (passages_later, new_hidden) = fence_with(0, passages, new_hidden)
    got = [lax.ppermute(sent[0], "groups", partners)]
    step(0)
    passages = passages_later
    sent += [pick_columns(passages, 1 - side, half, *cuts[i : i + 2]) for i in (1, 2)]
    kept = pick_columns(passages, side, half, 0, tokens)
    new_rows = jnp.swapaxes(new_hidden, 0, 1).reshape(count, half_model)
    new_rows = jnp.pad(new_rows, ((0, new_padded - count), (0, 0)))
    new_sent = pick_columns(new_rows, 1 - side, half, 0, new_padded)
    new_kept = pick_columns(new_rows, side, half, 0, new_padded)
    got[0], sent, kept, new_sent, new_kept, lengths, destinations = fence_with(
        0, got[0], sent, kept, new_sent, new_kept, lengths, destinations
    )

    got.append(lax.ppermute(sent[1], "groups", partners))
    step(0)
    kept_other = lax.ppermute(kept, "tensor", cores)
    got_other = [lax.ppermute(got[0], "tensor", cores)]
    kept_other, got_other = fence_with(1, kept_other, got_other)
    step(1)
    position, new_position, key_info, query_info = token_tables(
        lengths, destinations, row_index, tokens, requests, steps, new_padded
    )
    angles, new_angles = angle_table(position), angle_table(new_position)
    tables = (angles, new_angles, key_info, query_info)
    got[1], tables, places, ring[1][-1] = fence_with(0, got[1], tables, places, ring[1][-1])

    own_hidden = [(kept, kept_other)]
    early = row_count - 3
    got.append(lax.ppermute(sent[2], "groups", partners))
    step(0)
    got_other.append(lax.ppermute(got[1], "tensor", cores))
    (got_other[1],) = fence_with(1, got_other[1])
    step(1)
    for k in range(3, half_rows - 1):
        (ring[1][-1],) = fence_with(0, ring[1][-1])
        step(0)
        step(1)
    held = [project(0, own_hidden, None, 0, early), project(1, own_hidden, None, 0, early - 2)]
    ends[0] = halved(ring[0][-1])
    got[2], new_sent, held, places, ring[1][-1], ends[0] = fence_with(
        0, got[2], new_sent, held, places, ring[1][-1], ends[0]
    )

    step(0)
    got_other.append(lax.ppermute(got[2], "tensor", cores))
    new_kept = jnp.concatenate([new_kept, lax.ppermute(new_sent, "groups", partners)], 0)
    new_other = lax.ppermute(new_kept, "tensor", cores)
    (got_other[2],) = fence_with(1, got_other[2])
    step(1)
    away_hidden = list(zip(got, got_other)) + [(new_kept, new_other)]
    away = project(0, away_hidden, None, 0, row_count, tokens)
    away, places, held = fence(homeward(away), places, held)
    (places,) = fence_with(1, places)
    ends[1] = halved(ring[1][-1])
    step(1)
    homed = [lax.ppermute(away[0], "groups", partners)]
    new_own, new_away = [away[2]], [away[1]]
    away = project(1, away_hidden, None, 0, row_count - 1)
    away = homeward(project(1, away_hidden, away, row_count - 1, row_count, tokens))
    new_own.append(away[2])
    new_away.append(away[1])
    new_back = lax.ppermute(jnp.concatenate(new_away, 1), "groups", partners)
    held[0] = project(0, own_hidden, held[0], early, row_count)
    queries = jnp.swapaxes(queries, 0, 1).reshape(count, -1)
    held, queries, places, away, new_back, homed[0] = fence(
        held, queries, places, away, new_back, homed[0]
    )
    homed.append(lax.ppermute(away[0], "groups", partners))
    angles, new_angles, key_info, query_info = tables
    moved = pack(new_own, new_back, new_angles, queries)
    moved, places = fence(moved, places)
    held[1] = project(1, own_hidden, held[1], early - 2, row_count)
    moved = moved.reshape(steps, requests, -1)
    moved = jnp.swapaxes(moved, 0, 1)
    moved = lax.all_to_all(moved, "rows", split_axis=0, concat_axis=0, tiled=True)
    moved = jnp.swapaxes(moved, 0, 1).reshape(count, -1)
    heads_width = queries.shape[1]
    query_rows, new_pairs = moved[:, :heads_width], moved[:, heads_width:]
    new_pairs = jnp.pad(new_pairs, ((0, new_padded - count), (0, 0)))
    homed = [total.astype(jnp.float32) * (1.0 / RAISE) for total in homed]
    attended = finish(held, homed, angles, key_info, query_info, new_pairs, query_rows)
    attended = jnp.swapaxes(attended.reshape(steps, requests, -1), 0, 1)
    return lax.all_to_all(attended, "rows", split_axis=0, concat_axis=0, tiled=True)


def solution(mesh):
    placed = (
        P(("groups", "rows"), "tensor"),
        P("rows", None, "tensor"),
        P(("groups", "rows"), None, "tensor"),
        P(("groups", "rows"), None, "tensor"),
        P("groups", None),
        P("groups", None),
    )
    return jax.shard_map(
        body,
        mesh=mesh,
        in_specs=placed,
        out_specs=P(("groups", "rows"), None, "tensor"),
        check_vma=False,
    )
```

```python
import functools
import math

import jax
import jax.numpy as jnp
import numpy as np
from jax import lax
from jax.experimental import pallas as pl
from jax.experimental.pallas import tpu as pltpu
from jax.sharding import PartitionSpec as P

HD = 128
HALF = HD // 2
CHUNKS = 2
MOST_SHARDS = 8
VMEM_BYTES = 20 << 20
MERGED = 4
RAISE = 16.0


def angle_table(positions):
    index_float = jnp.arange(HALF, dtype=jnp.float32)
    inverse = jnp.exp(index_float * (-2.0 * math.log(1000000.0) / HD))
    angles = positions.astype(jnp.float32)[:, None] * inverse
    return jnp.concatenate([jnp.cos(angles), jnp.sin(angles)], 1)


def token_tables(lengths, destinations, row_index, tokens, requests, steps, padded):
    my_lengths = lax.dynamic_index_in_dim(lengths, row_index, 0, keepdims=False)
    my_targets = lax.dynamic_index_in_dim(destinations, row_index, 0, keepdims=False)
    ends = jnp.cumsum(my_lengths)
    starts = ends - my_lengths
    token = jnp.arange(tokens, dtype=jnp.int32)[:, None]
    inside = (starts[None, :] <= token) & (token < ends[None, :])
    token_position = token[:, 0] - jnp.sum(jnp.where(inside, starts[None, :], 0), axis=1)
    token_target = jnp.sum(jnp.where(inside, my_targets[None, :], 0), axis=1)
    received = jnp.sum(jnp.where(destinations == row_index, lengths, 0), axis=1)
    step = np.repeat(np.arange(steps, dtype=np.int32), requests)
    new_target = np.tile(np.arange(requests, dtype=np.int32), steps)
    new_position = jnp.tile(received, steps) + step
    spare = np.zeros((padded - requests * steps,), np.int32)
    target = jnp.concatenate([token_target, np.concatenate([new_target, spare - 1])])
    seen_from = jnp.asarray(np.concatenate([np.zeros((tokens,), np.int32), step, spare]))
    query_info = jnp.asarray(np.stack([new_target, step], 1))
    return token_position, new_position, jnp.stack([target, seen_from], 0), query_info


def rotate(first, second, cosine, sine):
    return [first * cosine - second * sine, second * cosine + first * sine]


def finish_kernel(chunks, group, *refs):
    held, homed, refs = refs[:chunks], refs[chunks : 2 * chunks], refs[2 * chunks :]
    angle_ref, keys_ref, rows_ref, new_ref, query_ref, out_ref = refs
    cosine, sine = angle_ref[:, :HALF], angle_ref[:, HALF:]
    allowed = (keys_ref[0:1, :] == rows_ref[:, 0:1]) & (keys_ref[1:2, :] <= rows_ref[:, 1:2])
    allowed = jnp.concatenate([allowed.astype(jnp.float32)] * group, 0) > 0.5
    queries = query_ref[...].astype(jnp.float32)
    count = queries.shape[0]
    width = held[0].shape[1]
    heads = width // (2 * HD)
    for h in range(chunks * heads):
        c, local = h // heads, h % heads
        key_at = slice(local * HD, (local + 1) * HD)
        value_at = slice((heads + local) * HD, (heads + local + 1) * HD)
        new_at = c * width
        both = held[c][:, key_at] + homed[c][:, key_at]
        keys = jnp.concatenate(rotate(both[:, :HALF], both[:, HALF:], cosine, sine), -1)
        values = held[c][:, value_at] + homed[c][:, value_at]
        keys, values = (
            jnp.concatenate(
                [cached.astype(jnp.bfloat16), new_ref[:, new_at + at.start : new_at + at.stop]], 0
            )
            for cached, at in ((keys, key_at), (values, value_at))
        )
        at = h * group * HD
        query = jnp.concatenate(
            [queries[:, at + g * HD : at + (g + 1) * HD] for g in range(group)], 0
        ).astype(jnp.bfloat16)
        scores = lax.dot_general(
            query, keys, (((1,), (1,)), ((), ())), preferred_element_type=jnp.float32
        )
        scores = jnp.where(allowed, scores * (1.0 / math.sqrt(HD)), jnp.float32(-1e30))
        raised = jnp.exp(scores - jnp.max(scores, axis=-1, keepdims=True))
        total = jnp.sum(raised, axis=-1, keepdims=True)
        weights = (raised / total).astype(jnp.bfloat16)
        output = jnp.dot(weights, values, preferred_element_type=jnp.float32)
        for g in range(group):
            out_ref[:, at + g * HD : at + (g + 1) * HD] = output[
                g * count : (g + 1) * count
            ].astype(jnp.bfloat16)


def finish(held, homed, angles, key_info, query_info, new_pairs, queries):
    rows, width = held[0].shape
    heads = len(held) * width // (2 * HD)
    group = queries.shape[1] // (heads * HD)
    count = queries.shape[0]
    vmem = pl.BlockSpec(memory_space=pltpu.VMEM)
    operands = [*held, *homed, angles, key_info, query_info, new_pairs, queries]
    return pl.pallas_call(
        functools.partial(finish_kernel, len(held), group),
        out_shape=jax.ShapeDtypeStruct(queries.shape, jnp.bfloat16),
        in_specs=[vmem] * len(operands),
        out_specs=vmem,
        compiler_params=pltpu.CompilerParams(vmem_limit_bytes=VMEM_BYTES),
        cost_estimate=pl.CostEstimate(
            flops=4 * heads * group * count * rows * HD,
            bytes_accessed=8 * len(held) * rows * width + 4 * queries.size,
            transcendentals=heads * group * count * rows,
        ),
        name="rotate_attend",
    )(*operands)


def own_kernel(side_ref, weight_ref, out_ref):
    chunk = weight_ref.shape[2]
    for kind in range(2):
        out_ref[:, kind * chunk : (kind + 1) * chunk] = weight_ref[:, kind, :]


def own_half(weight, side, c):
    depth, kinds, width = weight.shape
    half, chunk = depth // 2, width // CHUNKS
    return pl.pallas_call(
        own_kernel,
        out_shape=jax.ShapeDtypeStruct((half, kinds * chunk), weight.dtype),
        grid_spec=pltpu.PrefetchScalarGridSpec(
            num_scalar_prefetch=1,
            grid=(2,),
            in_specs=[
                pl.BlockSpec((half // 2, kinds, chunk), lambda i, s: (2 * s[0] + i, 0, c))
            ],
            out_specs=pl.BlockSpec((half // 2, kinds * chunk), lambda i, s: (i, 0)),
        ),
        compiler_params=pltpu.CompilerParams(vmem_limit_bytes=VMEM_BYTES),
        cost_estimate=pl.CostEstimate(
            flops=0, bytes_accessed=8 * half * chunk * kinds, transcendentals=0
        ),
        name="own_half",
    )(side.reshape(1), weight)


def pack_kernel(chunks, own_ref, *refs):
    owns, (got_ref, angle_ref, query_ref, out_ref) = (own_ref, *refs[: chunks - 1]), refs[chunks - 1 :]
    cosine, sine = angle_ref[:, :HALF], angle_ref[:, HALF:]
    count, base = query_ref.shape
    width = owns[0].shape[1]
    half = width // 2
    out_ref[:, :base] = query_ref[...]
    for c in range(chunks):
        for h in range(half // HD):
            at = h * HD
            both = owns[c][:, at : at + HD] + got_ref[:count, c * width + at : c * width + at + HD]
            both = jnp.concatenate(rotate(both[:, :HALF], both[:, HALF:], cosine, sine), -1)
            at += base + c * width
            out_ref[:, at : at + HD] = both.astype(jnp.bfloat16)
        values = owns[c][:, half:] + got_ref[:count, c * width + half : (c + 1) * width]
        at = base + c * width + half
        out_ref[:, at : at + half] = values.astype(jnp.bfloat16)


def pack(owns, got, angles, queries):
    vmem = pl.BlockSpec(memory_space=pltpu.VMEM)
    width = queries.shape[1] + got.shape[1]
    return pl.pallas_call(
        functools.partial(pack_kernel, len(owns)),
        out_shape=jax.ShapeDtypeStruct((queries.shape[0], width), jnp.bfloat16),
        in_specs=[vmem] * (len(owns) + 3),
        out_specs=vmem,
        compiler_params=pltpu.CompilerParams(vmem_limit_bytes=VMEM_BYTES),
        cost_estimate=pl.CostEstimate(
            flops=0, bytes_accessed=4 * queries.size + 10 * got.size, transcendentals=0
        ),
        name="pack_new",
    )(*owns, got, angles, queries)


def pick_kernel(first, side_ref, source_ref, out_ref):
    out_ref[...] = source_ref[first : first + out_ref.shape[0], :]


def pick_columns(source, side, half, first, end):
    rows, blocks = source.shape[0], source.shape[1] // (2 * half)
    return pl.pallas_call(
        functools.partial(pick_kernel, first),
        out_shape=jax.ShapeDtypeStruct((end - first, blocks * half), source.dtype),
        grid_spec=pltpu.PrefetchScalarGridSpec(
            num_scalar_prefetch=1,
            grid=(blocks,),
            in_specs=[pl.BlockSpec((rows, half), lambda j, s: (0, 2 * j + s[0]))],
            out_specs=pl.BlockSpec((end - first, half), lambda j, s: (0, j)),
        ),
        compiler_params=pltpu.CompilerParams(vmem_limit_bytes=VMEM_BYTES),
        cost_estimate=pl.CostEstimate(
            flops=0, bytes_accessed=4 * (end - first) * blocks * half, transcendentals=0
        ),
        name="pick_columns",
    )(side.reshape(1), source)


def product_kernel(depths, parts, base, has_total, *refs):
    place_ref, refs = refs[0], refs[1:]
    hidden, refs = refs[: 2 * parts], refs[2 * parts :]
    weights, out_ref = refs[: sum(len(pieces) for pieces in depths)], refs[-1]
    half = sum(depths[0])
    blocks = hidden[0].shape[1] // half

    total, used = refs[-2][...] if has_total else None, 0
    for p, pieces in enumerate(depths):
        place = place_ref[base + p]
        here = place < blocks
        columns = pl.ds(pl.multiple_of(jnp.where(here, place, place - blocks) * half, half), half)
        rows = [
            jnp.where(here, hidden[2 * q][:, columns], hidden[2 * q + 1][:, columns])
            for q in range(parts)
        ]
        rows = rows[0] if parts == 1 else jnp.concatenate(rows, 0)
        piece = [w[...] for w in weights[used : used + len(pieces)]]
        piece = piece[0] if len(piece) == 1 else jnp.concatenate(piece, 0)
        used += len(pieces)
        term = jnp.dot(rows, piece, preferred_element_type=jnp.float32)
        total = term if total is None else total + term
    out_ref[...] = total


def products(total, hidden, weights, places, base):
    shards = len(weights)
    flat = [w for shard in weights for w in shard]
    depths = tuple(tuple(w.shape[0] for w in shard) for shard in weights)
    half, width = sum(depths[0]), flat[0].shape[1]
    rows = sum(pair[0].shape[0] for pair in hidden)
    operands = [places] + [array for pair in hidden for array in pair] + flat
    if total is not None:
        operands.append(total)
    vmem = pl.BlockSpec(memory_space=pltpu.VMEM)
    return pl.pallas_call(
        functools.partial(
            product_kernel, depths, len(hidden), base, total is not None
        ),
        out_shape=jax.ShapeDtypeStruct((rows, width), jnp.float32),
        in_specs=[pl.BlockSpec(memory_space=pltpu.SMEM)] + [vmem] * (len(operands) - 1),
        out_specs=vmem,
        compiler_params=pltpu.CompilerParams(vmem_limit_bytes=VMEM_BYTES),
        cost_estimate=pl.CostEstimate(
            flops=2 * rows * half * width * shards,
            bytes_accessed=shards * 2 * half * (rows + width) + 4 * rows * width,
            transcendentals=0,
        ),
        name="products",
    )(*operands)


def ring_order(row_count):
    evens = list(range(0, row_count, 2))
    odds = list(range(1, row_count, 2))
    return evens + odds[::-1]


def fence(*values):
    return lax.optimization_barrier(values)


def body(passages, kv_weight, new_hidden, queries, lengths, destinations):
    tokens = passages.shape[0]
    requests, steps, half_model = new_hidden.shape
    row_count = lax.axis_size("rows")
    group_count = lax.axis_size("groups")
    row_index = lax.axis_index("rows")
    side = lax.axis_index("groups") % 2
    core = lax.axis_index("tensor")
    depth = kv_weight.shape[0]
    half = depth // 2
    local_heads = kv_weight.shape[2] // HD
    group = queries.shape[2] // kv_weight.shape[2]
    count = requests * steps
    new_padded = -(-count // 16) * 16
    half_rows = row_count // 2

    partners = [(g, g ^ 1) for g in range(group_count)]
    cores = [(0, 1), (1, 0)]
    order = ring_order(row_count)
    onward = [(order[i], order[(i + 1) % row_count]) for i in range(row_count)]
    back = [(b, a) for a, b in onward]
    place = {row: i for i, row in enumerate(order)}
    shard_order = [
        [order[(place[r] + d) % row_count] for r in range(row_count)]
        for k in range(half_rows + 1)
        for d in ([0] if k == 0 else [-k, k] if k < half_rows else [k])
    ]
    owners = lax.dynamic_index_in_dim(jnp.array(shard_order, jnp.int32), row_index, 1, keepdims=False)
    places = ((owners // half_rows) ^ core) * half_rows + owners % half_rows

    own = [own_half(kv_weight, side, 0)]

    ring, ends = [[(own[0], own[0])]], [None, None]

    def halved(pair):
        return pair[0][: half // 2], pair[1][half // 2 :]

    def step(c):
        pair = ring[c][-1]
        if len(ring[c]) == half_rows:
            pair = ends[c]
        ring[c].append((lax.ppermute(pair[0], "rows", onward), lax.ppermute(pair[1], "rows", back)))

    def fence_with(c, *others):
        ring[c][-1], others = fence(ring[c][-1], others)
        return others

    def project(c, hidden, total, begin, end):
        weights = [(own[c],)] + [(w,) for pair in ring[c][1:half_rows] for w in pair]
        weights += ring[c][half_rows:]
        for at in range(begin, end, MOST_SHARDS):
            some = weights[at : min(at + MOST_SHARDS, end)]
            total = products(total, hidden, some, places, at)
        return total

    def homeward(total):
        tokens_total = (total[:tokens] * RAISE).astype(jnp.float16)
        return tokens_total, total[tokens + new_padded :], total[tokens : tokens + count]

    cuts = (0, 3 * tokens // 20, 23 * tokens // 40, tokens)
    sent = [pick_columns(passages, 1 - side, half, cuts[0], cuts[1])]
    passages_later, new_hidden, weight_later = fence_with(0, passages, new_hidden, kv_weight)
    got = [lax.ppermute(sent[0], "groups", partners)]
    step(0)
    passages = passages_later
    own.append(own_half(weight_later, side, 1))
    ring.append([(own[1], own[1])])
    sent += [pick_columns(passages, 1 - side, half, *cuts[i : i + 2]) for i in (1, 2)]
    kept = pick_columns(passages, side, half, 0, tokens)
    new_rows = jnp.swapaxes(new_hidden, 0, 1).reshape(count, half_model)
    new_rows = jnp.pad(new_rows, ((0, new_padded - count), (0, 0)))
    new_sent = pick_columns(new_rows, 1 - side, half, 0, new_padded)
    new_kept = pick_columns(new_rows, side, half, 0, new_padded)
    got[0], sent, kept, new_sent, new_kept, ring[1][0] = fence_with(
        0, got[0], sent, kept, new_sent, new_kept, ring[1][0]
    )

    got.append(lax.ppermute(sent[1], "groups", partners))
    step(0)
    kept_other = lax.ppermute(kept, "tensor", cores)
    got_other = [lax.ppermute(got[0], "tensor", cores)]
    kept_other, got_other, lengths, destinations = fence_with(
        1, kept_other, got_other, lengths, destinations
    )
    step(1)
    position, new_position, key_info, query_info = token_tables(
        lengths, destinations, row_index, tokens, requests, steps, new_padded
    )
    angles, new_angles = angle_table(position), angle_table(new_position)
    tables = (angles, new_angles, key_info, query_info)
    got[1], tables, places, ring[1][-1] = fence_with(0, got[1], tables, places, ring[1][-1])

    own_hidden = [(kept, kept_other)]
    early = row_count - 3
    got.append(lax.ppermute(sent[2], "groups", partners))
    step(0)
    got_other.append(lax.ppermute(got[1], "tensor", cores))
    (got_other[1],) = fence_with(1, got_other[1])
    step(1)
    for k in range(3, half_rows - 1):
        (ring[1][-1],) = fence_with(0, ring[1][-1])
        step(0)
        step(1)
    held = [project(0, own_hidden, None, 0, early)]
    ends[0] = halved(ring[0][-1])
    got[2], new_sent, held, places, ring[1][-1], ends[0] = fence_with(
        0, got[2], new_sent, held, places, ring[1][-1], ends[0]
    )

    step(0)
    got_other.append(lax.ppermute(got[2], "tensor", cores))
    new_kept = jnp.concatenate([new_kept, lax.ppermute(new_sent, "groups", partners)], 0)
    new_other = lax.ppermute(new_kept, "tensor", cores)
    (got_other[2],) = fence_with(1, got_other[2])
    step(1)
    away_hidden = list(zip(got, got_other)) + [(new_kept, new_other)]
    held.append(project(1, own_hidden, None, 0, early))
    places, held = fence(places, held)
    away = project(0, away_hidden, None, 0, row_count)
    away, places = fence(homeward(away), places)
    (places,) = fence_with(1, places)
    ends[1] = halved(ring[1][-1])
    step(1)
    homed = [lax.ppermute(away[0], "groups", partners)]
    new_own, new_away = [away[2]], [away[1]]
    away = project(1, away_hidden, None, 0, row_count - 1)
    away = homeward(project(1, away_hidden, away, row_count - 1, row_count))
    new_own.append(away[2])
    new_away.append(away[1])
    new_back = lax.ppermute(jnp.concatenate(new_away, 1), "groups", partners)
    held[0] = project(0, own_hidden, held[0], early, row_count)
    queries = jnp.swapaxes(queries, 0, 1).reshape(count, -1)
    held, queries, places, away, new_back, homed[0] = fence(
        held, queries, places, away, new_back, homed[0]
    )
    homed.append(lax.ppermute(away[0], "groups", partners))
    angles, new_angles, key_info, query_info = tables
    moved = pack(new_own, new_back, new_angles, queries)
    moved, places = fence(moved, places)
    held[1] = project(1, own_hidden, held[1], early, row_count)
    moved = moved.reshape(steps, requests, -1)
    moved = jnp.swapaxes(moved, 0, 1)
    moved = lax.all_to_all(moved, "rows", split_axis=0, concat_axis=0, tiled=True)
    moved = jnp.swapaxes(moved, 0, 1).reshape(count, -1)
    heads_width = queries.shape[1]
    query_rows, new_pairs = moved[:, :heads_width], moved[:, heads_width:]
    new_pairs = jnp.pad(new_pairs, ((0, new_padded - count), (0, 0)))
    homed = [total.astype(jnp.float32) * (1.0 / RAISE) for total in homed]
    attended = finish(held, homed, angles, key_info, query_info, new_pairs, query_rows)
    attended = jnp.swapaxes(attended.reshape(steps, requests, -1), 0, 1)
    return lax.all_to_all(attended, "rows", split_axis=0, concat_axis=0, tiled=True)


def solution(mesh):
    placed = (
        P(("groups", "rows"), "tensor"),
        P("rows", None, "tensor"),
        P(("groups", "rows"), None, "tensor"),
        P(("groups", "rows"), None, "tensor"),
        P("groups", None),
        P("groups", None),
    )
    return jax.shard_map(
        body,
        mesh=mesh,
        in_specs=placed,
        out_specs=P(("groups", "rows"), None, "tensor"),
        check_vma=False,
    )
```

```python
import functools
import math

import jax
import jax.numpy as jnp
import numpy as np
from jax import lax
from jax.experimental import pallas as pl
from jax.experimental.pallas import tpu as pltpu
from jax.sharding import PartitionSpec as P

HD = 128
HALF = HD // 2
CHUNKS = 2
MOST_SHARDS = 8
VMEM_BYTES = 20 << 20
MERGED = 4
RAISE = 16.0


def angle_table(positions):
    index_float = jnp.arange(HALF, dtype=jnp.float32)
    inverse = jnp.exp(index_float * (-2.0 * math.log(1000000.0) / HD))
    angles = positions.astype(jnp.float32)[:, None] * inverse
    return jnp.concatenate([jnp.cos(angles), jnp.sin(angles)], 1)


def token_tables(lengths, destinations, row_index, tokens, requests, steps, padded):
    my_lengths = lax.dynamic_index_in_dim(lengths, row_index, 0, keepdims=False)
    my_targets = lax.dynamic_index_in_dim(destinations, row_index, 0, keepdims=False)
    ends = jnp.cumsum(my_lengths)
    starts = ends - my_lengths
    token = jnp.arange(tokens, dtype=jnp.int32)[:, None]
    inside = (starts[None, :] <= token) & (token < ends[None, :])
    token_position = token[:, 0] - jnp.sum(jnp.where(inside, starts[None, :], 0), axis=1)
    token_target = jnp.sum(jnp.where(inside, my_targets[None, :], 0), axis=1)
    received = jnp.sum(jnp.where(destinations == row_index, lengths, 0), axis=1)
    step = np.repeat(np.arange(steps, dtype=np.int32), requests)
    new_target = np.tile(np.arange(requests, dtype=np.int32), steps)
    new_position = jnp.tile(received, steps) + step
    spare = np.zeros((padded - requests * steps,), np.int32)
    target = jnp.concatenate([token_target, np.concatenate([new_target, spare - 1])])
    seen_from = jnp.asarray(np.concatenate([np.zeros((tokens,), np.int32), step, spare]))
    query_info = jnp.asarray(np.stack([new_target, step], 1))
    return token_position, new_position, jnp.stack([target, seen_from], 0), query_info


def rotate(first, second, cosine, sine):
    return [first * cosine - second * sine, second * cosine + first * sine]


def finish_kernel(c, group, held_ref, homed_ref, angle_ref, keys_ref, rows_ref, new_ref, query_ref, *refs):
    out_ref = refs[-1]
    if c > 0:
        out_ref[:, : refs[0].shape[1]] = refs[0][...]
    cosine, sine = angle_ref[:, :HALF], angle_ref[:, HALF:]
    allowed = (keys_ref[0:1, :] == rows_ref[:, 0:1]) & (keys_ref[1:2, :] <= rows_ref[:, 1:2])
    allowed = jnp.concatenate([allowed.astype(jnp.float32)] * group, 0) > 0.5
    queries = query_ref[...].astype(jnp.float32)
    count = queries.shape[0]
    width = held_ref.shape[1]
    heads = width // (2 * HD)
    for local in range(heads):
        h = c * heads + local
        key_at = slice(local * HD, (local + 1) * HD)
        value_at = slice((heads + local) * HD, (heads + local + 1) * HD)
        new_at = c * width
        both = held_ref[:, key_at] + homed_ref[:, key_at]
        keys = jnp.concatenate(rotate(both[:, :HALF], both[:, HALF:], cosine, sine), -1)
        values = held_ref[:, value_at] + homed_ref[:, value_at]
        keys, values = (
            jnp.concatenate(
                [cached.astype(jnp.bfloat16), new_ref[:, new_at + at.start : new_at + at.stop]], 0
            )
            for cached, at in ((keys, key_at), (values, value_at))
        )
        at = h * group * HD
        query = jnp.concatenate(
            [queries[:, at + g * HD : at + (g + 1) * HD] for g in range(group)], 0
        ).astype(jnp.bfloat16)
        scores = lax.dot_general(
            query, keys, (((1,), (1,)), ((), ())), preferred_element_type=jnp.float32
        )
        scores = jnp.where(allowed, scores * (1.0 / math.sqrt(HD)), jnp.float32(-1e30))
        raised = jnp.exp(scores - jnp.max(scores, axis=-1, keepdims=True))
        total = jnp.sum(raised, axis=-1, keepdims=True)
        weights = (raised / total).astype(jnp.bfloat16)
        output = jnp.dot(weights, values, preferred_element_type=jnp.float32)
        for g in range(group):
            out_ref[:, at + g * HD : at + (g + 1) * HD] = output[
                g * count : (g + 1) * count
            ].astype(jnp.bfloat16)


def finish(c, done, held, homed, angles, key_info, query_info, new_pairs, queries):
    rows, width = held.shape
    heads = width // (2 * HD)
    group = queries.shape[1] // (CHUNKS * heads * HD)
    count = queries.shape[0]
    vmem = pl.BlockSpec(memory_space=pltpu.VMEM)
    operands = [held, homed, angles, key_info, query_info, new_pairs, queries]
    if done is not None:
        operands.append(done)
    return pl.pallas_call(
        functools.partial(finish_kernel, c, group),
        out_shape=jax.ShapeDtypeStruct((count, (c + 1) * heads * group * HD), jnp.bfloat16),
        in_specs=[vmem] * len(operands),
        out_specs=vmem,
        compiler_params=pltpu.CompilerParams(vmem_limit_bytes=VMEM_BYTES),
        cost_estimate=pl.CostEstimate(
            flops=4 * heads * group * count * rows * HD,
            bytes_accessed=8 * rows * width + 4 * queries.size,
            transcendentals=heads * group * count * rows,
        ),
        name="rotate_attend",
    )(*operands)


def own_kernel(side_ref, weight_ref, out_ref):
    chunk = weight_ref.shape[2]
    for kind in range(2):
        out_ref[:, kind * chunk : (kind + 1) * chunk] = weight_ref[:, kind, :]


def own_half(weight, side, c):
    depth, kinds, width = weight.shape
    half, chunk = depth // 2, width // CHUNKS
    return pl.pallas_call(
        own_kernel,
        out_shape=jax.ShapeDtypeStruct((half, kinds * chunk), weight.dtype),
        grid_spec=pltpu.PrefetchScalarGridSpec(
            num_scalar_prefetch=1,
            grid=(2,),
            in_specs=[
                pl.BlockSpec((half // 2, kinds, chunk), lambda i, s: (2 * s[0] + i, 0, c))
            ],
            out_specs=pl.BlockSpec((half // 2, kinds * chunk), lambda i, s: (i, 0)),
        ),
        compiler_params=pltpu.CompilerParams(vmem_limit_bytes=VMEM_BYTES),
        cost_estimate=pl.CostEstimate(
            flops=0, bytes_accessed=8 * half * chunk * kinds, transcendentals=0
        ),
        name="own_half",
    )(side.reshape(1), weight)


def pack_kernel(chunks, own_ref, *refs):
    owns, (got_ref, angle_ref, query_ref, out_ref) = (own_ref, *refs[: chunks - 1]), refs[chunks - 1 :]
    cosine, sine = angle_ref[:, :HALF], angle_ref[:, HALF:]
    count, base = query_ref.shape
    width = owns[0].shape[1]
    half = width // 2
    out_ref[:, :base] = query_ref[...]
    for c in range(chunks):
        for h in range(half // HD):
            at = h * HD
            both = owns[c][:, at : at + HD] + got_ref[:count, c * width + at : c * width + at + HD]
            both = jnp.concatenate(rotate(both[:, :HALF], both[:, HALF:], cosine, sine), -1)
            at += base + c * width
            out_ref[:, at : at + HD] = both.astype(jnp.bfloat16)
        values = owns[c][:, half:] + got_ref[:count, c * width + half : (c + 1) * width]
        at = base + c * width + half
        out_ref[:, at : at + half] = values.astype(jnp.bfloat16)


def pack(owns, got, angles, queries):
    vmem = pl.BlockSpec(memory_space=pltpu.VMEM)
    width = queries.shape[1] + got.shape[1]
    return pl.pallas_call(
        functools.partial(pack_kernel, len(owns)),
        out_shape=jax.ShapeDtypeStruct((queries.shape[0], width), jnp.bfloat16),
        in_specs=[vmem] * (len(owns) + 3),
        out_specs=vmem,
        compiler_params=pltpu.CompilerParams(vmem_limit_bytes=VMEM_BYTES),
        cost_estimate=pl.CostEstimate(
            flops=0, bytes_accessed=4 * queries.size + 10 * got.size, transcendentals=0
        ),
        name="pack_new",
    )(*owns, got, angles, queries)


def pick_kernel(first, side_ref, source_ref, out_ref):
    out_ref[...] = source_ref[first : first + out_ref.shape[0], :]


def pick_columns(source, side, half, first, end):
    rows, blocks = source.shape[0], source.shape[1] // (2 * half)
    return pl.pallas_call(
        functools.partial(pick_kernel, first),
        out_shape=jax.ShapeDtypeStruct((end - first, blocks * half), source.dtype),
        grid_spec=pltpu.PrefetchScalarGridSpec(
            num_scalar_prefetch=1,
            grid=(blocks,),
            in_specs=[pl.BlockSpec((rows, half), lambda j, s: (0, 2 * j + s[0]))],
            out_specs=pl.BlockSpec((end - first, half), lambda j, s: (0, j)),
        ),
        compiler_params=pltpu.CompilerParams(vmem_limit_bytes=VMEM_BYTES),
        cost_estimate=pl.CostEstimate(
            flops=0, bytes_accessed=4 * (end - first) * blocks * half, transcendentals=0
        ),
        name="pick_columns",
    )(side.reshape(1), source)


def product_kernel(depths, parts, base, has_total, *refs):
    place_ref, refs = refs[0], refs[1:]
    hidden, refs = refs[: 2 * parts], refs[2 * parts :]
    weights, out_ref = refs[: sum(len(pieces) for pieces in depths)], refs[-1]
    half = sum(depths[0])
    blocks = hidden[0].shape[1] // half

    total, used = refs[-2][...] if has_total else None, 0
    for p, pieces in enumerate(depths):
        place = place_ref[base + p]
        here = place < blocks
        columns = pl.ds(pl.multiple_of(jnp.where(here, place, place - blocks) * half, half), half)
        rows = [
            jnp.where(here, hidden[2 * q][:, columns], hidden[2 * q + 1][:, columns])
            for q in range(parts)
        ]
        rows = rows[0] if parts == 1 else jnp.concatenate(rows, 0)
        piece = [w[...] for w in weights[used : used + len(pieces)]]
        piece = piece[0] if len(piece) == 1 else jnp.concatenate(piece, 0)
        used += len(pieces)
        term = jnp.dot(rows, piece, preferred_element_type=jnp.float32)
        total = term if total is None else total + term
    out_ref[...] = total


def products(total, hidden, weights, places, base):
    shards = len(weights)
    flat = [w for shard in weights for w in shard]
    depths = tuple(tuple(w.shape[0] for w in shard) for shard in weights)
    half, width = sum(depths[0]), flat[0].shape[1]
    rows = sum(pair[0].shape[0] for pair in hidden)
    operands = [places] + [array for pair in hidden for array in pair] + flat
    if total is not None:
        operands.append(total)
    vmem = pl.BlockSpec(memory_space=pltpu.VMEM)
    return pl.pallas_call(
        functools.partial(
            product_kernel, depths, len(hidden), base, total is not None
        ),
        out_shape=jax.ShapeDtypeStruct((rows, width), jnp.float32),
        in_specs=[pl.BlockSpec(memory_space=pltpu.SMEM)] + [vmem] * (len(operands) - 1),
        out_specs=vmem,
        compiler_params=pltpu.CompilerParams(vmem_limit_bytes=VMEM_BYTES),
        cost_estimate=pl.CostEstimate(
            flops=2 * rows * half * width * shards,
            bytes_accessed=shards * 2 * half * (rows + width) + 4 * rows * width,
            transcendentals=0,
        ),
        name="products",
    )(*operands)


def ring_order(row_count):
    evens = list(range(0, row_count, 2))
    odds = list(range(1, row_count, 2))
    return evens + odds[::-1]


def fence(*values):
    return lax.optimization_barrier(values)


def body(passages, kv_weight, new_hidden, queries, lengths, destinations):
    tokens = passages.shape[0]
    requests, steps, half_model = new_hidden.shape
    row_count = lax.axis_size("rows")
    group_count = lax.axis_size("groups")
    row_index = lax.axis_index("rows")
    side = lax.axis_index("groups") % 2
    core = lax.axis_index("tensor")
    depth = kv_weight.shape[0]
    half = depth // 2
    local_heads = kv_weight.shape[2] // HD
    group = queries.shape[2] // kv_weight.shape[2]
    count = requests * steps
    new_padded = -(-count // 16) * 16
    half_rows = row_count // 2

    partners = [(g, g ^ 1) for g in range(group_count)]
    cores = [(0, 1), (1, 0)]
    order = ring_order(row_count)
    onward = [(order[i], order[(i + 1) % row_count]) for i in range(row_count)]
    back = [(b, a) for a, b in onward]
    place = {row: i for i, row in enumerate(order)}
    shard_order = [
        [order[(place[r] + d) % row_count] for r in range(row_count)]
        for k in range(half_rows + 1)
        for d in ([0] if k == 0 else [-k, k] if k < half_rows else [k])
    ]
    owners = lax.dynamic_index_in_dim(jnp.array(shard_order, jnp.int32), row_index, 1, keepdims=False)
    places = ((owners // half_rows) ^ core) * half_rows + owners % half_rows

    own = [own_half(kv_weight, side, 0)]

    ring, ends = [[(own[0], own[0])]], [None, None]

    def halved(pair):
        return pair[0][: half // 2], pair[1][half // 2 :]

    def step(c):
        pair = ring[c][-1]
        if len(ring[c]) == half_rows:
            pair = ends[c]
        ring[c].append((lax.ppermute(pair[0], "rows", onward), lax.ppermute(pair[1], "rows", back)))

    def fence_with(c, *others):
        ring[c][-1], others = fence(ring[c][-1], others)
        return others

    def project(c, hidden, total, begin, end):
        weights = [(own[c],)] + [(w,) for pair in ring[c][1:half_rows] for w in pair]
        weights += ring[c][half_rows:]
        for at in range(begin, end, MOST_SHARDS):
            some = weights[at : min(at + MOST_SHARDS, end)]
            total = products(total, hidden, some, places, at)
        return total

    def homeward(total):
        tokens_total = (total[:tokens] * RAISE).astype(jnp.float16)
        return tokens_total, total[tokens + new_padded :], total[tokens : tokens + count]

    cuts = (0, 3 * tokens // 20, 23 * tokens // 40, tokens)
    sent = [pick_columns(passages, 1 - side, half, cuts[0], cuts[1])]
    passages_later, new_hidden, weight_later = fence_with(0, passages, new_hidden, kv_weight)
    got = [lax.ppermute(sent[0], "groups", partners)]
    step(0)
    passages = passages_later
    own.append(own_half(weight_later, side, 1))
    ring.append([(own[1], own[1])])
    sent += [pick_columns(passages, 1 - side, half, *cuts[i : i + 2]) for i in (1, 2)]
    kept = pick_columns(passages, side, half, 0, tokens)
    new_rows = jnp.swapaxes(new_hidden, 0, 1).reshape(count, half_model)
    new_rows = jnp.pad(new_rows, ((0, new_padded - count), (0, 0)))
    new_sent = pick_columns(new_rows, 1 - side, half, 0, new_padded)
    new_kept = pick_columns(new_rows, side, half, 0, new_padded)
    got[0], sent, kept, new_sent, new_kept, ring[1][0] = fence_with(
        0, got[0], sent, kept, new_sent, new_kept, ring[1][0]
    )

    got.append(lax.ppermute(sent[1], "groups", partners))
    step(0)
    kept_other = lax.ppermute(kept, "tensor", cores)
    got_other = [lax.ppermute(got[0], "tensor", cores)]
    kept_other, got_other, lengths, destinations = fence_with(
        1, kept_other, got_other, lengths, destinations
    )
    step(1)
    position, new_position, key_info, query_info = token_tables(
        lengths, destinations, row_index, tokens, requests, steps, new_padded
    )
    angles, new_angles = angle_table(position), angle_table(new_position)
    tables = (angles, new_angles, key_info, query_info)
    got[1], tables, places, ring[1][-1] = fence_with(0, got[1], tables, places, ring[1][-1])

    own_hidden = [(kept, kept_other)]
    early = row_count - 3
    got.append(lax.ppermute(sent[2], "groups", partners))
    step(0)
    got_other.append(lax.ppermute(got[1], "tensor", cores))
    (got_other[1],) = fence_with(1, got_other[1])
    step(1)
    for k in range(3, half_rows - 1):
        (ring[1][-1],) = fence_with(0, ring[1][-1])
        step(0)
        step(1)
    held = [project(0, own_hidden, None, 0, early)]
    ends[0] = halved(ring[0][-1])
    got[2], new_sent, held, places, ring[1][-1], ends[0] = fence_with(
        0, got[2], new_sent, held, places, ring[1][-1], ends[0]
    )

    step(0)
    got_other.append(lax.ppermute(got[2], "tensor", cores))
    new_kept = jnp.concatenate([new_kept, lax.ppermute(new_sent, "groups", partners)], 0)
    new_other = lax.ppermute(new_kept, "tensor", cores)
    (got_other[2],) = fence_with(1, got_other[2])
    step(1)
    away_hidden = list(zip(got, got_other)) + [(new_kept, new_other)]
    held.append(project(1, own_hidden, None, 0, early))
    places, held = fence(places, held)
    away = project(0, away_hidden, None, 0, row_count)
    away, places = fence(homeward(away), places)
    (places,) = fence_with(1, places)
    ends[1] = halved(ring[1][-1])
    step(1)
    homed = [lax.ppermute(away[0], "groups", partners)]
    new_own, new_away = [away[2]], [away[1]]
    away = project(1, away_hidden, None, 0, row_count - 1)
    away = homeward(project(1, away_hidden, away, row_count - 1, row_count))
    new_own.append(away[2])
    new_away.append(away[1])
    new_back = lax.ppermute(jnp.concatenate(new_away, 1), "groups", partners)
    held[0] = project(0, own_hidden, held[0], early, row_count)
    queries = jnp.swapaxes(queries, 0, 1).reshape(count, -1)
    places, away = fence(places, away)
    held[1] = project(1, own_hidden, held[1], early, row_count)
    held, queries, away, new_back, homed[0] = fence(held, queries, away, new_back, homed[0])
    homed.append(lax.ppermute(away[0], "groups", partners))
    angles, new_angles, key_info, query_info = tables
    moved = pack(new_own, new_back, new_angles, queries)
    moved = moved.reshape(steps, requests, -1)
    moved = jnp.swapaxes(moved, 0, 1)
    moved = lax.all_to_all(moved, "rows", split_axis=0, concat_axis=0, tiled=True)
    moved = jnp.swapaxes(moved, 0, 1).reshape(count, -1)
    heads_width = queries.shape[1]
    query_rows, new_pairs = moved[:, :heads_width], moved[:, heads_width:]
    new_pairs = jnp.pad(new_pairs, ((0, new_padded - count), (0, 0)))
    homed = [total.astype(jnp.float32) * (1.0 / RAISE) for total in homed]
    attended = None
    for c in range(CHUNKS):
        attended = finish(
            c, attended, held[c], homed[c], angles, key_info, query_info, new_pairs, query_rows
        )
    attended = jnp.swapaxes(attended.reshape(steps, requests, -1), 0, 1)
    return lax.all_to_all(attended, "rows", split_axis=0, concat_axis=0, tiled=True)


def solution(mesh):
    placed = (
        P(("groups", "rows"), "tensor"),
        P("rows", None, "tensor"),
        P(("groups", "rows"), None, "tensor"),
        P(("groups", "rows"), None, "tensor"),
        P("groups", None),
        P("groups", None),
    )
    return jax.shard_map(
        body,
        mesh=mesh,
        in_specs=placed,
        out_specs=P(("groups", "rows"), None, "tensor"),
        check_vma=False,
    )
```

```python
import functools
import math

import jax
import jax.numpy as jnp
import numpy as np
from jax import lax
from jax.experimental import pallas as pl
from jax.experimental.pallas import tpu as pltpu
from jax.sharding import PartitionSpec as P

HD = 128
HALF = HD // 2
CHUNKS = 2
MOST_SHARDS = 8
VMEM_BYTES = 20 << 20
MERGED = 4
RAISE = 16.0


def angle_table(positions):
    index_float = jnp.arange(HALF, dtype=jnp.float32)
    inverse = jnp.exp(index_float * (-2.0 * math.log(1000000.0) / HD))
    angles = positions.astype(jnp.float32)[:, None] * inverse
    return jnp.concatenate([jnp.cos(angles), jnp.sin(angles)], 1)


def token_tables(lengths, destinations, row_index, tokens, requests, steps, padded):
    my_lengths = lax.dynamic_index_in_dim(lengths, row_index, 0, keepdims=False)
    my_targets = lax.dynamic_index_in_dim(destinations, row_index, 0, keepdims=False)
    ends = jnp.cumsum(my_lengths)
    starts = ends - my_lengths
    token = jnp.arange(tokens, dtype=jnp.int32)[:, None]
    inside = (starts[None, :] <= token) & (token < ends[None, :])
    token_position = token[:, 0] - jnp.sum(jnp.where(inside, starts[None, :], 0), axis=1)
    token_target = jnp.sum(jnp.where(inside, my_targets[None, :], 0), axis=1)
    received = jnp.sum(jnp.where(destinations == row_index, lengths, 0), axis=1)
    step = np.repeat(np.arange(steps, dtype=np.int32), requests)
    new_target = np.tile(np.arange(requests, dtype=np.int32), steps)
    new_position = jnp.tile(received, steps) + step
    spare = np.zeros((padded - requests * steps,), np.int32)
    target = jnp.concatenate([token_target, np.concatenate([new_target, spare - 1])])
    seen_from = jnp.asarray(np.concatenate([np.zeros((tokens,), np.int32), step, spare]))
    query_info = jnp.asarray(np.stack([new_target, step], 1))
    return token_position, new_position, jnp.stack([target, seen_from], 0), query_info


def rotate(first, second, cosine, sine):
    return [first * cosine - second * sine, second * cosine + first * sine]


def finish_kernel(c, group, held_ref, homed_ref, angle_ref, keys_ref, rows_ref, new_ref, query_ref, *refs):
    out_ref = refs[-1]
    if c > 0:
        out_ref[:, : refs[0].shape[1]] = refs[0][...]
    cosine, sine = angle_ref[:, :HALF], angle_ref[:, HALF:]
    allowed = (keys_ref[0:1, :] == rows_ref[:, 0:1]) & (keys_ref[1:2, :] <= rows_ref[:, 1:2])
    allowed = jnp.concatenate([allowed.astype(jnp.float32)] * group, 0) > 0.5
    queries = query_ref[...].astype(jnp.float32)
    count = queries.shape[0]
    width = held_ref.shape[1]
    heads = width // (2 * HD)
    for local in range(heads):
        h = c * heads + local
        key_at = slice(local * HD, (local + 1) * HD)
        value_at = slice((heads + local) * HD, (heads + local + 1) * HD)
        new_at = c * width
        both = held_ref[:, key_at] + homed_ref[:, key_at]
        keys = jnp.concatenate(rotate(both[:, :HALF], both[:, HALF:], cosine, sine), -1)
        values = held_ref[:, value_at] + homed_ref[:, value_at]
        keys, values = (
            jnp.concatenate(
                [cached.astype(jnp.bfloat16), new_ref[:, new_at + at.start : new_at + at.stop]], 0
            )
            for cached, at in ((keys, key_at), (values, value_at))
        )
        at = h * group * HD
        query = jnp.concatenate(
            [queries[:, at + g * HD : at + (g + 1) * HD] for g in range(group)], 0
        ).astype(jnp.bfloat16)
        scores = lax.dot_general(
            query, keys, (((1,), (1,)), ((), ())), preferred_element_type=jnp.float32
        )
        scores = jnp.where(allowed, scores * (1.0 / math.sqrt(HD)), jnp.float32(-1e30))
        raised = jnp.exp(scores - jnp.max(scores, axis=-1, keepdims=True))
        total = jnp.sum(raised, axis=-1, keepdims=True)
        weights = (raised / total).astype(jnp.bfloat16)
        output = jnp.dot(weights, values, preferred_element_type=jnp.float32)
        for g in range(group):
            out_ref[:, at + g * HD : at + (g + 1) * HD] = output[
                g * count : (g + 1) * count
            ].astype(jnp.bfloat16)


def finish(c, done, held, homed, angles, key_info, query_info, new_pairs, queries):
    rows, width = held.shape
    heads = width // (2 * HD)
    group = queries.shape[1] // (CHUNKS * heads * HD)
    count = queries.shape[0]
    vmem = pl.BlockSpec(memory_space=pltpu.VMEM)
    operands = [held, homed, angles, key_info, query_info, new_pairs, queries]
    if done is not None:
        operands.append(done)
    return pl.pallas_call(
        functools.partial(finish_kernel, c, group),
        out_shape=jax.ShapeDtypeStruct((count, (c + 1) * heads * group * HD), jnp.bfloat16),
        in_specs=[vmem] * len(operands),
        out_specs=vmem,
        compiler_params=pltpu.CompilerParams(vmem_limit_bytes=VMEM_BYTES),
        cost_estimate=pl.CostEstimate(
            flops=4 * heads * group * count * rows * HD,
            bytes_accessed=8 * rows * width + 4 * queries.size,
            transcendentals=heads * group * count * rows,
        ),
        name="rotate_attend",
    )(*operands)


def own_kernel(side_ref, weight_ref, out_ref):
    chunk = weight_ref.shape[2]
    for kind in range(2):
        out_ref[:, kind * chunk : (kind + 1) * chunk] = weight_ref[:, kind, :]


def own_half(weight, side, c):
    depth, kinds, width = weight.shape
    half, chunk = depth // 2, width // CHUNKS
    return pl.pallas_call(
        own_kernel,
        out_shape=jax.ShapeDtypeStruct((half, kinds * chunk), weight.dtype),
        grid_spec=pltpu.PrefetchScalarGridSpec(
            num_scalar_prefetch=1,
            grid=(2,),
            in_specs=[
                pl.BlockSpec((half // 2, kinds, chunk), lambda i, s: (2 * s[0] + i, 0, c))
            ],
            out_specs=pl.BlockSpec((half // 2, kinds * chunk), lambda i, s: (i, 0)),
        ),
        compiler_params=pltpu.CompilerParams(vmem_limit_bytes=VMEM_BYTES),
        cost_estimate=pl.CostEstimate(
            flops=0, bytes_accessed=8 * half * chunk * kinds, transcendentals=0
        ),
        name="own_half",
    )(side.reshape(1), weight)


def pack_kernel(chunks, own_ref, *refs):
    owns, refs = (own_ref, *refs[: chunks - 1]), refs[chunks - 1 :]
    gots, (angle_ref, query_ref, out_ref) = refs[:chunks], refs[chunks:]
    cosine, sine = angle_ref[:, :HALF], angle_ref[:, HALF:]
    base = query_ref.shape[1]
    width = owns[0].shape[1]
    half = width // 2
    out_ref[:, :base] = query_ref[...]
    for c in range(chunks):
        for h in range(half // HD):
            at = h * HD
            both = owns[c][:, at : at + HD] + gots[c][:, at : at + HD]
            both = jnp.concatenate(rotate(both[:, :HALF], both[:, HALF:], cosine, sine), -1)
            at += base + c * width
            out_ref[:, at : at + HD] = both.astype(jnp.bfloat16)
        values = owns[c][:, half:] + gots[c][:, half:]
        at = base + c * width + half
        out_ref[:, at : at + half] = values.astype(jnp.bfloat16)


def pack(owns, gots, angles, queries):
    vmem = pl.BlockSpec(memory_space=pltpu.VMEM)
    width = queries.shape[1] + sum(got.shape[1] for got in gots)
    return pl.pallas_call(
        functools.partial(pack_kernel, len(owns)),
        out_shape=jax.ShapeDtypeStruct((queries.shape[0], width), jnp.bfloat16),
        in_specs=[vmem] * (2 * len(owns) + 2),
        out_specs=vmem,
        compiler_params=pltpu.CompilerParams(vmem_limit_bytes=VMEM_BYTES),
        cost_estimate=pl.CostEstimate(
            flops=0, bytes_accessed=4 * queries.size + 20 * gots[0].size, transcendentals=0
        ),
        name="pack_new",
    )(*owns, *gots, angles, queries)


def pick_kernel(first, side_ref, source_ref, out_ref):
    out_ref[...] = source_ref[first : first + out_ref.shape[0], :]


def pick_columns(source, side, half, first, end):
    rows, blocks = source.shape[0], source.shape[1] // (2 * half)
    return pl.pallas_call(
        functools.partial(pick_kernel, first),
        out_shape=jax.ShapeDtypeStruct((end - first, blocks * half), source.dtype),
        grid_spec=pltpu.PrefetchScalarGridSpec(
            num_scalar_prefetch=1,
            grid=(blocks,),
            in_specs=[pl.BlockSpec((rows, half), lambda j, s: (0, 2 * j + s[0]))],
            out_specs=pl.BlockSpec((end - first, half), lambda j, s: (0, j)),
        ),
        compiler_params=pltpu.CompilerParams(vmem_limit_bytes=VMEM_BYTES),
        cost_estimate=pl.CostEstimate(
            flops=0, bytes_accessed=4 * (end - first) * blocks * half, transcendentals=0
        ),
        name="pick_columns",
    )(side.reshape(1), source)


def product_kernel(depths, parts, base, has_total, *refs):
    place_ref, refs = refs[0], refs[1:]
    hidden, refs = refs[: 2 * parts], refs[2 * parts :]
    weights, out_ref = refs[: sum(len(pieces) for pieces in depths)], refs[-1]
    half = sum(depths[0])
    blocks = hidden[0].shape[1] // half

    total, used = refs[-2][...] if has_total else None, 0
    for p, pieces in enumerate(depths):
        place = place_ref[base + p]
        here = place < blocks
        columns = pl.ds(pl.multiple_of(jnp.where(here, place, place - blocks) * half, half), half)
        rows = [
            jnp.where(here, hidden[2 * q][:, columns], hidden[2 * q + 1][:, columns])
            for q in range(parts)
        ]
        rows = rows[0] if parts == 1 else jnp.concatenate(rows, 0)
        piece = [w[...] for w in weights[used : used + len(pieces)]]
        piece = piece[0] if len(piece) == 1 else jnp.concatenate(piece, 0)
        used += len(pieces)
        term = jnp.dot(rows, piece, preferred_element_type=jnp.float32)
        total = term if total is None else total + term
    out_ref[...] = total


def products(total, hidden, weights, places, base):
    shards = len(weights)
    flat = [w for shard in weights for w in shard]
    depths = tuple(tuple(w.shape[0] for w in shard) for shard in weights)
    half, width = sum(depths[0]), flat[0].shape[1]
    rows = sum(pair[0].shape[0] for pair in hidden)
    operands = [places] + [array for pair in hidden for array in pair] + flat
    if total is not None:
        operands.append(total)
    vmem = pl.BlockSpec(memory_space=pltpu.VMEM)
    return pl.pallas_call(
        functools.partial(
            product_kernel, depths, len(hidden), base, total is not None
        ),
        out_shape=jax.ShapeDtypeStruct((rows, width), jnp.float32),
        in_specs=[pl.BlockSpec(memory_space=pltpu.SMEM)] + [vmem] * (len(operands) - 1),
        out_specs=vmem,
        compiler_params=pltpu.CompilerParams(vmem_limit_bytes=VMEM_BYTES),
        cost_estimate=pl.CostEstimate(
            flops=2 * rows * half * width * shards,
            bytes_accessed=shards * 2 * half * (rows + width) + 4 * rows * width,
            transcendentals=0,
        ),
        name="products",
    )(*operands)


def ring_order(row_count):
    evens = list(range(0, row_count, 2))
    odds = list(range(1, row_count, 2))
    return evens + odds[::-1]


def fence(*values):
    return lax.optimization_barrier(values)


def body(passages, kv_weight, new_hidden, queries, lengths, destinations):
    tokens = passages.shape[0]
    requests, steps, half_model = new_hidden.shape
    row_count = lax.axis_size("rows")
    group_count = lax.axis_size("groups")
    row_index = lax.axis_index("rows")
    side = lax.axis_index("groups") % 2
    core = lax.axis_index("tensor")
    depth = kv_weight.shape[0]
    half = depth // 2
    local_heads = kv_weight.shape[2] // HD
    group = queries.shape[2] // kv_weight.shape[2]
    count = requests * steps
    new_padded = -(-count // 16) * 16
    half_rows = row_count // 2

    partners = [(g, g ^ 1) for g in range(group_count)]
    cores = [(0, 1), (1, 0)]
    order = ring_order(row_count)
    onward = [(order[i], order[(i + 1) % row_count]) for i in range(row_count)]
    back = [(b, a) for a, b in onward]
    place = {row: i for i, row in enumerate(order)}
    shard_order = [
        [order[(place[r] + d) % row_count] for r in range(row_count)]
        for k in range(half_rows + 1)
        for d in ([0] if k == 0 else [-k, k] if k < half_rows else [k])
    ]
    owners = lax.dynamic_index_in_dim(jnp.array(shard_order, jnp.int32), row_index, 1, keepdims=False)
    places = ((owners // half_rows) ^ core) * half_rows + owners % half_rows

    own = [own_half(kv_weight, side, 0)]

    ring, ends = [[(own[0], own[0])]], [None, None]

    def halved(pair):
        return pair[0][: half // 2], pair[1][half // 2 :]

    def step(c):
        pair = ring[c][-1]
        if len(ring[c]) == half_rows:
            pair = ends[c]
        ring[c].append((lax.ppermute(pair[0], "rows", onward), lax.ppermute(pair[1], "rows", back)))

    def fence_with(c, *others):
        ring[c][-1], others = fence(ring[c][-1], others)
        return others

    def project(c, hidden, total, begin, end):
        weights = [(own[c],)] + [(w,) for pair in ring[c][1:half_rows] for w in pair]
        weights += ring[c][half_rows:]
        for at in range(begin, end, MOST_SHARDS):
            some = weights[at : min(at + MOST_SHARDS, end)]
            total = products(total, hidden, some, places, at)
        return total

    def homeward(total):
        tokens_total = (total[:tokens] * RAISE).astype(jnp.float16)
        at = tokens + new_padded
        return tokens_total, total[at : at + count], total[tokens : tokens + count]

    cuts = (0, 3 * tokens // 20, 23 * tokens // 40, tokens)
    sent = [pick_columns(passages, 1 - side, half, cuts[0], cuts[1])]
    passages_later, new_hidden, weight_later = fence_with(0, passages, new_hidden, kv_weight)
    got = [lax.ppermute(sent[0], "groups", partners)]
    step(0)
    passages = passages_later
    own.append(own_half(weight_later, side, 1))
    ring.append([(own[1], own[1])])
    sent += [pick_columns(passages, 1 - side, half, *cuts[i : i + 2]) for i in (1, 2)]
    kept = pick_columns(passages, side, half, 0, tokens)
    new_rows = jnp.swapaxes(new_hidden, 0, 1).reshape(count, half_model)
    new_rows = jnp.pad(new_rows, ((0, new_padded - count), (0, 0)))
    new_sent = pick_columns(new_rows, 1 - side, half, 0, new_padded)
    new_kept = pick_columns(new_rows, side, half, 0, new_padded)
    got[0], sent, kept, new_sent, new_kept, ring[1][0] = fence_with(
        0, got[0], sent, kept, new_sent, new_kept, ring[1][0]
    )

    got.append(lax.ppermute(sent[1], "groups", partners))
    step(0)
    kept_other = lax.ppermute(kept, "tensor", cores)
    got_other = [lax.ppermute(got[0], "tensor", cores)]
    kept_other, got_other, lengths, destinations = fence_with(
        1, kept_other, got_other, lengths, destinations
    )
    step(1)
    position, new_position, key_info, query_info = token_tables(
        lengths, destinations, row_index, tokens, requests, steps, new_padded
    )
    angles, new_angles = angle_table(position), angle_table(new_position)
    tables = (angles, new_angles, key_info, query_info)
    got[1], tables, places, ring[1][-1] = fence_with(0, got[1], tables, places, ring[1][-1])

    own_hidden = [(kept, kept_other)]
    early = row_count - 3
    got.append(lax.ppermute(sent[2], "groups", partners))
    step(0)
    got_other.append(lax.ppermute(got[1], "tensor", cores))
    (got_other[1],) = fence_with(1, got_other[1])
    step(1)
    for k in range(3, half_rows - 1):
        (ring[1][-1],) = fence_with(0, ring[1][-1])
        step(0)
        step(1)
    held = [project(0, own_hidden, None, 0, early)]
    ends[0] = halved(ring[0][-1])
    got[2], new_sent, held, places, ring[1][-1], ends[0] = fence_with(
        0, got[2], new_sent, held, places, ring[1][-1], ends[0]
    )

    step(0)
    got_other.append(lax.ppermute(got[2], "tensor", cores))
    new_kept = jnp.concatenate([new_kept, lax.ppermute(new_sent, "groups", partners)], 0)
    new_other = lax.ppermute(new_kept, "tensor", cores)
    (got_other[2],) = fence_with(1, got_other[2])
    step(1)
    away_hidden = list(zip(got, got_other)) + [(new_kept, new_other)]
    held.append(project(1, own_hidden, None, 0, early))
    places, held = fence(places, held)
    away = project(0, away_hidden, None, 0, row_count)
    away, places = fence(homeward(away), places)
    (places,) = fence_with(1, places)
    ends[1] = halved(ring[1][-1])
    step(1)
    homed = [lax.ppermute(away[0], "groups", partners)]
    new_own, new_back = [away[2]], [lax.ppermute(away[1], "groups", partners)]
    away = project(1, away_hidden, None, 0, row_count - 1)
    away = homeward(project(1, away_hidden, away, row_count - 1, row_count))
    new_own.append(away[2])
    new_back.append(lax.ppermute(away[1], "groups", partners))
    held[0] = project(0, own_hidden, held[0], early, row_count)
    queries = jnp.swapaxes(queries, 0, 1).reshape(count, -1)
    places, away = fence(places, away)
    held[1] = project(1, own_hidden, held[1], early, row_count)
    held, queries, away, new_back, homed[0] = fence(held, queries, away, new_back, homed[0])
    homed.append(lax.ppermute(away[0], "groups", partners))
    angles, new_angles, key_info, query_info = tables
    moved = pack(new_own, new_back, new_angles, queries)
    moved = moved.reshape(steps, requests, -1)
    moved = jnp.swapaxes(moved, 0, 1)
    moved = lax.all_to_all(moved, "rows", split_axis=0, concat_axis=0, tiled=True)
    moved = jnp.swapaxes(moved, 0, 1).reshape(count, -1)
    heads_width = queries.shape[1]
    query_rows, new_pairs = moved[:, :heads_width], moved[:, heads_width:]
    new_pairs = jnp.pad(new_pairs, ((0, new_padded - count), (0, 0)))
    homed = [total.astype(jnp.float32) * (1.0 / RAISE) for total in homed]
    attended = None
    for c in range(CHUNKS):
        attended = finish(
            c, attended, held[c], homed[c], angles, key_info, query_info, new_pairs, query_rows
        )
    attended = jnp.swapaxes(attended.reshape(steps, requests, -1), 0, 1)
    return lax.all_to_all(attended, "rows", split_axis=0, concat_axis=0, tiled=True)


def solution(mesh):
    placed = (
        P(("groups", "rows"), "tensor"),
        P("rows", None, "tensor"),
        P(("groups", "rows"), None, "tensor"),
        P(("groups", "rows"), None, "tensor"),
        P("groups", None),
        P("groups", None),
    )
    return jax.shard_map(
        body,
        mesh=mesh,
        in_specs=placed,
        out_specs=P(("groups", "rows"), None, "tensor"),
        check_vma=False,
    )
```

```python
import functools
import math

import jax
import jax.numpy as jnp
import numpy as np
from jax import lax
from jax.experimental import pallas as pl
from jax.experimental.pallas import tpu as pltpu
from jax.sharding import PartitionSpec as P

HD = 128
HALF = HD // 2
CHUNKS = 2
MOST_SHARDS = 8
VMEM_BYTES = 20 << 20
MERGED = 4
RAISE = 16.0


def angle_table(positions):
    index_float = jnp.arange(HALF, dtype=jnp.float32)
    inverse = jnp.exp(index_float * (-2.0 * math.log(1000000.0) / HD))
    angles = positions.astype(jnp.float32)[:, None] * inverse
    return jnp.concatenate([jnp.cos(angles), jnp.sin(angles)], 1)


def token_tables(lengths, destinations, row_index, tokens, requests, steps, padded):
    my_lengths = lax.dynamic_index_in_dim(lengths, row_index, 0, keepdims=False)
    my_targets = lax.dynamic_index_in_dim(destinations, row_index, 0, keepdims=False)
    ends = jnp.cumsum(my_lengths)
    starts = ends - my_lengths
    token = jnp.arange(tokens, dtype=jnp.int32)[:, None]
    inside = (starts[None, :] <= token) & (token < ends[None, :])
    token_position = token[:, 0] - jnp.sum(jnp.where(inside, starts[None, :], 0), axis=1)
    token_target = jnp.sum(jnp.where(inside, my_targets[None, :], 0), axis=1)
    received = jnp.sum(jnp.where(destinations == row_index, lengths, 0), axis=1)
    step = np.repeat(np.arange(steps, dtype=np.int32), requests)
    new_target = np.tile(np.arange(requests, dtype=np.int32), steps)
    new_position = jnp.tile(received, steps) + step
    spare = np.zeros((padded - requests * steps,), np.int32)
    target = jnp.concatenate([token_target, np.concatenate([new_target, spare - 1])])
    seen_from = jnp.asarray(np.concatenate([np.zeros((tokens,), np.int32), step, spare]))
    query_info = jnp.asarray(np.stack([new_target, step], 1))
    return token_position, new_position, jnp.stack([target, seen_from], 0), query_info


def rotate(first, second, cosine, sine):
    return [first * cosine - second * sine, second * cosine + first * sine]


def finish_kernel(c, group, held_ref, homed_ref, angle_ref, keys_ref, rows_ref, new_ref, query_ref, *refs):
    out_ref = refs[-1]
    if c > 0:
        out_ref[:, : refs[0].shape[1]] = refs[0][...]
    cosine, sine = angle_ref[:, :HALF], angle_ref[:, HALF:]
    allowed = (keys_ref[0:1, :] == rows_ref[:, 0:1]) & (keys_ref[1:2, :] <= rows_ref[:, 1:2])
    allowed = jnp.concatenate([allowed.astype(jnp.float32)] * group, 0) > 0.5
    queries = query_ref[...].astype(jnp.float32)
    count = queries.shape[0]
    width = held_ref.shape[1]
    heads = width // (2 * HD)
    for local in range(heads):
        h = c * heads + local
        key_at = slice(local * HD, (local + 1) * HD)
        value_at = slice((heads + local) * HD, (heads + local + 1) * HD)
        new_at = c * width
        both = held_ref[:, key_at] + homed_ref[:, key_at]
        keys = jnp.concatenate(rotate(both[:, :HALF], both[:, HALF:], cosine, sine), -1)
        values = held_ref[:, value_at] + homed_ref[:, value_at]
        keys, values = (
            jnp.concatenate(
                [cached.astype(jnp.bfloat16), new_ref[:, new_at + at.start : new_at + at.stop]], 0
            )
            for cached, at in ((keys, key_at), (values, value_at))
        )
        at = h * group * HD
        query = jnp.concatenate(
            [queries[:, at + g * HD : at + (g + 1) * HD] for g in range(group)], 0
        ).astype(jnp.bfloat16)
        scores = lax.dot_general(
            query, keys, (((1,), (1,)), ((), ())), preferred_element_type=jnp.float32
        )
        scores = jnp.where(allowed, scores * (1.0 / math.sqrt(HD)), jnp.float32(-1e30))
        raised = jnp.exp(scores - jnp.max(scores, axis=-1, keepdims=True))
        total = jnp.sum(raised, axis=-1, keepdims=True)
        weights = (raised / total).astype(jnp.bfloat16)
        output = jnp.dot(weights, values, preferred_element_type=jnp.float32)
        for g in range(group):
            out_ref[:, at + g * HD : at + (g + 1) * HD] = output[
                g * count : (g + 1) * count
            ].astype(jnp.bfloat16)


def finish(c, done, held, homed, angles, key_info, query_info, new_pairs, queries):
    rows, width = held.shape
    heads = width // (2 * HD)
    group = queries.shape[1] // (CHUNKS * heads * HD)
    count = queries.shape[0]
    vmem = pl.BlockSpec(memory_space=pltpu.VMEM)
    operands = [held, homed, angles, key_info, query_info, new_pairs, queries]
    if done is not None:
        operands.append(done)
    return pl.pallas_call(
        functools.partial(finish_kernel, c, group),
        out_shape=jax.ShapeDtypeStruct((count, (c + 1) * heads * group * HD), jnp.bfloat16),
        in_specs=[vmem] * len(operands),
        out_specs=vmem,
        compiler_params=pltpu.CompilerParams(vmem_limit_bytes=VMEM_BYTES),
        cost_estimate=pl.CostEstimate(
            flops=4 * heads * group * count * rows * HD,
            bytes_accessed=8 * rows * width + 4 * queries.size,
            transcendentals=heads * group * count * rows,
        ),
        name="rotate_attend",
    )(*operands)


def own_kernel(side_ref, weight_ref, out_ref):
    chunk = weight_ref.shape[2]
    for kind in range(2):
        out_ref[:, kind * chunk : (kind + 1) * chunk] = weight_ref[:, kind, :]


def own_half(weight, side, c):
    depth, kinds, width = weight.shape
    half, chunk = depth // 2, width // CHUNKS
    return pl.pallas_call(
        own_kernel,
        out_shape=jax.ShapeDtypeStruct((half, kinds * chunk), weight.dtype),
        grid_spec=pltpu.PrefetchScalarGridSpec(
            num_scalar_prefetch=1,
            grid=(2,),
            in_specs=[
                pl.BlockSpec((half // 2, kinds, chunk), lambda i, s: (2 * s[0] + i, 0, c))
            ],
            out_specs=pl.BlockSpec((half // 2, kinds * chunk), lambda i, s: (i, 0)),
        ),
        compiler_params=pltpu.CompilerParams(vmem_limit_bytes=VMEM_BYTES),
        cost_estimate=pl.CostEstimate(
            flops=0, bytes_accessed=8 * half * chunk * kinds, transcendentals=0
        ),
        name="own_half",
    )(side.reshape(1), weight)


def pack_kernel(chunks, own_ref, *refs):
    owns, refs = (own_ref, *refs[: chunks - 1]), refs[chunks - 1 :]
    gots, (angle_ref, query_ref, out_ref) = refs[:chunks], refs[chunks:]
    cosine, sine = angle_ref[:, :HALF], angle_ref[:, HALF:]
    base = query_ref.shape[1]
    width = owns[0].shape[1]
    half = width // 2
    out_ref[:, :base] = query_ref[...]
    for c in range(chunks):
        for h in range(half // HD):
            at = h * HD
            both = owns[c][:, at : at + HD] + gots[c][:, at : at + HD]
            both = jnp.concatenate(rotate(both[:, :HALF], both[:, HALF:], cosine, sine), -1)
            at += base + c * width
            out_ref[:, at : at + HD] = both.astype(jnp.bfloat16)
        values = owns[c][:, half:] + gots[c][:, half:]
        at = base + c * width + half
        out_ref[:, at : at + half] = values.astype(jnp.bfloat16)


def pack(owns, gots, angles, queries):
    vmem = pl.BlockSpec(memory_space=pltpu.VMEM)
    width = queries.shape[1] + sum(got.shape[1] for got in gots)
    return pl.pallas_call(
        functools.partial(pack_kernel, len(owns)),
        out_shape=jax.ShapeDtypeStruct((queries.shape[0], width), jnp.bfloat16),
        in_specs=[vmem] * (2 * len(owns) + 2),
        out_specs=vmem,
        compiler_params=pltpu.CompilerParams(vmem_limit_bytes=VMEM_BYTES),
        cost_estimate=pl.CostEstimate(
            flops=0, bytes_accessed=4 * queries.size + 20 * gots[0].size, transcendentals=0
        ),
        name="pack_new",
    )(*owns, *gots, angles, queries)


def pick_kernel(first, side_ref, source_ref, out_ref):
    out_ref[...] = source_ref[first : first + out_ref.shape[0], :]


def pick_columns(source, side, half, first, end):
    rows, blocks = source.shape[0], source.shape[1] // (2 * half)
    return pl.pallas_call(
        functools.partial(pick_kernel, first),
        out_shape=jax.ShapeDtypeStruct((end - first, blocks * half), source.dtype),
        grid_spec=pltpu.PrefetchScalarGridSpec(
            num_scalar_prefetch=1,
            grid=(blocks,),
            in_specs=[pl.BlockSpec((rows, half), lambda j, s: (0, 2 * j + s[0]))],
            out_specs=pl.BlockSpec((end - first, half), lambda j, s: (0, j)),
        ),
        compiler_params=pltpu.CompilerParams(vmem_limit_bytes=VMEM_BYTES),
        cost_estimate=pl.CostEstimate(
            flops=0, bytes_accessed=4 * (end - first) * blocks * half, transcendentals=0
        ),
        name="pick_columns",
    )(side.reshape(1), source)


def product_kernel(depths, parts, base, has_total, *refs):
    place_ref, refs = refs[0], refs[1:]
    hidden, refs = refs[: 2 * parts], refs[2 * parts :]
    weights, out_ref = refs[: sum(len(pieces) for pieces in depths)], refs[-1]
    half = sum(depths[0])
    blocks = hidden[0].shape[1] // half

    total, used = refs[-2][...] if has_total else None, 0
    for p, pieces in enumerate(depths):
        place = place_ref[base + p]
        here = place < blocks
        columns = pl.ds(pl.multiple_of(jnp.where(here, place, place - blocks) * half, half), half)
        rows = [
            jnp.where(here, hidden[2 * q][:, columns], hidden[2 * q + 1][:, columns])
            for q in range(parts)
        ]
        rows = rows[0] if parts == 1 else jnp.concatenate(rows, 0)
        piece = [w[...] for w in weights[used : used + len(pieces)]]
        piece = piece[0] if len(piece) == 1 else jnp.concatenate(piece, 0)
        used += len(pieces)
        term = jnp.dot(rows, piece, preferred_element_type=jnp.float32)
        total = term if total is None else total + term
    out_ref[...] = total


def products(total, hidden, weights, places, base):
    shards = len(weights)
    flat = [w for shard in weights for w in shard]
    depths = tuple(tuple(w.shape[0] for w in shard) for shard in weights)
    half, width = sum(depths[0]), flat[0].shape[1]
    rows = sum(pair[0].shape[0] for pair in hidden)
    operands = [places] + [array for pair in hidden for array in pair] + flat
    if total is not None:
        operands.append(total)
    vmem = pl.BlockSpec(memory_space=pltpu.VMEM)
    return pl.pallas_call(
        functools.partial(
            product_kernel, depths, len(hidden), base, total is not None
        ),
        out_shape=jax.ShapeDtypeStruct((rows, width), jnp.float32),
        in_specs=[pl.BlockSpec(memory_space=pltpu.SMEM)] + [vmem] * (len(operands) - 1),
        out_specs=vmem,
        compiler_params=pltpu.CompilerParams(vmem_limit_bytes=VMEM_BYTES),
        cost_estimate=pl.CostEstimate(
            flops=2 * rows * half * width * shards,
            bytes_accessed=shards * 2 * half * (rows + width) + 4 * rows * width,
            transcendentals=0,
        ),
        name="products",
    )(*operands)


def ring_order(row_count):
    evens = list(range(0, row_count, 2))
    odds = list(range(1, row_count, 2))
    return evens + odds[::-1]


def fence(*values):
    return lax.optimization_barrier(values)


def body(passages, kv_weight, new_hidden, queries, lengths, destinations):
    tokens = passages.shape[0]
    requests, steps, half_model = new_hidden.shape
    row_count = lax.axis_size("rows")
    group_count = lax.axis_size("groups")
    row_index = lax.axis_index("rows")
    side = lax.axis_index("groups") % 2
    core = lax.axis_index("tensor")
    depth = kv_weight.shape[0]
    half = depth // 2
    local_heads = kv_weight.shape[2] // HD
    group = queries.shape[2] // kv_weight.shape[2]
    count = requests * steps
    new_padded = -(-count // 16) * 16
    half_rows = row_count // 2

    partners = [(g, g ^ 1) for g in range(group_count)]
    cores = [(0, 1), (1, 0)]
    order = ring_order(row_count)
    onward = [(order[i], order[(i + 1) % row_count]) for i in range(row_count)]
    back = [(b, a) for a, b in onward]
    place = {row: i for i, row in enumerate(order)}
    shard_order = [
        [order[(place[r] + d) % row_count] for r in range(row_count)]
        for k in range(half_rows + 1)
        for d in ([0] if k == 0 else [-k, k] if k < half_rows else [k])
    ]
    owners = lax.dynamic_index_in_dim(jnp.array(shard_order, jnp.int32), row_index, 1, keepdims=False)
    places = ((owners // half_rows) ^ core) * half_rows + owners % half_rows

    own = [own_half(kv_weight, side, 0)]

    ring, ends = [[(own[0], own[0])]], [None, None]

    def halved(pair):
        return pair[0][: half // 2], pair[1][half // 2 :]

    def step(c):
        pair = ring[c][-1]
        if len(ring[c]) == half_rows:
            pair = ends[c]
        ring[c].append((lax.ppermute(pair[0], "rows", onward), lax.ppermute(pair[1], "rows", back)))

    def fence_with(c, *others):
        ring[c][-1], others = fence(ring[c][-1], others)
        return others

    def project(c, hidden, total, begin, end):
        weights = [(own[c],)] + [(w,) for pair in ring[c][1:half_rows] for w in pair]
        weights += ring[c][half_rows:]
        for at in range(begin, end, MOST_SHARDS):
            some = weights[at : min(at + MOST_SHARDS, end)]
            total = products(total, hidden, some, places, at)
        return total

    def homeward(total):
        tokens_total = (total[:tokens] * RAISE).astype(jnp.float16)
        at = tokens + new_padded
        return tokens_total, total[at : at + count], total[tokens : tokens + count]

    cuts = (0, 3 * tokens // 20, 23 * tokens // 40, tokens)
    sent = [pick_columns(passages, 1 - side, half, cuts[0], cuts[1])]
    passages_later, new_hidden, weight_later = fence_with(0, passages, new_hidden, kv_weight)
    got = [lax.ppermute(sent[0], "groups", partners)]
    step(0)
    passages = passages_later
    own.append(own_half(weight_later, side, 1))
    ring.append([(own[1], own[1])])
    sent += [pick_columns(passages, 1 - side, half, *cuts[i : i + 2]) for i in (1, 2)]
    kept = pick_columns(passages, side, half, 0, tokens)
    new_rows = jnp.swapaxes(new_hidden, 0, 1).reshape(count, half_model)
    new_rows = jnp.pad(new_rows, ((0, new_padded - count), (0, 0)))
    new_sent = pick_columns(new_rows, 1 - side, half, 0, new_padded)
    new_kept = pick_columns(new_rows, side, half, 0, new_padded)
    got[0], sent, kept, new_sent, new_kept, ring[1][0] = fence_with(
        0, got[0], sent, kept, new_sent, new_kept, ring[1][0]
    )

    got.append(lax.ppermute(sent[1], "groups", partners))
    step(0)
    kept_other = lax.ppermute(kept, "tensor", cores)
    got_other = [lax.ppermute(got[0], "tensor", cores)]
    kept_other, got_other, lengths, destinations = fence_with(
        1, kept_other, got_other, lengths, destinations
    )
    step(1)
    position, new_position, key_info, query_info = token_tables(
        lengths, destinations, row_index, tokens, requests, steps, new_padded
    )
    angles, new_angles = angle_table(position), angle_table(new_position)
    tables = (angles, new_angles, key_info, query_info)
    got[1], tables, places, ring[1][-1] = fence_with(0, got[1], tables, places, ring[1][-1])

    own_hidden = [(kept, kept_other)]
    early = row_count - 3
    got.append(lax.ppermute(sent[2], "groups", partners))
    step(0)
    got_other.append(lax.ppermute(got[1], "tensor", cores))
    (got_other[1],) = fence_with(1, got_other[1])
    step(1)
    for k in range(3, half_rows - 1):
        (ring[1][-1],) = fence_with(0, ring[1][-1])
        step(0)
        step(1)
    held = [project(0, own_hidden, None, 0, early)]
    ends[0] = halved(ring[0][-1])
    got[2], new_sent, held, places, ring[1][-1], ends[0] = fence_with(
        0, got[2], new_sent, held, places, ring[1][-1], ends[0]
    )

    step(0)
    got_other.append(lax.ppermute(got[2], "tensor", cores))
    new_kept = jnp.concatenate([new_kept, lax.ppermute(new_sent, "groups", partners)], 0)
    new_other = lax.ppermute(new_kept, "tensor", cores)
    (got_other[2],) = fence_with(1, got_other[2])
    step(1)
    away_hidden = list(zip(got, got_other)) + [(new_kept, new_other)]
    held.append(project(1, own_hidden, None, 0, early))
    places, held = fence(places, held)
    away = project(0, away_hidden, None, 0, row_count)
    away, places = fence(homeward(away), places)
    (places,) = fence_with(1, places)
    ends[1] = halved(ring[1][-1])
    step(1)
    homed = [lax.ppermute(away[0], "groups", partners)]
    new_own, new_back = [away[2]], [lax.ppermute(away[1], "groups", partners)]
    away = project(1, away_hidden, None, 0, row_count - 1)
    away = homeward(project(1, away_hidden, away, row_count - 1, row_count))
    new_own.append(away[2])
    new_back.append(lax.ppermute(away[1], "groups", partners))
    held[0] = project(0, own_hidden, held[0], early, row_count)
    queries = jnp.swapaxes(queries, 0, 1).reshape(count, -1)
    held, queries, places, away, new_back, homed[0] = fence(
        held, queries, places, away, new_back, homed[0]
    )
    homed.append(lax.ppermute(away[0], "groups", partners))
    angles, new_angles, key_info, query_info = tables
    moved = pack(new_own, new_back, new_angles, queries)
    moved, places = fence(moved, places)
    held[1] = project(1, own_hidden, held[1], early, row_count)
    moved = moved.reshape(steps, requests, -1)
    moved = jnp.swapaxes(moved, 0, 1)
    moved = lax.all_to_all(moved, "rows", split_axis=0, concat_axis=0, tiled=True)
    moved = jnp.swapaxes(moved, 0, 1).reshape(count, -1)
    heads_width = queries.shape[1]
    query_rows, new_pairs = moved[:, :heads_width], moved[:, heads_width:]
    new_pairs = jnp.pad(new_pairs, ((0, new_padded - count), (0, 0)))
    homed = [total.astype(jnp.float32) * (1.0 / RAISE) for total in homed]
    attended = None
    for c in range(CHUNKS):
        attended = finish(
            c, attended, held[c], homed[c], angles, key_info, query_info, new_pairs, query_rows
        )
    attended = jnp.swapaxes(attended.reshape(steps, requests, -1), 0, 1)
    return lax.all_to_all(attended, "rows", split_axis=0, concat_axis=0, tiled=True)


def solution(mesh):
    placed = (
        P(("groups", "rows"), "tensor"),
        P("rows", None, "tensor"),
        P(("groups", "rows"), None, "tensor"),
        P(("groups", "rows"), None, "tensor"),
        P("groups", None),
        P("groups", None),
    )
    return jax.shard_map(
        body,
        mesh=mesh,
        in_specs=placed,
        out_specs=P(("groups", "rows"), None, "tensor"),
        check_vma=False,
    )
```
